32 devices in a mesh: grp: 4 (over y, x), sub: 8 (over z, core).
Axes of the slice: x: 2, y: 2, z: 4, core: 2. Of those that a mesh axis runs over, the one named last changes fastest.
Arguments:
- loads: float32 [4, 8, 32, 768], P('grp', 'sub'), may hold values from -6 to 6, as said below
- stiffness: bfloat16 [4, 8, 768, 768], P('grp', 'sub'), as said below
- flexibility: bfloat16 [4, 8, 768, 768], P('grp', 'sub'), as said below
- coarse_inverse: float32 [4, 96, 96], P('grp'), as said below
- face_nodes: int32 [4, 8, 4], P('grp', 'sub'), may hold values from 16 to 64, as said below
- corner_index: int32 [4, 8, 12], P('grp', 'sub'), may hold values from 0 to 767, as said below
Outputs:
- multipliers: float32 [4, 8, 32, 768], P('grp', 'sub')
- direction: float32 [4, 8, 32, 768], P('grp', 'sub')
The draws below stay inside these ranges and needn't reach their ends.
Inputs may be any that keep to these rules, and one draw needn't show every extreme that they name: `face_nodes`: matched subdomains hold the same value for the face they share; at least 16. `corner_index`: distinct within a subdomain. `stiffness`: symmetric positive definite for every subdomain. `flexibility`: symmetric positive definite for every subdomain. `coarse_inverse`: symmetric positive definite for every group. `loads`: A jump: equal on both copies of each face, zero at nodes not below face_nodes.
All inputs are finite; a program needn't handle non-finite values.
Results may differ from the reference program's by a relative error of at most 0.012.
The reference program's roundings to bfloat16 on the way count: a program that leaves them out, or rounds other values in their place, can miss the bound.
Values sent between devices are 32-bit elements; how exact they have to be, the bound alone decides.
No kernel may reach another device: no remote copies, remote signals or barrier semaphores. Data moves between devices by JAX's collectives and lax.ppermute only.
A program may use at most 64 MiB of HBM per device.

```python
import jax
import jax.numpy as jnp
import numpy as np
from jax import lax

NODES = 64
LOADS = 32
CORNERS = 12
ITERS = 2
DOFS = 768
CDOFS = 96
N_GRP = 4
N_SUB = 8


def spd_base(key, lead, order):
    key_off, key_diag = jax.random.split(key, 2)
    raw = jax.random.uniform(key_off, lead + (order, order), jnp.float32, -1.0, 1.0) * (0.8 / order ** 0.5)
    symmetric = raw + jnp.swapaxes(raw, -1, -2)
    diagonal = jax.random.uniform(key_diag, lead + (order,), jnp.float32, 2.0, 4.0)
    identity = jnp.eye(order, dtype=jnp.float32)
    return symmetric * (1.0 - identity) + diagonal[..., None] * identity


def draw_stiffness(key, part):
    key_use = jax.random.fold_in(key, 11)
    matrix = spd_base(key_use, (N_GRP, N_SUB), DOFS)
    return matrix.astype(jnp.bfloat16)


def draw_flexibility(key, part):
    key_use = jax.random.fold_in(key, 23)
    matrix = spd_base(key_use, (N_GRP, N_SUB), DOFS)
    return matrix.astype(jnp.bfloat16)


def draw_coarse_inverse(key, part):
    key_use = jax.random.fold_in(key, 37)
    matrix = spd_base(key_use, (N_GRP,), CDOFS)
    return matrix


def face_nodes_common(key):
    base = jax.random.randint(jax.random.fold_in(key, 41), (N_GRP, N_SUB, 4), NODES // 4, NODES + 1)
    base = base.at[0, 0, :].set(NODES)
    sub_ids = jnp.arange(N_SUB)
    grp_ids = jnp.arange(N_GRP)
    columns = []
    for face_index in range(3):
        lower = sub_ids - (sub_ids & 1 << face_index)
        columns.append(base[:, lower, face_index])
    lower_grp = grp_ids - (grp_ids & 1)
    columns.append(base[lower_grp][:, :, 3])
    return jnp.stack(columns, axis=-1).astype(jnp.int32)


def draw_face_nodes(key, part):
    return face_nodes_common(key)


def draw_loads(key, part):
    live_nodes = face_nodes_common(key)
    face_dofs = 3 * NODES
    field = jax.random.normal(jax.random.fold_in(key, 67), (N_GRP, N_SUB, LOADS, DOFS), jnp.float32)
    sub_ids = jnp.arange(N_SUB)
    grp_ids = jnp.arange(N_GRP)
    positions = jnp.arange(DOFS)
    face_of = positions // face_dofs
    node_of = positions % NODES
    sign_sub = [1.0 - 2.0 * (sub_ids >> f & 1).astype(jnp.float32) for f in range(3)]
    pieces = []
    for face_index in range(4):
        block = field[..., face_index * face_dofs:(face_index + 1) * face_dofs]
        if face_index < 3:
            across = block[:, sub_ids ^ 1 << face_index]
            sign = jnp.broadcast_to(sign_sub[face_index][None, :], (N_GRP, N_SUB))
        else:
            across = block[grp_ids ^ 1]
            sign = jnp.broadcast_to((1.0 - 2.0 * (grp_ids & 1).astype(jnp.float32))[:, None], (N_GRP, N_SUB))
        pieces.append((block - across) * sign[:, :, None, None])
    jumped = jnp.concatenate(pieces, axis=3)
    live = live_nodes[:, :, face_of]
    mask = (node_of[None, None, :] < live).astype(jnp.float32)[:, :, None, :]
    return jnp.clip(jumped * mask, -6.0, 6.0)


def draw_corner_index(key, part):
    keys = jax.random.split(jax.random.fold_in(key, 53), N_GRP * N_SUB)
    chosen = jax.vmap(lambda single: jax.random.permutation(single, DOFS)[:CORNERS])(keys)
    return chosen.reshape(N_GRP, N_SUB, CORNERS).astype(jnp.int32)


def setup_inputs(seed: int = 0) -> dict:
    key_list = jax.random.split(jax.random.key(seed), 7)
    return {
        "loads": draw_loads(jax.random.fold_in(key_list[6], 71), 0),
        "stiffness": draw_stiffness(jax.random.fold_in(key_list[6], 71), 0),
        "flexibility": draw_flexibility(jax.random.fold_in(key_list[6], 71), 0),
        "coarse_inverse": draw_coarse_inverse(jax.random.fold_in(key_list[6], 71), 0),
        "face_nodes": draw_face_nodes(jax.random.fold_in(key_list[6], 71), 0),
        "corner_index": draw_corner_index(jax.random.fold_in(key_list[6], 71), 0),
    }


def reference(loads, stiffness, flexibility, coarse_inverse, face_nodes, corner_index):
    face_dofs = 3 * NODES
    sub_ids = np.arange(N_SUB)
    grp_ids = np.arange(N_GRP)
    sign_rows = []
    for face_index in range(3):
        bit_vals = ((sub_ids >> face_index) & 1).astype(np.float32)
        sign_rows.append(np.broadcast_to(1.0 - 2.0 * bit_vals[None, :], (N_GRP, N_SUB)))
    bit_grp = (grp_ids & 1).astype(np.float32)
    sign_rows.append(np.broadcast_to(1.0 - 2.0 * bit_grp[:, None], (N_GRP, N_SUB)))
    face_sign = jnp.asarray(np.stack(sign_rows, axis=-1), dtype=jnp.float32)
    positions = jnp.arange(DOFS)
    face_of = positions // face_dofs
    node_of = positions % NODES
    sign_vec = face_sign[:, :, face_of][:, :, None, :]
    live = face_nodes[:, :, face_of]
    mask_vec = (node_of[None, None, :] < live).astype(jnp.float32)[:, :, None, :]

    def jump(values):
        pieces = []
        for face_index in range(4):
            block = values[..., face_index * face_dofs:(face_index + 1) * face_dofs]
            if face_index < 3:
                across = block[:, sub_ids ^ (1 << face_index)]
            else:
                across = block[grp_ids ^ 1]
            pieces.append(block - across)
        return jnp.concatenate(pieces, axis=3) * sign_vec * mask_vec

    def local_product(vectors, matrices):
        flat_vectors = vectors.reshape(N_GRP * N_SUB, LOADS, DOFS)
        flat_matrices = matrices.reshape(N_GRP * N_SUB, DOFS, DOFS)
        result = lax.map(lambda pair: jnp.dot(pair[0], pair[1], preferred_element_type=jnp.float32), (flat_vectors, flat_matrices))
        return result.reshape(N_GRP, N_SUB, LOADS, DOFS)

    onehot = (corner_index[:, :, :, None] == positions[None, None, None, :]).astype(jnp.float32)

    def precondition(residual):
        scaled = 0.5 * sign_vec * residual
        local = local_product(scaled.astype(jnp.bfloat16), stiffness)
        index_full = jnp.broadcast_to(corner_index[:, :, None, :], (N_GRP, N_SUB, LOADS, CORNERS))
        corner_vals = jnp.take_along_axis(scaled, index_full, axis=3)
        corner_all = corner_vals.transpose(0, 2, 1, 3).reshape(N_GRP, LOADS, CDOFS)
        coarse = jnp.einsum("grm,gmn->grn", corner_all, coarse_inverse, precision=lax.Precision.HIGHEST)
        coarse = coarse.reshape(N_GRP, LOADS, N_SUB, CORNERS).transpose(0, 2, 1, 3)
        local = local + jnp.einsum("gsrk,gskd->gsrd", coarse, onehot, precision=lax.Precision.HIGHEST)
        return jump(local)

    def apply_flex(direction):
        signed = sign_vec * direction
        image = local_product(signed.astype(jnp.bfloat16), flexibility)
        return jump(image)

    def inner(first, second):
        return jnp.sum(first * second, axis=(0, 1, 3))

    residual = loads * mask_vec
    multipliers = jnp.zeros_like(residual)
    zvec = precondition(residual)
    direction = zvec
    rz_now = inner(residual, zvec)
    for iteration in range(ITERS):
        image = apply_flex(direction)
        alpha = (rz_now / inner(direction, image))[:, None]
        multipliers = multipliers + alpha * direction
        residual = residual - alpha * image
        zvec = precondition(residual)
        rz_next = inner(residual, zvec)
        direction = zvec + (rz_next / rz_now)[:, None] * direction
        rz_now = rz_next
    return multipliers, direction
```

```python
import jax
import jax.numpy as jnp
from jax import lax
from jax.sharding import PartitionSpec as P

HI = lax.Precision.HIGHEST
NT = (((1,), (1,)), ((), ()))
TN = (((0,), (0,)), ((), ()))
NN = (((1,), (0,)), ((), ()))
Q4 = 4


def dot32(a, b, dims):
    return lax.dot_general(a, b, dims, precision=HI, preferred_element_type=jnp.float32)


def dot16(a, b):
    return lax.dot_general(a, b, NN, preferred_element_type=jnp.float32)


def swap(block, axis, distance):
    count = lax.axis_size(axis)
    return lax.ppermute(block, axis, [(i, i ^ distance) for i in range(count) if i ^ distance < count])


def exchange(field):
    width = field.shape[1] // 4
    face = [field[:, f * width : (f + 1) * width] for f in range(4)]
    return [swap(face[0], "sub", 1), swap(face[1], "sub", 2), swap(face[2], "sub", 4), swap(face[3], "grp", 1)]


def send_all(blocks):
    return lax.all_to_all(blocks, ("grp", "sub"), 0, 0, tiled=True)


def pack(columns):
    rows = columns.shape[0] // 4
    return jnp.concatenate([columns[r * rows : (r + 1) * rows] for r in range(4)], axis=1)


def unpack(lanes):
    loads = lanes.shape[1] // 4
    return jnp.concatenate([lanes[:, r * loads : (r + 1) * loads] for r in range(4)], axis=0)


def column(row):
    n = row.shape[1]
    eye = (lax.broadcasted_iota(jnp.int32, (n, n), 0) == lax.broadcasted_iota(jnp.int32, (n, n), 1))
    return jnp.sum(jnp.where(eye, row, 0.0), axis=1, keepdims=True)


def row_sum(product):
    return dot32(jnp.ones((1, product.shape[1]), jnp.float32), product, NT)


def jump(field, across, sign_mask):
    return (field - jnp.concatenate(across, axis=1)) * sign_mask


def contributions(image, corner_map, own_inverse, cross_inverse, sign_vec, scalars, groups, grp_pos):
    half = corner_map.shape[0] // 2
    corner = dot32(corner_map, 0.5 * sign_vec * image, NT)
    own = pack(dot32(own_inverse, corner[:half], NN))
    cross = pack(dot32(cross_inverse, corner[half:], NN))
    n_row = own.shape[0]
    is_last = lax.broadcasted_iota(jnp.int32, (n_row, 1), 0) % 4 == 3
    totals = jnp.where(is_last, jnp.concatenate(scalars, axis=1), 0.0)
    blocks = []
    for g in range(groups):
        blocks.append(totals + jnp.where(g == grp_pos, own, jnp.where(g == grp_pos ^ 1, cross, 0.0)))
    return jnp.stack(blocks)


def body(loads, stiffness, flexibility, coarse_inverse, face_nodes, corner_index):
    rhs, stiff, flex = loads[0, 0], stiffness[0, 0], flexibility[0, 0]
    live_nodes, ids = face_nodes[0, 0], corner_index[0, 0]
    n_load, dofs = rhs.shape
    face_dofs = dofs // 4
    nodes = face_dofs // 3
    corners = ids.shape[0]
    n_q = corners // 4
    groups, subs = lax.axis_size("grp"), lax.axis_size("sub")
    n_dev = groups * subs
    sub_pos, grp_pos = lax.axis_index("sub"), lax.axis_index("grp")

    position = jnp.arange(dofs)[None, :]
    face_of = position // face_dofs
    bits = jnp.stack([sub_pos & 1, sub_pos >> 1 & 1, sub_pos >> 2 & 1, grp_pos & 1])
    sign_vec = jnp.zeros((1, dofs), jnp.float32)
    live = jnp.zeros((1, dofs), jnp.int32)
    for f in range(4):
        sign_vec = jnp.where(face_of == f, 1.0 - 2.0 * bits[f].astype(jnp.float32), sign_vec)
        live = jnp.where(face_of == f, live_nodes[f], live)
    mask_vec = (position % nodes < live).astype(jnp.float32)
    sign_mask = sign_vec * mask_vec

    id_rq = jnp.pad(ids.reshape(n_q, 4), ((0, Q4 - n_q), (0, 0)), constant_values=-1).T.reshape(-1, 1)
    onehot = (id_rq == position).astype(jnp.float32)
    place = jnp.arange(subs * 16)[:, None]
    source = place % (subs * 4) // 4 * corners + place % 4 * 4 + place // (subs * 4)
    valid = place % 4 < n_q
    select = ((jnp.arange(subs * corners)[None, :] == source) & valid).astype(jnp.float32)
    own_inverse = dot32(dot32(select, coarse_inverse[0], NN), select, NT)
    cross_inverse = swap(own_inverse, "grp", 1)

    resid = rhs * mask_vec
    scaled = 0.5 * sign_vec * resid
    packed = pack(dot32(onehot, scaled, NT))
    packed_ids = pack(jnp.broadcast_to(id_rq.astype(jnp.float32), (16, n_load)))
    first = jnp.concatenate([packed, packed_ids], axis=0)
    first = send_all(jnp.broadcast_to(first[None], (n_dev,) + first.shape))
    local = dot16(scaled.astype(jnp.bfloat16), stiff)
    across = exchange(local)

    first = first.reshape(groups, subs, 2, 4, 4 * n_load)
    corner_map, field, own_field = [], [], []
    coarse = []
    sub_row = jnp.tile(jnp.repeat(jnp.arange(subs), 4), 4)[:, None]
    is_own = (sub_row == sub_pos).astype(jnp.float32)
    for which, matrix in ((grp_pos, own_inverse), (grp_pos ^ 1, cross_inverse)):
        pair = lax.dynamic_index_in_dim(first, which, 0, keepdims=False)
        values = unpack(pair[:, 0].reshape(subs * 4, -1))
        id_rows = unpack(pair[:, 1].reshape(subs * 4, -1))[:, :1]
        here = (id_rows == position.astype(jnp.float32)).astype(jnp.float32)
        coarse.append(dot32(matrix, values, NN))
        if len(coarse) == 1:
            weight = is_own
            for f in range(3):
                weight = weight - jnp.where(face_of == f, (sub_row == sub_pos ^ 1 << f).astype(jnp.float32), 0.0)
            own_field = dot32(coarse[0], here * is_own, TN)
        else:
            weight = -jnp.where(face_of == 3, is_own, 0.0)
        corner_map.append(here * weight * sign_mask)
    corner_map = jnp.concatenate(corner_map, axis=0)
    coarse = jnp.concatenate(coarse, axis=0)
    zvec = jump(local, across, sign_mask) + dot32(coarse, corner_map, TN)
    zero = jnp.zeros((1, n_load), jnp.float32)

    def spread(image, scalars):
        blocks = contributions(
            image, corner_map, own_inverse, cross_inverse, sign_vec, scalars, groups, grp_pos
        )
        return send_all(blocks.reshape(n_dev, 4, 4 * n_load))

    def collect(received):
        total = unpack(jnp.sum(received, axis=0))
        return dot32(total, onehot, TN), [total[4 * i + 3 : 4 * i + 4] for i in range(4)]

    signed = sign_vec * zvec
    image = dot16(signed.astype(jnp.bfloat16), flex)
    rz_part = row_sum(resid * zvec)
    curve_part = 2.0 * row_sum(signed * image)
    received = spread(image, [rz_part, curve_part, zero, zero])
    across = exchange(image)

    image_field, (rz0, curve0, _, _) = collect(received)
    flexed = jump(image, across, sign_mask)
    alpha = column(rz0 / curve0)
    mult = alpha * zvec
    resid = resid - alpha * flexed
    local_coarse = own_field - alpha * image_field
    local = dot16((0.5 * sign_vec * resid).astype(jnp.bfloat16), stiff) + local_coarse
    across = exchange(local)

    znew = jump(local, across, sign_mask)
    signed = sign_vec * znew
    high = signed.astype(jnp.bfloat16)
    low = (signed - high.astype(jnp.float32)).astype(jnp.bfloat16)
    both = dot16(jnp.concatenate([high, low], axis=0), flex)
    image = both[:n_load] + both[n_load:]
    parts = [row_sum(resid * znew), 2.0 * row_sum(signed * image), row_sum(znew * flexed), zero]
    received = spread(image, parts)
    across = exchange(image)

    new_field, (rz1, curve_zz, curve_zd, _) = collect(received)
    beta_row = rz1 / rz0
    beta = column(beta_row)
    flexed = jump(image, across, sign_mask) + beta * flexed
    direction = znew + beta * zvec
    alpha = column(rz1 / (curve_zz + 2.0 * beta_row * curve_zd + beta_row * beta_row * curve0))
    mult = mult + alpha * direction
    resid = resid - alpha * flexed
    local_coarse = local_coarse - alpha * (new_field + beta * image_field)
    local = dot16((0.5 * sign_vec * resid).astype(jnp.bfloat16), stiff) + local_coarse
    last = jnp.concatenate([2.0 * row_sum(sign_vec * resid * local), zero, zero, zero], axis=1)
    received = send_all(jnp.broadcast_to(last[None], (n_dev, 1, 4 * n_load)))
    across = exchange(local)
    rz2 = jnp.sum(received, axis=0)[:, :n_load]
    direction = jump(local, across, sign_mask) + column(rz2 / rz1) * direction
    return (mult[None, None], direction[None, None])


def solution(mesh):
    in_specs = (
        P("grp", "sub", None, None),
        P("grp", "sub", None, None),
        P("grp", "sub", None, None),
        P("grp", None, None),
        P("grp", "sub", None),
        P("grp", "sub", None),
    )
    out_specs = (P("grp", "sub", None, None), P("grp", "sub", None, None))
    return jax.shard_map(body, mesh=mesh, in_specs=in_specs, out_specs=out_specs, check_vma=False)
```

```python
import functools

import jax
import jax.numpy as jnp
from jax import lax
from jax.experimental import pallas as pl
from jax.experimental.pallas import tpu as pltpu
from jax.sharding import PartitionSpec as P

F32, BF16 = jnp.float32, jnp.bfloat16
NT = (((1,), (1,)), ((), ()))
NN = (((1,), (0,)), ((), ()))
LANES = 128


def exact(a, b, dims=NN):
    return lax.dot_general(a, b, dims, precision=lax.Precision.HIGHEST, preferred_element_type=F32)


def rounded(a, b):
    return lax.dot_general(a, b, NN, preferred_element_type=F32)


def thirds(x):
    high = x.astype(BF16)
    rest = x - high.astype(F32)
    mid = rest.astype(BF16)
    return jnp.concatenate([high, mid, (rest - mid.astype(F32)).astype(BF16)], axis=0)


def by_map(x, corner_map, dims):
    n = x.shape[0]
    out = lax.dot_general(thirds(x), corner_map, dims, preferred_element_type=F32)
    return out[:n] + out[n : 2 * n] + out[2 * n :]


def iota(shape, axis):
    return lax.broadcasted_iota(jnp.int32, shape, axis)


def windows(dofs):
    width = dofs // 4
    return [(f * width // LANES * LANES, -(-(f + 1) * width // LANES) * LANES) for f in range(4)]


def face_vectors(info, nodes_ref, dofs):
    width = dofs // 4
    pos = iota((1, dofs), 1)
    sub_pos, grp_pos = info[0], info[1]
    bits = [sub_pos & 1, (sub_pos >> 1) & 1, (sub_pos >> 2) & 1, grp_pos & 1]
    sign = jnp.zeros((1, dofs), F32)
    live = jnp.zeros((1, dofs), jnp.int32)
    node = pos
    for f in range(4):
        inside = (pos >= f * width) & (pos < (f + 1) * width)
        sign = jnp.where(inside, (1 - 2 * bits[f]).astype(F32), sign)
        live = jnp.where(inside, nodes_ref[f], live)
    for step in range(1, 12):
        node = jnp.where(pos >= step * (width // 3), pos - step * (width // 3), node)
    mask = jnp.where(node < live, 1.0, 0.0)
    return sign, mask


def corner_rows(ids_ref, dofs):
    row = iota((16, 1), 0)
    ids = jnp.full((16, 1), -1, jnp.int32)
    for k in range(ids_ref.shape[0]):
        ids = jnp.where(row == 4 * (k % 4) + k // 4, ids_ref[k], ids)
    return jnp.where(ids == iota((16, dofs), 1), 1.0, 0.0)


def across(wins, dofs):
    spans, width = windows(dofs), dofs // 4
    n = wins[0].shape[0]
    tiles = []
    for low in range(0, dofs, LANES):
        tile = None
        for f, (start, stop) in enumerate(spans):
            if start <= low < stop:
                part = wins[f][:, low - start : low - start + LANES]
                tile = part if tile is None else jnp.where(iota((n, LANES), 1) + low < f * width, tile, part)
        tiles.append(tile)
    return jnp.concatenate(tiles, axis=1)


def put_windows(refs, field):
    for ref, (start, stop) in zip(refs, windows(field.shape[1])):
        ref[: field.shape[0], :] = field[:, start:stop]


def same_block(n_row, n_col, row_block, col_block):
    return iota((n_row, n_col), 0) // row_block == iota((n_row, n_col), 1) // col_block


def to_column(row):
    n = row.shape[1]
    return jnp.sum(jnp.where(same_block(n, n, 1, 1), row, 0.0), axis=1, keepdims=True)


def to_row(column):
    n = column.shape[0]
    return jnp.sum(jnp.where(same_block(n, n, 1, 1), column, 0.0), axis=0, keepdims=True)


def total_of(received):
    total = received[0:8]
    for low in range(8, received.shape[0], 8):
        total = total + received[low : low + 8]
    return total + pltpu.roll(total, 4, 0)


def sums_of(total, n_load):
    column = to_column(total[3:4])
    return [column[i * n_load : (i + 1) * n_load] for i in range(4)]


def corner_field(total, ids_ref, n_load, dofs):
    flipped = total.T
    pos = iota((1, dofs), 1)
    field = jnp.zeros((n_load, dofs), F32)
    for k in range(ids_ref.shape[0]):
        q, r = k // 4, k % 4
        field = jnp.where(pos == ids_ref[k], flipped[r * n_load : (r + 1) * n_load, q : q + 1], field)
    return field


def put_contributions(ref, image, corner_map, spread, sign, sums, info, groups):
    n_load = image.shape[0]
    at_corners = by_map(0.5 * sign * image, corner_map, NT)
    tiled = jnp.concatenate([at_corners] * 4, axis=0)
    n, n_corner = tiled.shape
    inner = iota((n, n_corner), 1) < 64
    pair = jnp.concatenate([jnp.where(inner, tiled, 0.0), jnp.where(inner, 0.0, tiled)], axis=0)
    full = exact(spread, pair, NT)
    rows = full.shape[0] // 4
    keep = iota((4 * rows, 2 * n), 0) // rows == iota((4 * rows, 2 * n), 1) % n // n_load
    full = jnp.where(keep, full, 0.0)
    packed = full[:rows] + full[rows : 2 * rows] + full[2 * rows : 3 * rows] + full[3 * rows :]
    zero = jnp.zeros((n_load, 1), F32)
    sums = to_row(jnp.concatenate(sums + [zero] * (4 - len(sums)), axis=0))
    is_last = iota((rows, 1), 0) % 4 == 3
    totals = jnp.where(is_last, sums, 0.0)
    for g in range(groups):
        same, near = g == info[1], g == (info[1] ^ 1)
        ref[g * rows : (g + 1) * rows, :] = totals + jnp.where(same, packed[:, :n], jnp.where(near, packed[:, n:], 0.0))


def first_corners(info, nodes, ids, loads, out):
    dofs, n_load = loads.shape[1], loads.shape[0]
    sign, mask = face_vectors(info, nodes, dofs)
    scaled = 0.5 * sign * (loads[...] * mask)
    values = by_map(scaled, corner_rows(ids, dofs).astype(BF16), NT)
    flipped = jnp.concatenate([values] * 4, axis=0).T
    flipped = jnp.where(same_block(16, 4 * n_load, 4, n_load), flipped, 0.0)
    block = flipped[:8] + flipped[8:]
    block = block + pltpu.roll(block, 4, 0)
    for low in range(0, out.shape[0], 8):
        out[low : low + 8, :] = block


def first_local(info, nodes, ids, loads, stiff, inverse, local_out, spread_out, *wins):
    dofs = loads.shape[1]
    sign, mask = face_vectors(info, nodes, dofs)
    scaled = 0.5 * sign * (loads[...] * mask)
    local = rounded(scaled.astype(BF16), stiff[...])
    local_out[...] = local
    put_windows(wins, local)
    corner = corner_rows(ids, dofs)
    for ref, (start, stop) in zip(wins, windows(dofs)):
        ref[32:48, :] = corner[:, start:stop]
    n = inverse.shape[0]
    corners = ids.shape[0]
    subs = n // corners
    sub_pos = info[0]
    row = iota((64, 1), 0)
    owner = jnp.where(row < 16, sub_pos, jnp.where(row < 32, sub_pos ^ 1, jnp.where(row < 48, sub_pos ^ 2, sub_pos ^ 4)))
    source = owner * corners + row % 4 * 4 + row // 4 % 4
    pick = jnp.where((source == iota((64, n), 1)) & (row % 4 * 4 < corners), 1.0, 0.0)
    place = iota((16 * subs, 1), 0)
    source = place // 4 % subs * corners + place % 4 * 4 + place // (4 * subs)
    order = jnp.where((source == iota((16 * subs, n), 1)) & (place % 4 * 4 < corners), 1.0, 0.0)
    spread = exact(exact(pick, inverse[...]), order, NT)
    spread_out[...] = spread
    last = wins[3]
    wide = last.shape[1]
    n_piece = (last.shape[0] - 48) // 16
    own = jnp.concatenate([spread[:16], jnp.zeros((16, max(n_piece * wide - 16 * subs, LANES)), F32)], axis=1)
    for i in range(n_piece):
        last[48 + 16 * i : 64 + 16 * i, :] = own[:, i * wide : (i + 1) * wide]


def maps(info, nodes, ids, local, spread, w0, w1, w2, w3, jumped_out, map_out, spread_out):
    n_load, dofs = local.shape
    sign, mask = face_vectors(info, nodes, dofs)
    sign_mask = sign * mask
    wins = [w0, w1, w2, w3]
    jumped_out[...] = (local[...] - across([w[:n_load, :] for w in wins], dofs)) * sign_mask
    map_out[0:16, :] = (corner_rows(ids, dofs) * sign_mask).astype(BF16)
    other = across([w[32:48, :] for w in wins], dofs) * sign_mask
    width = dofs // 4
    for f in range(4):
        pos = iota((1, dofs), 1)
        inside = (pos >= f * width) & (pos < (f + 1) * width)
        map_out[16 + 16 * f : 32 + 16 * f, :] = jnp.where(inside, -other, 0.0).astype(BF16)
    pieces = [w3[low : low + 16, :] for low in range(48, w3.shape[0], 16)]
    cross = pieces[0] if len(pieces) == 1 else jnp.concatenate(pieces, axis=1)
    rows = jnp.concatenate([spread[...], cross[:, : spread.shape[1]], jnp.zeros((48, spread.shape[1]), F32)], axis=0)
    spread_out[...] = rows.T[:, :80]


def first_image(
    groups, info, nodes, received, loads, jumped, corner_map, spread, flex, z_out, image_out, own_out, out, *wins
):
    n_load, dofs = loads.shape
    sign, mask = face_vectors(info, nodes, dofs)
    rows = spread.shape[0] // 4
    coarse = None
    for which, inner in ((info[1], True), (info[1] ^ 1, False)):
        block = received[pl.ds(pl.multiple_of(which * rows, 8), rows), :]
        flipped = block.T
        part = jnp.zeros((n_load, 80), F32)
        for r in range(4):
            part = part + exact(flipped[r * n_load : (r + 1) * n_load], spread[r * rows : (r + 1) * rows, :])
        coarse = part if coarse is None else jnp.where(iota((n_load, 80), 1) < 64, coarse, part)
    own = jnp.where(iota((n_load, 80), 1) < 16, coarse, 0.0)
    fields = by_map(jnp.concatenate([coarse, own], axis=0), corner_map[...], NN)
    zvec = jumped[...] + fields[:n_load]
    own_out[...] = sign * fields[n_load:]
    z_out[...] = zvec
    signed = sign * zvec
    image = rounded(signed.astype(BF16), flex[...])
    image_out[...] = image
    put_windows(wins, image)
    rz = jnp.sum(loads[...] * mask * zvec, axis=1, keepdims=True)
    curve = 2.0 * jnp.sum(signed * image, axis=1, keepdims=True)
    put_contributions(out, image, corner_map[...], spread[...], sign, [rz, curve], info, groups)


def second_local(
    info, nodes, ids, received, image, a0, a1, a2, a3, zvec, loads, own, stiff,
    resid_out, flexed_out, mult_out, own_out, added_out, total_out, local_out, *wins,
):
    n_load, dofs = loads.shape
    sign, mask = face_vectors(info, nodes, dofs)
    total = total_of(received)
    total_out[...] = total
    rz, curve, _, _ = sums_of(total, n_load)
    alpha = rz / curve
    flexed = (image[...] - across([a0, a1, a2, a3], dofs)) * (sign * mask)
    flexed_out[...] = flexed
    mult_out[...] = alpha * zvec[...]
    resid = loads[...] * mask - alpha * flexed
    resid_out[...] = resid
    added = corner_field(total, ids, n_load, dofs)
    added_out[...] = added
    own_new = own[...] - alpha * added
    own_out[...] = own_new
    local = rounded((0.5 * sign * resid).astype(BF16), stiff[...]) + own_new
    local_out[...] = local
    put_windows(wins, local)


def second_image(
    groups, info, nodes, local, a0, a1, a2, a3, resid, flexed, corner_map, spread, flex, z_out, image_out, out, *wins
):
    n_load, dofs = local.shape
    sign, mask = face_vectors(info, nodes, dofs)
    zvec = (local[...] - across([a0, a1, a2, a3], dofs)) * (sign * mask)
    z_out[...] = zvec
    signed = sign * zvec
    high = signed.astype(BF16)
    low = (signed - high.astype(F32)).astype(BF16)
    both = rounded(jnp.concatenate([high, low], axis=0), flex[...])
    image = both[:n_load] + both[n_load:]
    image_out[...] = image
    put_windows(wins, image)
    rz = jnp.sum(resid[...] * zvec, axis=1, keepdims=True)
    curve = 2.0 * jnp.sum(signed * image, axis=1, keepdims=True)
    mixed = jnp.sum(zvec * flexed[...], axis=1, keepdims=True)
    put_contributions(out, image, corner_map[...], spread[...], sign, [rz, curve, mixed], info, groups)


def third_local(
    info, nodes, ids, received, before, image, a0, a1, a2, a3, zold, znew, flexed, resid, mult, own, added, stiff,
    mult_out, direction_out, local_out, total_out, out, *wins,
):
    n_load, dofs = image.shape
    sign, mask = face_vectors(info, nodes, dofs)
    total = total_of(received)
    total_out[...] = total
    rz0, curve0, _, _ = sums_of(before[...], n_load)
    rz1, curve_new, curve_mixed, _ = sums_of(total, n_load)
    beta = rz1 / rz0
    alpha = rz1 / (curve_new + 2.0 * beta * curve_mixed + beta * beta * curve0)
    flexed_new = (image[...] - across([a0, a1, a2, a3], dofs)) * (sign * mask) + beta * flexed[...]
    direction = znew[...] + beta * zold[...]
    direction_out[...] = direction
    mult_out[...] = mult[...] + alpha * direction
    resid_new = resid[...] - alpha * flexed_new
    own_new = own[...] - alpha * (corner_field(total, ids, n_load, dofs) + beta * added[...])
    local = rounded((0.5 * sign * resid_new).astype(BF16), stiff[...]) + own_new
    local_out[...] = local
    put_windows(wins, local)
    rz2 = 2.0 * jnp.sum(sign * resid_new * local, axis=1, keepdims=True)
    zero = jnp.zeros((n_load, 1), F32)
    block = jnp.where(iota((8, 1), 0) % 4 == 3, to_row(jnp.concatenate([rz2, zero, zero, zero], axis=0)), 0.0)
    for low in range(0, out.shape[0], 8):
        out[low : low + 8, :] = block


def last_direction(info, nodes, received, before, local, a0, a1, a2, a3, direction, out):
    n_load, dofs = local.shape
    sign, mask = face_vectors(info, nodes, dofs)
    rz2 = sums_of(total_of(received), n_load)[0]
    rz1 = sums_of(before[...], n_load)[0]
    zvec = (local[...] - across([a0, a1, a2, a3], dofs)) * (sign * mask)
    out[...] = zvec + (rz2 / rz1) * direction[...]


def call(name, kernel, n_scalar, args, outs):
    shapes = [jax.ShapeDtypeStruct(s, d) for s, d in outs]
    n_bytes = sum(a.size * a.dtype.itemsize for a in args) + sum(s.size * s.dtype.itemsize for s in shapes)
    smem, vmem = pl.BlockSpec(memory_space=pltpu.SMEM), pl.BlockSpec(memory_space=pltpu.VMEM)
    return pl.pallas_call(
        kernel,
        out_shape=shapes,
        in_specs=[smem] * n_scalar + [vmem] * (len(args) - n_scalar),
        out_specs=[vmem] * len(shapes),
        cost_estimate=pl.CostEstimate(flops=40_000_000, bytes_accessed=n_bytes, transcendentals=0),
        compiler_params=pltpu.CompilerParams(vmem_limit_bytes=32 * 2**20),
        name=name,
    )(*args)


def swap(block, axis, distance):
    count = lax.axis_size(axis)
    return lax.ppermute(block, axis, [(i, i ^ distance) for i in range(count) if i ^ distance < count])


def exchange(wins):
    return [swap(wins[0], "sub", 1), swap(wins[1], "sub", 2), swap(wins[2], "sub", 4), swap(wins[3], "grp", 1)]


def send_all(rows):
    devices = lax.axis_size("grp") * lax.axis_size("sub")
    blocks = rows.reshape(devices, 4, rows.shape[1])
    return lax.all_to_all(blocks, ("grp", "sub"), 0, 0, tiled=True).reshape(rows.shape)


def body(loads, stiffness, flexibility, coarse_inverse, face_nodes, corner_index):
    rhs, stiff, flex, inverse = loads[0, 0], stiffness[0, 0], flexibility[0, 0], coarse_inverse[0]
    nodes, ids = face_nodes[0, 0], corner_index[0, 0]
    n_load, dofs = rhs.shape
    groups, subs = lax.axis_size("grp"), lax.axis_size("sub")
    info = jnp.stack([lax.axis_index("sub"), lax.axis_index("grp")])
    field = ((n_load, dofs), F32)
    sent = ((groups * subs * 4, 4 * n_load), F32)
    total = ((8, 4 * n_load), F32)
    spans = [stop - start for start, stop in windows(dofs)]
    wins = [((n_load, w), F32) for w in spans]
    extra = -(-16 * subs // spans[3]) * 16
    wide = [((48, w), F32) for w in spans[:3]] + [((48 + extra, spans[3]), F32)]

    (corners,) = call("corners1", first_corners, 3, [info, nodes, ids, rhs], [sent])
    corners = send_all(corners)
    local, spread, *faces = call(
        "local1", first_local, 3, [info, nodes, ids, rhs, stiff, inverse], [field, ((64, 16 * subs), F32)] + wide
    )
    faces = exchange(faces)
    jumped, corner_map, spread = call(
        "maps", maps, 3, [info, nodes, ids, local, spread] + faces, [field, ((80, dofs), BF16), ((16 * subs, 80), F32)]
    )
    zold, image, own, sums, *faces = call(
        "image1", functools.partial(first_image, groups), 2,
        [info, nodes, corners, rhs, jumped, corner_map, spread, flex], [field, field, field, sent] + wins,
    )
    sums = send_all(sums)
    faces = exchange(faces)
    resid, flexed, mult, own, added, before, local, *faces = call(
        "local2", second_local, 3, [info, nodes, ids, sums, image] + faces + [zold, rhs, own, stiff],
        [field] * 5 + [total, field] + wins,
    )
    faces = exchange(faces)
    znew, image, sums, *faces = call(
        "image2", functools.partial(second_image, groups), 2,
        [info, nodes, local] + faces + [resid, flexed, corner_map, spread, flex], [field, field, sent] + wins,
    )
    sums = send_all(sums)
    faces = exchange(faces)
    mult, direction, local, before, sums, *faces = call(
        "local3", third_local, 3,
        [info, nodes, ids, sums, before, image] + faces + [zold, znew, flexed, resid, mult, own, added, stiff],
        [field, field, field, total, sent] + wins,
    )
    sums = send_all(sums)
    faces = exchange(faces)
    (direction,) = call(
        "direction", last_direction, 2, [info, nodes, sums, before, local] + faces + [direction], [field]
    )
    return (mult[None, None], direction[None, None])


def solution(mesh):
    in_specs = (
        P("grp", "sub", None, None),
        P("grp", "sub", None, None),
        P("grp", "sub", None, None),
        P("grp", None, None),
        P("grp", "sub", None),
        P("grp", "sub", None),
    )
    out_specs = (P("grp", "sub", None, None), P("grp", "sub", None, None))
    return jax.shard_map(body, mesh=mesh, in_specs=in_specs, out_specs=out_specs, check_vma=False)
```

```python
import functools

import jax
import jax.numpy as jnp
from jax import lax
from jax.experimental import pallas as pl
from jax.experimental.pallas import tpu as pltpu
from jax.sharding import PartitionSpec as P

F32, BF16 = jnp.float32, jnp.bfloat16
NT = (((1,), (1,)), ((), ()))
NN = (((1,), (0,)), ((), ()))
LANES = 128


def exact(a, b, dims=NN):
    return lax.dot_general(a, b, dims, precision=lax.Precision.HIGHEST, preferred_element_type=F32)


def rounded(a, b):
    return lax.dot_general(a, b, NN, preferred_element_type=F32)


def thirds(x):
    high = x.astype(BF16)
    rest = x - high.astype(F32)
    mid = rest.astype(BF16)
    return jnp.concatenate([high, mid, (rest - mid.astype(F32)).astype(BF16)], axis=0)


def by_map(x, corner_map, dims):
    n = x.shape[0]
    out = lax.dot_general(thirds(x), corner_map, dims, preferred_element_type=F32)
    return out[:n] + out[n : 2 * n] + out[2 * n :]


def iota(shape, axis):
    return lax.broadcasted_iota(jnp.int32, shape, axis)


def windows(dofs):
    width = dofs // 4
    return [(f * width // LANES * LANES, -(-(f + 1) * width // LANES) * LANES) for f in range(4)]


def face_vectors(nodes_ref, dofs):
    width = dofs // 4
    pos = iota((1, dofs), 1)
    sub_pos, grp_pos = lax.axis_index("sub"), lax.axis_index("grp")
    bits = [sub_pos & 1, (sub_pos >> 1) & 1, (sub_pos >> 2) & 1, grp_pos & 1]
    sign = jnp.zeros((1, dofs), F32)
    live = jnp.zeros((1, dofs), jnp.int32)
    node = pos
    for f in range(4):
        inside = (pos >= f * width) & (pos < (f + 1) * width)
        sign = jnp.where(inside, (1 - 2 * bits[f]).astype(F32), sign)
        live = jnp.where(inside, nodes_ref[f], live)
    for step in range(1, 12):
        node = jnp.where(pos >= step * (width // 3), pos - step * (width // 3), node)
    mask = jnp.where(node < live, 1.0, 0.0)
    return sign, mask


def corner_rows(ids_ref, dofs):
    row = iota((16, 1), 0)
    ids = jnp.full((16, 1), -1, jnp.int32)
    for k in range(ids_ref.shape[0]):
        ids = jnp.where(row == 4 * (k % 4) + k // 4, ids_ref[k], ids)
    return jnp.where(ids == iota((16, dofs), 1), 1.0, 0.0)


def across(wins, dofs):
    spans, width = windows(dofs), dofs // 4
    n = wins[0].shape[0]
    tiles = []
    for low in range(0, dofs, LANES):
        tile = None
        for f, (start, stop) in enumerate(spans):
            if start <= low < stop:
                part = wins[f][:, low - start : low - start + LANES]
                tile = part if tile is None else jnp.where(iota((n, LANES), 1) + low < f * width, tile, part)
        tiles.append(tile)
    return jnp.concatenate(tiles, axis=1)


def put_windows(refs, field):
    for ref, (start, stop) in zip(refs, windows(field.shape[1])):
        ref[: field.shape[0], :] = field[:, start:stop]


def same_block(n_row, n_col, row_block, col_block):
    return iota((n_row, n_col), 0) // row_block == iota((n_row, n_col), 1) // col_block


def to_column(row):
    n = row.shape[1]
    return jnp.sum(jnp.where(same_block(n, n, 1, 1), row, 0.0), axis=1, keepdims=True)


def to_row(column):
    n = column.shape[0]
    return jnp.sum(jnp.where(same_block(n, n, 1, 1), column, 0.0), axis=0, keepdims=True)


def total_of(received):
    total = received[0:8]
    for low in range(8, received.shape[0], 8):
        total = total + received[low : low + 8]
    return total + pltpu.roll(total, 4, 0)


def sums_of(total, n_load):
    column = to_column(total[3:4])
    return [column[i * n_load : (i + 1) * n_load] for i in range(4)]


def halves(x):
    high = x.astype(BF16)
    return jnp.concatenate([high, (x - high.astype(F32)).astype(BF16)], axis=0)


def fine(x, matrix):
    n = x.shape[0]
    both = rounded(halves(x), matrix)
    return both[:n] + both[n:]


def finer(x, matrix):
    n = x.shape[0]
    high = matrix.astype(BF16)
    parts = halves(x)
    both = rounded(parts, high)
    return both[:n] + both[n:] + rounded(parts[:n], (matrix - high.astype(F32)).astype(BF16))


def packed_corners(scaled, corner):
    n_load = scaled.shape[0]
    values = by_map(scaled, corner.astype(BF16), NT)
    flipped = jnp.concatenate([values] * 4, axis=0).T
    flipped = jnp.where(same_block(16, 4 * n_load, 4, n_load), flipped, 0.0)
    block = flipped[:8] + flipped[8:]
    return block + pltpu.roll(block, 4, 0)


def with_sums(block, sums):
    zero = jnp.zeros_like(sums[0])
    row = to_row(jnp.concatenate(sums + [zero] * (4 - len(sums)), axis=0))
    return jnp.where(iota(block.shape, 0) % 4 == 3, row, block)


def put_all(out, block):
    for low in range(0, out.shape[0], 8):
        out[low : low + 8, :] = block


def group_corners(received, which, rows, n_load):
    block = received[pl.ds(pl.multiple_of(which * rows, 8), rows), :]
    block = jnp.where(iota(block.shape, 0) % 4 == 3, 0.0, block)
    tall = jnp.concatenate([block] * 4, axis=0)
    flipped = jnp.where(same_block(4 * rows, 4 * n_load, rows, n_load), tall, 0.0).T
    return sum(flipped[r * n_load : (r + 1) * n_load] for r in range(1, 4)) + flipped[:n_load]


def coarse_of(received, spread, n_load):
    rows = spread.shape[0] // 4
    grp_pos = lax.axis_index("grp")
    inner = finer(group_corners(received, grp_pos, rows, n_load), spread)
    outer = finer(group_corners(received, grp_pos ^ 1, rows, n_load), spread)
    return jnp.where(iota(inner.shape, 1) < 64, inner, outer)


def to_wide(matrix, wide):
    n = matrix.shape[0]
    if n < wide:
        return jnp.concatenate([matrix[: n // 2], matrix[n // 2 :]], axis=1)
    return jnp.concatenate([matrix[:, low : low + wide] for low in range(0, n, wide)], axis=0)


def from_wide(rows, n):
    wide = rows.shape[1]
    if n < wide:
        return jnp.concatenate([rows[:, :n], rows[:, n:]], axis=0)
    return jnp.concatenate([rows[low : low + n] for low in range(0, rows.shape[0], n)], axis=1)


def rows_sum(x):
    return jnp.sum(x, axis=1, keepdims=True)


def start(
    rhs_hbm, stiff_hbm, inverse_hbm, nodes_hbm, ids_hbm,
    sent, local_out, vectors, corner_out, resid_out, spread_out, coarse_out, w0, w1, w2, w3,
    rhs, stiff, inverse, nodes, ids, sems,
):
    pairs = [(nodes_hbm, nodes), (ids_hbm, ids), (rhs_hbm, rhs), (inverse_hbm, inverse), (stiff_hbm, stiff)]
    copies = [pltpu.make_async_copy(a, b, sems.at[i]) for i, (a, b) in enumerate(pairs)]
    for copy in copies:
        copy.start()
    n_load, dofs = rhs.shape
    wins = [w0, w1, w2, w3]
    copies[0].wait()
    sign, mask = face_vectors(nodes, dofs)
    vectors[0:1, :] = sign
    vectors[1:2, :] = mask
    vectors[2:3, :] = sign * mask
    vectors[3:8, :] = jnp.zeros((5, dofs), F32)
    copies[1].wait()
    corner = corner_rows(ids, dofs)
    corner_out[...] = corner
    for ref, (low, high) in zip(wins, windows(dofs)):
        ref[2 * n_load : 2 * n_load + 16, :] = corner[:, low:high]
    copies[2].wait()
    resid = rhs[...] * mask
    resid_out[...] = resid
    scaled = 0.5 * sign * resid
    put_all(sent, packed_corners(scaled, corner))
    copies[3].wait()
    n = inverse.shape[0]
    corners = ids.shape[0]
    subs = n // corners
    sub_pos = lax.axis_index("sub")
    row = iota((64, 1), 0)
    owner = jnp.where(row < 16, sub_pos, jnp.where(row < 32, sub_pos ^ 1, jnp.where(row < 48, sub_pos ^ 2, sub_pos ^ 4)))
    source = owner * corners + row % 4 * 4 + row // 4 % 4
    pick = jnp.where((source == iota((64, n), 1)) & (row % 4 * 4 < corners), 1.0, 0.0)
    place = iota((16 * subs, 1), 0)
    source = place // 4 % subs * corners + place % 4 * 4 + place // (4 * subs)
    order = jnp.where((source == iota((16 * subs, n), 1)) & (place % 4 * 4 < corners), 1.0, 0.0)
    both = exact(exact(jnp.concatenate([pick, order], axis=0), inverse[...]), order, NT)
    spread = both[:64]
    spread_out[...] = spread
    coarse_out[...] = to_wide(both[64:], w3.shape[1])
    wide = w3.shape[1]
    low = 2 * n_load + 16
    own = spread[:16]
    if 16 * subs < wide:
        own = jnp.concatenate([own, jnp.zeros((16, wide - 16 * subs), F32)], axis=1)
    for i in range(own.shape[1] // wide):
        w3[low + 16 * i : low + 16 * i + 16, :] = own[:, i * wide : (i + 1) * wide]
    copies[4].wait()
    local = rounded(halves(scaled), stiff[...])
    local_out[...] = local
    put_windows(wins, local)


def first_image(
    received, a0, a1, a2, a3, local, vectors, corner, resid, spread, inverse, flex,
    z_out, exact_out, image_out, sums_out, map_out, spread_out, *wins,
):
    n_load, dofs = resid.shape
    both = 2 * n_load
    came = [a0, a1, a2, a3]
    sign, sign_mask = vectors[0:1, :], vectors[2:3, :]
    jumped = (local[...] - across([a[:both, :] for a in came], dofs)) * sign_mask
    own = corner[...] * sign_mask
    other = across([a[both : both + 16, :] for a in came], dofs) * sign_mask
    width = dofs // 4
    pos = iota((1, dofs), 1)
    pieces = [own]
    for f in range(4):
        pieces.append(jnp.where((pos >= f * width) & (pos < (f + 1) * width), -other, 0.0))
    corner_map = jnp.concatenate(pieces, axis=0).astype(BF16)
    map_out[...] = corner_map
    n = spread.shape[1]
    pieces = [a3[low : low + 16, :] for low in range(both + 16, a3.shape[0], 16)]
    cross = pieces[0] if len(pieces) == 1 else jnp.concatenate(pieces, axis=1)
    rows = jnp.concatenate([spread[...], cross[:, :n], jnp.zeros((48, n), F32)], axis=0)
    spread_columns = rows.T[:, :80]
    spread_out[...] = spread_columns
    coarse = coarse_of(received, spread_columns, n_load)
    zvec = jumped[:n_load] + by_map(coarse, corner_map, NN)
    z_out[...] = zvec
    exact_out[...] = zvec + jumped[n_load:]
    signed = sign * zvec
    image = rounded(signed.astype(BF16), flex[...])
    image_out[...] = image
    put_windows(wins, image)
    wins[3][n_load:, :] = inverse[...]
    sums_out[...] = with_sums(
        jnp.zeros((8, 4 * n_load), F32), [rows_sum(resid[...] * zvec), 2.0 * rows_sum(signed * image)]
    )


def second_local(
    a0, a1, a2, a3, image, sums, exact_z, vectors, corner, inverse, stiff,
    flexed_out, local_out, inverse_out, sent, *wins,
):
    n_load, dofs = image.shape
    sign, sign_mask = vectors[0:1, :], vectors[2:3, :]
    n_row = inverse.shape[0]
    inverse_out[:n_row, :] = inverse[...]
    inverse_out[n_row:, :] = a3[n_load:, :]
    flexed = (image[...] - across([a[:n_load, :] for a in [a0, a1, a2, a3]], dofs)) * sign_mask
    flexed_out[...] = flexed
    scaled = 0.5 * sign * flexed
    third = jnp.where(iota((1, 4 * n_load), 1) // n_load == 2, 1.0, 0.0)
    mixed = with_sums(jnp.zeros((8, 4 * n_load), F32), [rows_sum(exact_z[...] * flexed)] * 4) * third
    is_sum = iota((8, 1), 0) % 4 == 3
    put_all(sent, jnp.where(is_sum, sums[...] + mixed, packed_corners(scaled, corner[...])))
    local = fine(scaled, stiff[...])
    local_out[...] = local
    put_windows(wins, local)


def second_image(
    received, a0, a1, a2, a3, local, flexed, exact_z, resid, vectors, corner_map, spread, flex,
    z_out, step_out, image_out, sums_out, total_out, *wins,
):
    n_load, dofs = local.shape
    sign, sign_mask = vectors[0:1, :], vectors[2:3, :]
    total = total_of(received)
    total_out[...] = total
    rz, curve, _, _ = sums_of(total, n_load)
    alpha = rz / curve
    coarse = coarse_of(received, spread[...], n_load)
    step = (local[...] - across([a0, a1, a2, a3], dofs)) * sign_mask + by_map(coarse, corner_map[...], NN)
    step = alpha * step
    step_out[...] = step
    zvec = exact_z[...] - step
    z_out[...] = zvec
    signed = sign * zvec
    image = alpha * fine(signed, flex[...])
    image_out[...] = image
    put_windows(wins, image)
    scaled_flexed = alpha * flexed[...]
    sums = [
        rows_sum((resid[...] - scaled_flexed) * zvec),
        2.0 * rows_sum(signed * image),
        rows_sum(zvec * scaled_flexed),
    ]
    sums_out[...] = with_sums(jnp.zeros((8, 4 * n_load), F32), sums)


def third_local(a0, a1, a2, a3, image, sums, vectors, corner, stiff, local_out, sent, *wins):
    n_load, dofs = image.shape
    sign, sign_mask = vectors[0:1, :], vectors[2:3, :]
    flexed = (image[...] - across([a0, a1, a2, a3], dofs)) * sign_mask
    scaled = 0.5 * sign * flexed
    local = fine(scaled, stiff[...])
    local_out[...] = local
    put_windows(wins, local)
    fourth = jnp.where(iota((1, 4 * n_load), 1) // n_load == 3, 1.0, 0.0)
    square = with_sums(jnp.zeros((8, 4 * n_load), F32), [4.0 * rows_sum(scaled * local)] * 4) * fourth
    is_sum = iota((8, 1), 0) % 4 == 3
    put_all(sent, jnp.where(is_sum, sums[...] + square, packed_corners(scaled, corner[...])))


def finish(
    received, a0, a1, a2, a3, local, before, zold, znew, step, vectors, corner_map, spread, *rest
):
    inverses, (mult_out, direction_out) = rest[:-2], rest[-2:]
    n_load, dofs = local.shape
    sign_mask = vectors[2:3, :]
    rz0, curve0, mixed0, _ = sums_of(before[...], n_load)
    rz1, curve, mixed, square = sums_of(total_of(received), n_load)
    n = spread.shape[0]
    index = 0
    for ref in inverses:
        height = n * n // ref.shape[1]
        for low in range(0, ref.shape[0], height):
            values = group_corners(received, lax.axis_index("grp") ^ index, n // 4, n_load)
            matrix = from_wide(ref[low : low + height, :], n)
            square = square + 4.0 * rows_sum(values * finer(values, matrix))
            index += 1
    alpha = rz0 / curve0
    beta = rz1 / rz0
    gamma = rz1 / (curve + 2.0 * beta * mixed + beta * beta * rz0)
    rz2 = square + 2.0 * beta * (mixed - curve) + beta * beta * (alpha * mixed0 - mixed)
    rz2 = rz1 - 2.0 * gamma * (curve + beta * mixed) + gamma * gamma * rz2
    coarse = coarse_of(received, spread[...], n_load)
    image = (local[...] - across([a0, a1, a2, a3], dofs)) * sign_mask + by_map(coarse, corner_map[...], NN)
    direction = znew[...] + beta * zold[...]
    mult_out[...] = alpha * (zold[...] + gamma * direction)
    direction_out[...] = znew[...] - gamma * (image + beta * step[...]) + (rz2 / rz1) * direction


def call(name, kernel, args, outs, scratch=(), space=pltpu.VMEM):
    shapes = [jax.ShapeDtypeStruct(s, d) for s, d in outs]
    n_bytes = sum(a.size * a.dtype.itemsize for a in args) + sum(s.size * s.dtype.itemsize for s in shapes)
    return pl.pallas_call(
        kernel,
        out_shape=shapes,
        in_specs=[pl.BlockSpec(memory_space=space)] * len(args),
        out_specs=[pl.BlockSpec(memory_space=pltpu.VMEM)] * len(shapes),
        scratch_shapes=scratch,
        cost_estimate=pl.CostEstimate(flops=40_000_000, bytes_accessed=n_bytes, transcendentals=0),
        compiler_params=pltpu.CompilerParams(vmem_limit_bytes=(12 << 20) + 2 * n_bytes),
        name=name,
    )(*args)


def swap(block, axis, distance):
    count = lax.axis_size(axis)
    return lax.ppermute(block, axis, [(i, i ^ distance) for i in range(count) if i ^ distance < count])


def exchange(wins):
    a2 = swap(wins[2], "sub", 4)
    a1 = swap(wins[1], "sub", 2)
    a3 = swap(wins[3], "grp", 1)
    return [swap(wins[0], "sub", 1), a1, a2, a3]


def send_all(rows):
    devices = lax.axis_size("grp") * lax.axis_size("sub")
    blocks = rows.reshape(devices, 4, rows.shape[1])
    return lax.all_to_all(blocks, ("grp", "sub"), 0, 0, tiled=True).reshape(rows.shape)


def body(loads, stiffness, flexibility, coarse_inverse, face_nodes, corner_index):
    rhs, stiff, flex, inverse = loads[0, 0], stiffness[0, 0], flexibility[0, 0], coarse_inverse[0]
    nodes, ids = face_nodes[0, 0], corner_index[0, 0]
    n_load, dofs = rhs.shape
    groups, subs = lax.axis_size("grp"), lax.axis_size("sub")
    n = 16 * subs
    field = ((n_load, dofs), F32)
    sent = ((groups * subs * 4, 4 * n_load), F32)
    total = ((8, 4 * n_load), F32)
    spans = [high - low for low, high in windows(dofs)]
    wins = [((n_load, w), F32) for w in spans]
    height = 2 * n_load + 16
    wide = [((height, w), F32) for w in spans[:3]] + [((height - (-n // spans[3]) * 16, spans[3]), F32)]

    corners, local, vectors, corner, resid, spread, coarse, *faces = call(
        "start", start, [rhs, stiff, inverse, nodes, ids],
        [sent, ((2 * n_load, dofs), F32), ((8, dofs), F32), ((16, dofs), F32), field, ((64, n), F32),
         ((n * n // spans[3], spans[3]), F32)] + wide,
        [pltpu.VMEM(rhs.shape, F32), pltpu.VMEM(stiff.shape, BF16), pltpu.VMEM(inverse.shape, F32),
         pltpu.SMEM(nodes.shape, jnp.int32), pltpu.SMEM(ids.shape, jnp.int32), pltpu.SemaphoreType.DMA((5,))],
        pl.ANY,
    )
    received = send_all(corners)
    faces = exchange(faces)
    more = wins[:3] + [((n_load + coarse.shape[0], spans[3]), F32)]
    zold, exact_z, image, sums, corner_map, spread, *faces = call(
        "image1", first_image, [received] + faces + [local, vectors, corner, resid, spread, coarse, flex],
        [field, field, field, total, ((80, dofs), BF16), ((n, 80), F32)] + more,
    )
    faces = exchange(faces)
    flexed, local, coarse, sent_rows, *faces = call(
        "local2", second_local, faces + [image, sums, exact_z, vectors, corner, coarse, stiff],
        [field, field, ((2 * coarse.shape[0], spans[3]), F32), sent] + wins,
    )
    received = send_all(sent_rows)
    faces = exchange(faces)
    znew, step, image, sums, before, *faces = call(
        "image2", second_image,
        [received] + faces + [local, flexed, exact_z, resid, vectors, corner_map, spread, flex],
        [field, field, field, total, total] + wins,
    )
    faces = exchange(faces)
    distance, coarse = 2, [coarse]
    while distance < groups:
        coarse.append(swap(jnp.concatenate(coarse, axis=0), "grp", distance))
        distance *= 2
    local, sent_rows, *faces = call(
        "local3", third_local, faces + [image, sums, vectors, corner, stiff], [field, sent] + wins
    )
    received = send_all(sent_rows)
    faces = exchange(faces)
    mult, direction = call(
        "finish", finish,
        [received] + faces + [local, before, zold, znew, step, vectors, corner_map, spread] + coarse, [field, field],
    )
    return (mult[None, None], direction[None, None])


def solution(mesh):
    in_specs = (
        P("grp", "sub", None, None),
        P("grp", "sub", None, None),
        P("grp", "sub", None, None),
        P("grp", None, None),
        P("grp", "sub", None),
        P("grp", "sub", None),
    )
    out_specs = (P("grp", "sub", None, None), P("grp", "sub", None, None))
    return jax.shard_map(body, mesh=mesh, in_specs=in_specs, out_specs=out_specs, check_vma=False)
```

```python
import functools

import jax
import jax.numpy as jnp
from jax import lax
from jax.experimental import pallas as pl
from jax.experimental.pallas import tpu as pltpu
from jax.sharding import PartitionSpec as P

F32, BF16 = jnp.float32, jnp.bfloat16
NT = (((1,), (1,)), ((), ()))
NN = (((1,), (0,)), ((), ()))
LANES = 128


def exact(a, b, dims=NN):
    return lax.dot_general(a, b, dims, precision=lax.Precision.HIGHEST, preferred_element_type=F32)


def rounded(a, b):
    return lax.dot_general(a, b, NN, preferred_element_type=F32)


def thirds(x):
    high = x.astype(BF16)
    rest = x - high.astype(F32)
    mid = rest.astype(BF16)
    return jnp.concatenate([high, mid, (rest - mid.astype(F32)).astype(BF16)], axis=0)


def by_map(x, corner_map, dims):
    n = x.shape[0]
    out = lax.dot_general(thirds(x), corner_map, dims, preferred_element_type=F32)
    return out[:n] + out[n : 2 * n] + out[2 * n :]


def iota(shape, axis):
    return lax.broadcasted_iota(jnp.int32, shape, axis)


FACES = (2, 1, 3, 0)
LAST = FACES.index(3)


def windows(dofs):
    width = dofs // 4
    return [(f * width // LANES * LANES, -(-(f + 1) * width // LANES) * LANES) for f in FACES]


def face_vectors(nodes_ref, dofs):
    width = dofs // 4
    pos = iota((1, dofs), 1)
    sub_pos, grp_pos = lax.axis_index("sub"), lax.axis_index("grp")
    bits = [sub_pos & 1, (sub_pos >> 1) & 1, (sub_pos >> 2) & 1, grp_pos & 1]
    sign = jnp.zeros((1, dofs), F32)
    live = jnp.zeros((1, dofs), jnp.int32)
    node = pos
    for f in range(4):
        inside = (pos >= f * width) & (pos < (f + 1) * width)
        sign = jnp.where(inside, (1 - 2 * bits[f]).astype(F32), sign)
        live = jnp.where(inside, nodes_ref[f], live)
    for step in range(1, 12):
        node = jnp.where(pos >= step * (width // 3), pos - step * (width // 3), node)
    mask = jnp.where(node < live, 1.0, 0.0)
    return sign, mask


def corner_ids(ids_ref, shape, axis):
    place = iota(shape, axis)
    ids = jnp.full(shape, -1, jnp.int32)
    for k in range(ids_ref.shape[0]):
        ids = jnp.where(place == 4 * (k % 4) + k // 4, ids_ref[k], ids)
    return ids


def corner_rows(ids, dofs):
    return jnp.where(ids == iota((16, dofs), 1), 1.0, 0.0)


def across(wins, dofs):
    by_face = sorted(zip(FACES, windows(dofs), wins), key=lambda item: item[0])
    width = dofs // 4
    n = wins[0].shape[0]
    tiles = []
    for low in range(0, dofs, LANES):
        tile = None
        for f, (start, stop), win in by_face:
            if start <= low < stop:
                part = win[:, low - start : low - start + LANES]
                tile = part if tile is None else jnp.where(iota((n, LANES), 1) + low < f * width, tile, part)
        tiles.append(tile)
    return jnp.concatenate(tiles, axis=1)


def jump(own, came, rows, sign_mask):
    return across([a[:rows, :] - b[:rows, :] for a, b in zip(own, came)], sign_mask.shape[1]) * sign_mask


def put_windows(refs, field):
    for ref, (start, stop) in zip(refs, windows(field.shape[1])):
        ref[: field.shape[0], :] = field[:, start:stop]


def same_block(n_row, n_col, row_block, col_block):
    return iota((n_row, n_col), 0) // row_block == iota((n_row, n_col), 1) // col_block


def to_column(row):
    n = row.shape[1]
    return jnp.sum(jnp.where(same_block(n, n, 1, 1), row, 0.0), axis=1, keepdims=True)


def to_row(column):
    n = column.shape[0]
    return jnp.sum(jnp.where(same_block(n, n, 1, 1), column, 0.0), axis=0, keepdims=True)


def total_of(received):
    total = received[0:8]
    for low in range(8, received.shape[0], 8):
        total = total + received[low : low + 8]
    return total + pltpu.roll(total, 4, 0)


def sums_of(total, n_load):
    column = to_column(total[3:4])
    return [column[i * n_load : (i + 1) * n_load] for i in range(4)]


def halves(x):
    high = x.astype(BF16)
    return jnp.concatenate([high, (x - high.astype(F32)).astype(BF16)], axis=0)


def fine(x, matrix):
    n = x.shape[0]
    both = rounded(halves(x), matrix)
    return both[:n] + both[n:]


def finer(x, matrix):
    n = x.shape[0]
    high = matrix.astype(BF16)
    low = (matrix - high.astype(F32)).astype(BF16)
    parts = halves(x)
    both = lax.dot_general(parts, high, NT, preferred_element_type=F32)
    return both[:n] + both[n:] + lax.dot_general(parts[:n], low, NT, preferred_element_type=F32)


def packed_corners(scaled, corner):
    n_load = scaled.shape[0]
    values = by_map(scaled, corner, NT)
    flipped = jnp.concatenate([values] * 4, axis=0).T
    flipped = jnp.where(same_block(16, 4 * n_load, 4, n_load), flipped, 0.0)
    block = flipped[:8] + flipped[8:]
    return block + pltpu.roll(block, 4, 0)


def with_sums(block, sums):
    zero = jnp.zeros_like(sums[0])
    row = to_row(jnp.concatenate(sums + [zero] * (4 - len(sums)), axis=0))
    return jnp.where(iota(block.shape, 0) % 4 == 3, row, block)


def put_all(out, block):
    for low in range(0, out.shape[0], 8):
        out[low : low + 8, :] = block


def group_corners(received, which, rows, n_load):
    block = received[pl.ds(pl.multiple_of(which * rows, 8), rows), :]
    block = jnp.where(iota(block.shape, 0) % 4 == 3, 0.0, block)
    tall = jnp.concatenate([block] * 4, axis=0)
    flipped = jnp.where(same_block(4 * rows, 4 * n_load, rows, n_load), tall, 0.0).T
    return sum(flipped[r * n_load : (r + 1) * n_load] for r in range(1, 4)) + flipped[:n_load]


def coarse_of(received, spread, n_load):
    rows = spread.shape[1] // 4
    grp_pos = lax.axis_index("grp")
    inner = finer(group_corners(received, grp_pos, rows, n_load), spread)
    outer = finer(group_corners(received, grp_pos ^ 1, rows, n_load), spread)
    return jnp.where(iota(inner.shape, 1) < 64, inner, outer)


def to_wide(matrix, wide):
    n_row, n = matrix.shape
    if n < wide:
        return jnp.concatenate([matrix[: n_row // 2], matrix[n_row // 2 :]], axis=1)
    return jnp.concatenate([matrix[:, low : low + wide] for low in range(0, n, wide)], axis=0)


def from_wide(rows, n):
    wide = rows.shape[1]
    if n < wide:
        return jnp.concatenate([rows[:, :n], rows[:, n:]], axis=0)
    n_row = rows.shape[0] * wide // n
    return jnp.concatenate([rows[low : low + n_row] for low in range(0, rows.shape[0], n_row)], axis=1)


def rows_sum(x):
    return jnp.sum(x, axis=1, keepdims=True)


def start(
    rhs_hbm, stiff_hbm, inverse_hbm, nodes_hbm, ids_hbm,
    sent, vectors, corner_out, resid_out, spread_out, coarse_out, low_out, w0, w1, w2, w3,
    rhs, stiff, inverse, nodes, ids, sems,
):
    pairs = [(nodes_hbm, nodes), (ids_hbm, ids), (rhs_hbm, rhs), (inverse_hbm, inverse), (stiff_hbm, stiff)]
    copies = [pltpu.make_async_copy(a, b, sems.at[i]) for i, (a, b) in enumerate(pairs)]
    for copy in copies:
        copy.start()
    n_load, dofs = rhs.shape
    wins = [w0, w1, w2, w3]
    copies[0].wait()
    sign, mask = face_vectors(nodes, dofs)
    vectors[0:1, :] = sign
    vectors[1:2, :] = mask
    vectors[2:3, :] = sign * mask
    vectors[3:8, :] = jnp.zeros((5, dofs), F32)
    copies[1].wait()
    corner = corner_rows(corner_ids(ids, (16, 1), 0), dofs).astype(BF16)
    corner_out[...] = corner
    for ref in wins:
        ref[n_load : n_load + 8, :] = corner_ids(ids, (8, ref.shape[1]), 1).astype(F32)
    copies[2].wait()
    resid = rhs[...] * mask
    resid_out[...] = resid
    scaled = 0.5 * sign * resid
    put_all(sent, packed_corners(scaled, corner))
    copies[3].wait()
    n = inverse.shape[0]
    corners = ids.shape[0]
    subs = n // corners
    sub_pos = lax.axis_index("sub")
    row = iota((64, 1), 0)
    owner = jnp.where(row < 16, sub_pos, jnp.where(row < 32, sub_pos ^ 1, jnp.where(row < 48, sub_pos ^ 2, sub_pos ^ 4)))
    source = owner * corners + row % 4 * 4 + row // 4 % 4
    pick = jnp.where((source == iota((64, n), 1)) & (row % 4 * 4 < corners), 1.0, 0.0)
    place = iota((16 * subs, 1), 0)
    source = place // 4 % subs * corners + place % 4 * 4 + place // (4 * subs)
    order = jnp.where((source == iota((16 * subs, n), 1)) & (place % 4 * 4 < corners), 1.0, 0.0)
    both = exact(exact(jnp.concatenate([pick, order], axis=0), inverse[...]), order, NT)
    spread_out[...] = both[:64]
    last = wins[LAST]
    coarse_out[...] = to_wide(both[64:], last.shape[1])
    last[n_load + 8 :, :] = to_wide(both[:16], last.shape[1])
    copies[4].wait()
    local = rounded(halves(scaled), stiff[...])
    put_windows(wins, local[:n_load])
    low_out[...] = local[n_load:]


def first_image(
    received, o0, o1, o2, o3, a0, a1, a2, a3, vectors, corner, resid, spread, low, flex,
    z_out, sums_out, map_out, spread_out, *wins,
):
    n_load, dofs = resid.shape
    came = [a0, a1, a2, a3]
    sign, sign_mask = vectors[0:1, :], vectors[2:3, :]
    width = dofs // 4
    pos = iota((1, dofs), 1)
    pieces = [corner[...].astype(F32) * sign_mask]
    for f in range(4):
        ids = to_column(came[FACES.index(f)][n_load : n_load + 1, :LANES])[:16].astype(jnp.int32)
        inside = (pos >= f * width) & (pos < (f + 1) * width)
        pieces.append(corner_rows(ids, dofs) * jnp.where(inside, -sign_mask, 0.0))
    corner_map = jnp.concatenate(pieces, axis=0).astype(BF16)
    map_out[...] = corner_map
    n = spread.shape[1]
    cross = from_wide(came[LAST][n_load + 8 :, :], n)
    spread_rows = jnp.concatenate([spread[...], cross], axis=0)
    spread_out[...] = spread_rows
    coarse = coarse_of(received, spread_rows, n_load)
    zvec = jump([o0, o1, o2, o3], came, n_load, sign_mask) + by_map(coarse, corner_map, NN)
    z_out[...] = zvec
    signed = sign * zvec
    image = rounded(signed.astype(BF16), flex[...])
    put_windows(wins, jnp.concatenate([image, low[...]], axis=0))
    sums_out[...] = with_sums(
        jnp.zeros((8, 4 * n_load), F32), [rows_sum(resid[...] * zvec), 2.0 * rows_sum(signed * image)]
    )


def second_local(
    o0, o1, o2, o3, a0, a1, a2, a3, sums, vectors, corner_map, stiff, flexed_out, low_out, sent, *wins
):
    n_load, dofs = flexed_out.shape
    sign, sign_mask = vectors[0:1, :], vectors[2:3, :]
    jumped = jump([o0, o1, o2, o3], [a0, a1, a2, a3], 2 * n_load, sign_mask)
    flexed = jumped[:n_load]
    flexed_out[...] = flexed
    low_out[...] = jumped[n_load:].astype(BF16)
    scaled = 0.5 * sign * flexed
    is_sum = iota((8, 1), 0) % 4 == 3
    corners = packed_corners(scaled, abs(corner_map[:16, :]))
    put_all(sent, jnp.where(is_sum, sums[...], corners))
    put_windows(wins, fine(scaled, stiff[...]))


def second_image(
    received, o0, o1, o2, o3, a0, a1, a2, a3, flexed, zold, low, resid, inverse, vectors, corner_map, spread, flex,
    z_out, step_out, sums_out, total_out, inverse_out, *wins,
):
    n_load, dofs = resid.shape
    sign, sign_mask = vectors[0:1, :], vectors[2:3, :]
    inverse_out[...] = inverse[...]
    total = total_of(received)
    total_out[...] = total
    rz, curve, _, _ = sums_of(total, n_load)
    alpha = rz / curve
    coarse = coarse_of(received, spread[...], n_load)
    step = jump([o0, o1, o2, o3], [a0, a1, a2, a3], n_load, sign_mask) + by_map(coarse, corner_map[...], NN)
    step = alpha * step
    step_out[...] = step
    zvec = zold[...] + low[...].astype(F32) - step
    z_out[...] = zvec
    signed = sign * zvec
    image = alpha * fine(signed, flex[...])
    put_windows(wins, image)
    scaled_flexed = alpha * flexed[...]
    sums = [
        rows_sum((resid[...] - scaled_flexed) * zvec),
        2.0 * rows_sum(signed * image),
        rows_sum(zvec * scaled_flexed),
    ]
    sums_out[...] = with_sums(jnp.zeros((8, 4 * n_load), F32), sums)


def third_local(o0, o1, o2, o3, a0, a1, a2, a3, sums, vectors, corner_map, stiff, *rest):
    inverses, (sent, *wins) = rest[:-5], rest[-5:]
    n_load, dofs = o0.shape[0], vectors.shape[1]
    sign, sign_mask = vectors[0:1, :], vectors[2:3, :]
    flexed = jump([o0, o1, o2, o3], [a0, a1, a2, a3], n_load, sign_mask)
    scaled = 0.5 * sign * flexed
    local = fine(scaled, stiff[...])
    put_windows(wins, local)
    low = n_load
    for ref in inverses:
        wins[LAST][low : low + ref.shape[0], :] = ref[...]
        low += ref.shape[0]
    fourth = jnp.where(iota((1, 4 * n_load), 1) // n_load == 3, 1.0, 0.0)
    square = with_sums(jnp.zeros((8, 4 * n_load), F32), [4.0 * rows_sum(scaled * local)] * 4) * fourth
    is_sum = iota((8, 1), 0) % 4 == 3
    put_all(sent, jnp.where(is_sum, sums[...] + square, packed_corners(scaled, abs(corner_map[:16, :]))))


def finish(
    received, o0, o1, o2, o3, a0, a1, a2, a3, before, zold, znew, step, vectors, corner_map, spread, *rest
):
    inverses, (mult_out, direction_out) = rest[:-2], rest[-2:]
    n_load, dofs = zold.shape
    sign_mask = vectors[2:3, :]
    rz0, curve0, _, _ = sums_of(before[...], n_load)
    rz1, curve, mixed, square = sums_of(total_of(received), n_load)
    n = spread.shape[1]
    height = n * n // a0.shape[1]
    held = jnp.concatenate([ref[...] for ref in inverses], axis=0)
    for side, rows in enumerate([held, [a0, a1, a2, a3][LAST][n_load:, :]]):
        for i in range(rows.shape[0] // height):
            values = group_corners(received, lax.axis_index("grp") ^ (2 * i + side), n // 4, n_load)
            matrix = from_wide(rows[i * height : (i + 1) * height], n)
            square = square + 4.0 * rows_sum(values * finer(values, matrix))
    alpha = rz0 / curve0
    beta = rz1 / rz0
    gamma = rz1 / (curve + 2.0 * beta * mixed + beta * beta * rz0)
    rz2 = square + 2.0 * beta * (mixed - curve) + beta * beta * (rz0 - mixed)
    rz2 = rz1 - 2.0 * gamma * (curve + beta * mixed) + gamma * gamma * rz2
    coarse = coarse_of(received, spread[...], n_load)
    image = jump([o0, o1, o2, o3], [a0, a1, a2, a3], n_load, sign_mask) + by_map(coarse, corner_map[...], NN)
    direction = znew[...] + beta * zold[...]
    mult_out[...] = alpha * (zold[...] + gamma * direction)
    direction_out[...] = znew[...] - gamma * (image + beta * step[...]) + (rz2 / rz1) * direction


def call(name, kernel, args, outs, scratch=(), space=pltpu.VMEM):
    shapes = [jax.ShapeDtypeStruct(s, d) for s, d in outs]
    n_bytes = sum(a.size * a.dtype.itemsize for a in args) + sum(s.size * s.dtype.itemsize for s in shapes)
    return pl.pallas_call(
        kernel,
        out_shape=shapes,
        in_specs=[pl.BlockSpec(memory_space=space)] * len(args),
        out_specs=[pl.BlockSpec(memory_space=pltpu.VMEM)] * len(shapes),
        scratch_shapes=scratch,
        cost_estimate=pl.CostEstimate(flops=40_000_000, bytes_accessed=n_bytes, transcendentals=0),
        compiler_params=pltpu.CompilerParams(vmem_limit_bytes=(12 << 20) + 2 * n_bytes if space == pltpu.VMEM else 54600 << 10),
        name=name,
    )(*args)


def swap(block, axis, distance):
    count = lax.axis_size(axis)
    return lax.ppermute(block, axis, [(i, i ^ distance) for i in range(count) if i ^ distance < count])


def exchange(wins):
    return [swap(win, "grp", 1) if f == 3 else swap(win, "sub", 1 << f) for f, win in zip(FACES, wins)]


def send_all(rows):
    devices = lax.axis_size("grp") * lax.axis_size("sub")
    blocks = rows.reshape(devices, 4, rows.shape[1])
    return lax.all_to_all(blocks, ("grp", "sub"), 0, 0, tiled=True).reshape(rows.shape)


def body(loads, stiffness, flexibility, coarse_inverse, face_nodes, corner_index):
    rhs, stiff, flex, inverse = loads[0, 0], stiffness[0, 0], flexibility[0, 0], coarse_inverse[0]
    nodes, ids = face_nodes[0, 0], corner_index[0, 0]
    n_load, dofs = rhs.shape
    groups, subs = lax.axis_size("grp"), lax.axis_size("sub")
    n = 16 * subs
    field = ((n_load, dofs), F32)
    sent = ((groups * subs * 4, 4 * n_load), F32)
    total = ((8, 4 * n_load), F32)
    spans = [high - low for low, high in windows(dofs)]
    coarse = ((n * n // spans[LAST], spans[LAST]), F32)

    def wins(rows, more=0):
        return [((rows + more * (i == LAST), w), F32) for i, w in enumerate(spans)]

    corners, vectors, corner, resid, spread, inverse, low, *own = call(
        "start", start, [rhs, stiff, inverse, nodes, ids],
        [sent, ((8, dofs), F32), ((16, dofs), BF16), field, ((64, n), F32), coarse, field]
        + wins(n_load + 8, 16 * n // spans[LAST]),
        [pltpu.VMEM(rhs.shape, F32), pltpu.VMEM(stiff.shape, BF16), pltpu.VMEM(inverse.shape, F32),
         pltpu.SMEM(nodes.shape, jnp.int32), pltpu.SMEM(ids.shape, jnp.int32), pltpu.SemaphoreType.DMA((5,))],
        pl.ANY,
    )
    received = send_all(corners)
    came = exchange(own)
    zold, sums, corner_map, spread, *own = call(
        "image1", first_image, [received] + own + came + [vectors, corner, resid, spread, low, flex],
        [field, total, ((80, dofs), BF16), ((80, n), F32)] + wins(2 * n_load),
    )
    came = exchange(own)
    flexed, low, sent_rows, *own = call(
        "local2", second_local, own + came + [sums, vectors, corner_map, stiff],
        [field, ((n_load, dofs), BF16), sent] + wins(n_load),
    )
    received = send_all(sent_rows)
    came = exchange(own)
    znew, step, sums, before, inverse, *own = call(
        "image2", second_image,
        [received] + own + came + [flexed, zold, low, resid, inverse, vectors, corner_map, spread, flex],
        [field, field, total, total, coarse] + wins(n_load),
    )
    came = exchange(own)
    distance, inverses = 2, [inverse]
    while distance < groups:
        inverses.append(swap(jnp.concatenate(inverses, axis=0), "grp", distance))
        distance *= 2
    sent_rows, *own = call(
        "local3", third_local, own + came + [sums, vectors, corner_map, stiff] + inverses,
        [sent] + wins(n_load, sum(a.shape[0] for a in inverses)),
    )
    received = send_all(sent_rows)
    came = exchange(own)
    mult, direction = call(
        "finish", finish,
        [received] + own + came + [before, zold, znew, step, vectors, corner_map, spread] + inverses, [field, field],
    )
    return (mult[None, None], direction[None, None])


def solution(mesh):
    in_specs = (
        P("grp", "sub", None, None),
        P("grp", "sub", None, None),
        P("grp", "sub", None, None),
        P("grp", None, None),
        P("grp", "sub", None),
        P("grp", "sub", None),
    )
    out_specs = (P("grp", "sub", None, None), P("grp", "sub", None, None))
    return jax.shard_map(body, mesh=mesh, in_specs=in_specs, out_specs=out_specs, check_vma=False)
```

```python
import functools

import jax
import jax.numpy as jnp
from jax import lax
from jax.experimental import pallas as pl
from jax.experimental.pallas import tpu as pltpu
from jax.sharding import PartitionSpec as P

F32, BF16 = jnp.float32, jnp.bfloat16
NT = (((1,), (1,)), ((), ()))
NN = (((1,), (0,)), ((), ()))
LANES = 128
START_LIMIT = 54600


def exact(a, b, dims=NN):
    return lax.dot_general(a, b, dims, precision=lax.Precision.HIGHEST, preferred_element_type=F32)


def rounded(a, b):
    return lax.dot_general(a, b, NN, preferred_element_type=F32)


def thirds(x):
    high = x.astype(BF16)
    rest = x - high.astype(F32)
    mid = rest.astype(BF16)
    return jnp.concatenate([high, mid, (rest - mid.astype(F32)).astype(BF16)], axis=0)


def by_map(x, corner_map, dims):
    n = x.shape[0]
    out = lax.dot_general(thirds(x), corner_map, dims, preferred_element_type=F32)
    return out[:n] + out[n : 2 * n] + out[2 * n :]


def iota(shape, axis):
    return lax.broadcasted_iota(jnp.int32, shape, axis)


FACES = (2, 1, 3, 0)
LAST = FACES.index(3)


def pick_lane(row, lane):
    return jnp.sum(jnp.where(iota(row.shape, 1) == lane, row, 0.0), axis=1, keepdims=True)


def face_vectors(info, dofs):
    width = dofs // 4
    pos = iota((1, dofs), 1)
    sub_pos, grp_pos = lax.axis_index("sub"), lax.axis_index("grp")
    bits = [sub_pos & 1, (sub_pos >> 1) & 1, (sub_pos >> 2) & 1, grp_pos & 1]
    sign = jnp.zeros((1, dofs), F32)
    live = jnp.zeros((1, dofs), jnp.int32)
    node = pos
    for f in range(4):
        inside = (pos >= f * width) & (pos < (f + 1) * width)
        sign = jnp.where(inside, (1 - 2 * bits[f]).astype(F32), sign)
        live = jnp.where(inside, pick_lane(info, f).astype(jnp.int32), live)
    for step in range(1, 12):
        node = jnp.where(pos >= step * (width // 3), pos - step * (width // 3), node)
    mask = jnp.where(node < live, 1.0, 0.0)
    return sign, mask


def corner_ids(info, corners):
    row = iota((16, 1), 0)
    ids = jnp.sum(jnp.where(iota((16, info.shape[1]), 1) == 4 + row % 4 * 4 + row // 4, info, 0.0), axis=1, keepdims=True)
    return jnp.where(row % 4 * 4 < corners, ids, -1.0)


def corner_rows(ids, dofs):
    return jnp.where(ids == iota((16, dofs), 1), 1.0, 0.0)


def size(n_row):
    return n_row + n_row // 2


def put_faces(refs, field):
    n, dofs = field.shape
    width = dofs // 4
    for f, ref in zip(FACES, refs):
        low = f * width
        start = low if low % LANES == 0 else low + LANES // 2
        half = field[:, low + LANES : low + 2 * LANES] if low % LANES == 0 else field[:, start - LANES : start]
        top, bottom = half[: n // 2], half[n // 2 :]
        if low % LANES == 0:
            bottom = pltpu.roll(bottom, LANES // 2, 1)
        else:
            top = pltpu.roll(top, LANES // 2, 1)
        ref[:n, :] = field[:, start : start + LANES]
        ref[n : size(n), :] = jnp.where(iota(top.shape, 1) < LANES // 2, top, bottom)


def from_faces(faces, n):
    by_face = [face for _, face in sorted(zip(FACES, faces), key=lambda item: item[0])]
    tiles = []
    for even, odd in (by_face[:2], by_face[2:]):
        first, second = even[n:], odd[n:]
        left = iota(first.shape, 1) < LANES // 2
        top = jnp.where(left, first, pltpu.roll(second, LANES // 2, 1))
        bottom = jnp.where(left, pltpu.roll(first, LANES // 2, 1), second)
        tiles += [even[:n], jnp.concatenate([top, bottom], axis=0), odd[:n]]
    return jnp.concatenate(tiles, axis=1)


def jump(own, came, n, sign_mask):
    return from_faces([a[: size(n), :] - b[: size(n), :] for a, b in zip(own, came)], n) * sign_mask


def same_block(n_row, n_col, row_block, col_block):
    return iota((n_row, n_col), 0) // row_block == iota((n_row, n_col), 1) // col_block


def to_column(row):
    n = row.shape[1]
    return jnp.sum(jnp.where(same_block(n, n, 1, 1), row, 0.0), axis=1, keepdims=True)


def to_row(column):
    n = column.shape[0]
    return jnp.sum(jnp.where(same_block(n, n, 1, 1), column, 0.0), axis=0, keepdims=True)


def total_of(received):
    total = received[0:8]
    for low in range(8, received.shape[0], 8):
        total = total + received[low : low + 8]
    return total + pltpu.roll(total, 4, 0)


def sums_of(total, n_load):
    column = to_column(total[3:4])
    return [column[i * n_load : (i + 1) * n_load] for i in range(4)]


def halves(x):
    high = x.astype(BF16)
    return jnp.concatenate([high, (x - high.astype(F32)).astype(BF16)], axis=0)


def fine(x, matrix):
    n = x.shape[0]
    both = rounded(halves(x), matrix)
    return both[:n] + both[n:]


def finer(x, matrix):
    n = x.shape[0]
    high = matrix.astype(BF16)
    low = (matrix - high.astype(F32)).astype(BF16)
    parts = halves(x)
    both = lax.dot_general(parts, high, NT, preferred_element_type=F32)
    return both[:n] + both[n:] + lax.dot_general(parts[:n], low, NT, preferred_element_type=F32)


def packed_corners(scaled, corner):
    n_load = scaled.shape[0]
    values = by_map(scaled, corner, NT)
    flipped = jnp.concatenate([values] * 4, axis=0).T
    flipped = jnp.where(same_block(16, 4 * n_load, 4, n_load), flipped, 0.0)
    block = flipped[:8] + flipped[8:]
    return block + pltpu.roll(block, 4, 0)


def with_sums(block, sums):
    zero = jnp.zeros_like(sums[0])
    row = to_row(jnp.concatenate(sums + [zero] * (4 - len(sums)), axis=0))
    return jnp.where(iota(block.shape, 0) % 4 == 3, row, block)


def put_all(out, block):
    for low in range(0, out.shape[0], 8):
        out[low : low + 8, :] = block


def group_corners(received, which, rows, n_load):
    block = received[pl.ds(pl.multiple_of(which * rows, 8), rows), :]
    block = jnp.where(iota(block.shape, 0) % 4 == 3, 0.0, block)
    tall = jnp.concatenate([block] * 4, axis=0)
    flipped = jnp.where(same_block(4 * rows, 4 * n_load, rows, n_load), tall, 0.0).T
    return sum(flipped[r * n_load : (r + 1) * n_load] for r in range(1, 4)) + flipped[:n_load]


def coarse_of(received, spread, n_load):
    rows = spread.shape[1] // 4
    grp_pos = lax.axis_index("grp")
    inner = finer(group_corners(received, grp_pos, rows, n_load), spread)
    outer = finer(group_corners(received, grp_pos ^ 1, rows, n_load), spread)
    return jnp.where(iota(inner.shape, 1) < 64, inner, outer)


def to_tiles(matrix):
    return jnp.concatenate([matrix[:, low : low + LANES] for low in range(0, matrix.shape[1], LANES)], axis=0)


def from_tiles(rows, n):
    n_row = rows.shape[0] * LANES // n
    return jnp.concatenate([rows[low : low + n_row] for low in range(0, rows.shape[0], n_row)], axis=1)


def rows_sum(x):
    return jnp.sum(x, axis=1, keepdims=True)


def start(
    corners, rhs_hbm, stiff_hbm, small,
    sent, vectors, corner_out, resid_out, spread_out, coarse_out, low_out, w0, w1, w2, w3,
    rhs, stiff, block, sems,
):
    pairs = [(rhs_hbm, rhs), (stiff_hbm, stiff), (block, sent)]
    copies = [pltpu.make_async_copy(a, b, sems.at[i]) for i, (a, b) in enumerate(pairs)]
    for copy in copies[:2]:
        copy.start()
    n_load, dofs = rhs.shape
    wins = [w0, w1, w2, w3]
    n = small.shape[0] - 8
    info = small[n : n + 1, :LANES]
    sign, mask = face_vectors(info, dofs)
    vectors[0:1, :] = sign
    vectors[1:2, :] = mask
    vectors[2:3, :] = sign * mask
    vectors[3:8, :] = jnp.zeros((5, dofs), F32)
    ids = corner_ids(info, corners)
    corner = corner_rows(ids.astype(jnp.int32), dofs).astype(BF16)
    corner_out[...] = corner
    ids = jnp.sum(jnp.where(same_block(16, LANES, 1, 1), ids, 0.0), axis=0, keepdims=True)
    for ref in wins:
        ref[size(n_load) : size(n_load) + 8, :] = jnp.broadcast_to(ids, (8, LANES))
    copies[0].wait()
    resid = rhs[...] * mask
    resid_out[...] = resid
    scaled = 0.5 * sign * resid
    put_all(block, packed_corners(scaled, corner))
    copies[2].start()
    wide = small.shape[1]
    subs = n // corners
    sub_pos = lax.axis_index("sub")
    row = iota((64, 1), 0)
    owner = jnp.where(row < 16, sub_pos, jnp.where(row < 32, sub_pos ^ 1, jnp.where(row < 48, sub_pos ^ 2, sub_pos ^ 4)))
    source = owner * corners + row % 4 * 4 + row // 4 % 4
    pick = jnp.where((source == iota((64, n), 1)) & (row % 4 * 4 < corners), 1.0, 0.0)
    place = iota((16 * subs, 1), 0)
    source = place // 4 % subs * corners + place % 4 * 4 + place // (4 * subs)
    order = jnp.where((source == iota((16 * subs, wide), 1)) & (place % 4 * 4 < corners), 1.0, 0.0).astype(BF16)
    pick = jnp.concatenate([pick, order[:, :n].astype(F32)], axis=0).astype(BF16)
    parts = thirds(small[:n, :])
    picked = rounded(pick, parts[:n]) + rounded(pick, parts[n : 2 * n]) + rounded(pick, parts[2 * n :])
    both = by_map(picked, order, NT)
    spread_out[...] = both[:64]
    coarse_out[...] = to_tiles(both[64:])
    wins[LAST][size(n_load) + 8 :, :] = to_tiles(both[:16])
    copies[1].wait()
    local = rounded(halves(scaled), stiff[...])
    put_faces(wins, local[:n_load])
    low_out[...] = local[n_load:]
    copies[2].wait()


def first_image(
    received, o0, o1, o2, o3, a0, a1, a2, a3, vectors, corner, resid, spread, low, inverse, flex,
    z_out, sums_out, map_out, spread_out, *wins,
):
    n_load, dofs = resid.shape
    came = [a0, a1, a2, a3]
    sign, sign_mask = vectors[0:1, :], vectors[2:3, :]
    width = dofs // 4
    pos = iota((1, dofs), 1)
    pieces = [corner[...].astype(F32) * sign_mask]
    for f in range(4):
        ids = to_column(came[FACES.index(f)][size(n_load) : size(n_load) + 1, :])[:16].astype(jnp.int32)
        inside = (pos >= f * width) & (pos < (f + 1) * width)
        pieces.append(corner_rows(ids, dofs) * jnp.where(inside, -sign_mask, 0.0))
    corner_map = jnp.concatenate(pieces, axis=0).astype(BF16)
    map_out[...] = corner_map
    n = spread.shape[1]
    cross = from_tiles(came[LAST][size(n_load) + 8 :, :], n)
    spread_rows = jnp.concatenate([spread[...], cross], axis=0)
    spread_out[...] = spread_rows
    coarse = coarse_of(received, spread_rows, n_load)
    zvec = jump([o0, o1, o2, o3], came, n_load, sign_mask) + by_map(coarse, corner_map, NN)
    z_out[...] = zvec
    signed = sign * zvec
    image = rounded(signed.astype(BF16), flex[...])
    put_faces(wins, jnp.concatenate([image, low[...]], axis=0))
    wins[LAST][size(2 * n_load) :, :] = inverse[...]
    sums_out[...] = with_sums(
        jnp.zeros((8, 4 * n_load), F32), [rows_sum(resid[...] * zvec), 2.0 * rows_sum(signed * image)]
    )


def second_local(
    o0, o1, o2, o3, a0, a1, a2, a3, sums, vectors, corner_map, stiff,
    flexed_out, low_out, inverse_out, sent, w0, w1, w2, w3, block, sem,
):
    n_load, dofs = flexed_out.shape
    sign, sign_mask = vectors[0:1, :], vectors[2:3, :]
    jumped = jump([o0, o1, o2, o3], [a0, a1, a2, a3], 2 * n_load, sign_mask)
    flexed = jumped[:n_load]
    flexed_out[...] = flexed
    for i, ref in enumerate([[o0, o1, o2, o3][LAST], [a0, a1, a2, a3][LAST]]):
        n_row = inverse_out.shape[0] // 2
        inverse_out[i * n_row : (i + 1) * n_row, :] = ref[size(2 * n_load) :, :]
    low_out[...] = jumped[n_load:].astype(BF16)
    scaled = 0.5 * sign * flexed
    is_sum = iota((8, 1), 0) % 4 == 3
    corners = packed_corners(scaled, abs(corner_map[:16, :]))
    put_all(block, jnp.where(is_sum, sums[...], corners))
    copy = pltpu.make_async_copy(block, sent, sem)
    copy.start()
    put_faces([w0, w1, w2, w3], fine(scaled, stiff[...]))
    copy.wait()


def second_image(
    received, o0, o1, o2, o3, a0, a1, a2, a3, flexed, zold, low, resid, vectors, corner_map, spread, flex,
    z_out, step_out, sums_out, total_out, *wins,
):
    n_load, dofs = resid.shape
    sign, sign_mask = vectors[0:1, :], vectors[2:3, :]
    total = total_of(received)
    total_out[...] = total
    rz, curve, _, _ = sums_of(total, n_load)
    alpha = rz / curve
    coarse = coarse_of(received, spread[...], n_load)
    step = jump([o0, o1, o2, o3], [a0, a1, a2, a3], n_load, sign_mask) + by_map(coarse, corner_map[...], NN)
    step = alpha * step
    step_out[...] = step
    zvec = zold[...] + low[...].astype(F32) - step
    z_out[...] = zvec
    signed = sign * zvec
    image = alpha * fine(signed, flex[...])
    put_faces(wins, image)
    scaled_flexed = alpha * flexed[...]
    sums = [
        rows_sum((resid[...] - scaled_flexed) * zvec),
        2.0 * rows_sum(signed * image),
        rows_sum(zvec * scaled_flexed),
    ]
    sums_out[...] = with_sums(jnp.zeros((8, 4 * n_load), F32), sums)


def third_local(o0, o1, o2, o3, a0, a1, a2, a3, sums, vectors, corner_map, stiff, sent, w0, w1, w2, w3, block, sem):
    n_load, dofs = o0.shape[0] * 2 // 3, vectors.shape[1]
    sign, sign_mask = vectors[0:1, :], vectors[2:3, :]
    flexed = jump([o0, o1, o2, o3], [a0, a1, a2, a3], n_load, sign_mask)
    scaled = 0.5 * sign * flexed
    local = fine(scaled, stiff[...])
    fourth = jnp.where(iota((1, 4 * n_load), 1) // n_load == 3, 1.0, 0.0)
    square = with_sums(jnp.zeros((8, 4 * n_load), F32), [4.0 * rows_sum(scaled * local)] * 4) * fourth
    is_sum = iota((8, 1), 0) % 4 == 3
    put_all(block, jnp.where(is_sum, sums[...] + square, packed_corners(scaled, abs(corner_map[:16, :]))))
    copy = pltpu.make_async_copy(block, sent, sem)
    copy.start()
    put_faces([w0, w1, w2, w3], local)
    copy.wait()


def finish(
    received, o0, o1, o2, o3, a0, a1, a2, a3, before, zold, znew, step, vectors, corner_map, spread, *rest
):
    inverses, (mult_hbm, direction_hbm, mult, direction_out, sems) = rest[:-5], rest[-5:]
    n_load, dofs = zold.shape
    sign_mask = vectors[2:3, :]
    rz0, curve0, _, _ = sums_of(before[...], n_load)
    rz1, curve, mixed, square = sums_of(total_of(received), n_load)
    alpha = rz0 / curve0
    beta = rz1 / rz0
    gamma = rz1 / (curve + 2.0 * beta * mixed + beta * beta * rz0)
    direction = znew[...] + beta * zold[...]
    mult[...] = alpha * (zold[...] + gamma * direction)
    copies = [pltpu.make_async_copy(a, b, sems.at[i]) for i, (a, b) in enumerate([(mult, mult_hbm), (direction_out, direction_hbm)])]
    copies[0].start()
    n = spread.shape[1]
    height = n * n // LANES
    index = 0
    for ref in inverses:
        for low in range(0, ref.shape[0], height):
            values = group_corners(received, lax.axis_index("grp") ^ index, n // 4, n_load)
            square = square + 4.0 * rows_sum(values * finer(values, from_tiles(ref[low : low + height, :], n)))
            index += 1
    rz2 = square + 2.0 * beta * (mixed - curve) + beta * beta * (rz0 - mixed)
    rz2 = rz1 - 2.0 * gamma * (curve + beta * mixed) + gamma * gamma * rz2
    coarse = coarse_of(received, spread[...], n_load)
    image = jump([o0, o1, o2, o3], [a0, a1, a2, a3], n_load, sign_mask) + by_map(coarse, corner_map[...], NN)
    direction_out[...] = znew[...] - gamma * (image + beta * step[...]) + (rz2 / rz1) * direction
    copies[1].start()
    copies[0].wait()
    copies[1].wait()


def call(name, kernel, args, outs, scratch=(), in_place=(), out_place=(), limit=None):
    shapes = [jax.ShapeDtypeStruct(s, d) for s, d in outs]
    n_bytes = sum(a.size * a.dtype.itemsize for a in args) + sum(s.size * s.dtype.itemsize for s in shapes)
    return pl.pallas_call(
        kernel,
        out_shape=shapes,
        in_specs=[pl.BlockSpec(memory_space=pl.ANY if i in in_place else pltpu.VMEM) for i in range(len(args))],
        out_specs=[pl.BlockSpec(memory_space=pl.ANY if i in out_place else pltpu.VMEM) for i in range(len(outs))],
        scratch_shapes=scratch,
        cost_estimate=pl.CostEstimate(flops=40_000_000, bytes_accessed=n_bytes, transcendentals=0),
        compiler_params=pltpu.CompilerParams(vmem_limit_bytes=limit or (12 << 20) + 2 * n_bytes),
        name=name,
    )(*args)


def behind(block, other):
    return pl.pallas_call(
        lambda block_ref, other_ref, out_ref: None,
        out_shape=jax.ShapeDtypeStruct(block.shape, block.dtype),
        in_specs=[pl.BlockSpec(memory_space=pl.ANY)] * 2,
        out_specs=pl.BlockSpec(memory_space=pl.ANY),
        input_output_aliases={0: 0},
        compiler_params=pltpu.CompilerParams(vmem_limit_bytes=1 << 20),
        name="behind",
    )(block, other)


def swap(block, axis, distance):
    count = lax.axis_size(axis)
    return lax.ppermute(block, axis, [(i, i ^ distance) for i in range(count) if i ^ distance < count])


def exchange(wins):
    return [swap(win, "grp", 1) if f == 3 else swap(win, "sub", 1 << f) for f, win in zip(FACES, wins)]


def send_all(rows):
    devices = lax.axis_size("grp") * lax.axis_size("sub")
    blocks = rows.reshape(devices, 4, rows.shape[1])
    return lax.all_to_all(blocks, ("grp", "sub"), 0, 0, tiled=True).reshape(rows.shape)


def body(loads, stiffness, flexibility, coarse_inverse, face_nodes, corner_index):
    rhs, stiff, flex, inverse = loads[0, 0], stiffness[0, 0], flexibility[0, 0], coarse_inverse[0]
    nodes, ids = face_nodes[0, 0], corner_index[0, 0]
    n_load, dofs = rhs.shape
    groups, subs = lax.axis_size("grp"), lax.axis_size("sub")
    n = 16 * subs
    field = ((n_load, dofs), F32)
    sent = ((groups * subs * 4, 4 * n_load), F32)
    total = ((8, 4 * n_load), F32)
    n_tile = n * n // LANES

    def faces(rows, more=0, last=0):
        return [((size(rows) + more + last * (i == LAST), LANES), F32) for i in range(4)]

    order = inverse.shape[0]
    wide = -(-order // LANES) * LANES
    few = ids.shape[0]
    small = jnp.pad(inverse, ((0, 8), (0, wide - order)))
    small = small + jnp.pad(nodes[None], ((order, 7), (0, wide - 4))).astype(F32)
    small = small + jnp.pad(ids[None], ((order, 7), (4, wide - 4 - few))).astype(F32)
    block = [pltpu.VMEM(sent[0], F32), pltpu.SemaphoreType.DMA]
    corners, vectors, corner, resid, spread, inverse, low, *own = call(
        "start", functools.partial(start, ids.shape[0]), [rhs, stiff, small],
        [sent, ((8, dofs), F32), ((16, dofs), BF16), field, ((64, n), F32), ((n_tile, LANES), F32), field]
        + faces(n_load, 8, 16 * n // LANES),
        [pltpu.VMEM(rhs.shape, F32), pltpu.VMEM(stiff.shape, BF16), block[0],
         pltpu.SemaphoreType.DMA((3,))],
        [0, 1], [0], START_LIMIT << 10,
    )
    received = send_all(corners)
    came = exchange(own)
    zold, sums, corner_map, spread, *own = call(
        "image1", first_image, [received] + own + came + [vectors, corner, resid, spread, low, inverse, flex],
        [field, total, ((80, dofs), BF16), ((80, n), F32)] + faces(2 * n_load, 0, n_tile),
    )
    came = exchange(own)
    flexed, low, inverse, sent_rows, *own = call(
        "local2", second_local, own + came + [sums, vectors, corner_map, stiff],
        [field, ((n_load, dofs), BF16), ((2 * n_tile, LANES), F32), sent] + faces(n_load),
        block, out_place=[3],
    )
    received = send_all(sent_rows)
    came = exchange(own)
    znew, step, sums, before, *own = call(
        "image2", second_image, [received] + own + came + [flexed, zold, low, resid, vectors, corner_map, spread, flex],
        [field, field, total, total] + faces(n_load),
    )
    came = exchange(own)
    inverses = [inverse]
    distance = 2
    while distance < groups:
        held = inverses[0] if distance == 2 else jnp.concatenate(inverses, axis=0)
        inverses.append(swap(behind(held, came[-1]), "grp", distance))
        distance *= 2
    sent_rows, *own = call(
        "local3", third_local, own + came + [sums, vectors, corner_map, stiff], [sent] + faces(n_load),
        block, out_place=[0],
    )
    received = send_all(sent_rows)
    came = exchange(own)
    mult, direction = call(
        "finish", finish,
        [received] + own + came + [before, zold, znew, step, vectors, corner_map, spread] + inverses, [field, field],
        [pltpu.VMEM(rhs.shape, F32)] * 2 + [pltpu.SemaphoreType.DMA((2,))], out_place=[0, 1],
    )
    return (mult[None, None], direction[None, None])


def solution(mesh):
    in_specs = (
        P("grp", "sub", None, None),
        P("grp", "sub", None, None),
        P("grp", "sub", None, None),
        P("grp", None, None),
        P("grp", "sub", None),
        P("grp", "sub", None),
    )
    out_specs = (P("grp", "sub", None, None), P("grp", "sub", None, None))
    return jax.shard_map(body, mesh=mesh, in_specs=in_specs, out_specs=out_specs, check_vma=False)
```

```python
import functools

import jax
import jax.numpy as jnp
from jax import lax
from jax.experimental import pallas as pl
from jax.experimental.pallas import tpu as pltpu
from jax.sharding import PartitionSpec as P

F32, BF16 = jnp.float32, jnp.bfloat16
NT = (((1,), (1,)), ((), ()))
NN = (((1,), (0,)), ((), ()))
LANES = 128
EXTRA = 72
START_LIMIT = 54600


def exact(a, b, dims=NN):
    return lax.dot_general(a, b, dims, precision=lax.Precision.HIGHEST, preferred_element_type=F32)


def rounded(a, b):
    return lax.dot_general(a, b, NN, preferred_element_type=F32)


def thirds(x):
    high = x.astype(BF16)
    rest = x - high.astype(F32)
    mid = rest.astype(BF16)
    return jnp.concatenate([high, mid, (rest - mid.astype(F32)).astype(BF16)], axis=0)


def by_map(x, corner_map, dims):
    n = x.shape[0]
    out = lax.dot_general(thirds(x), corner_map, dims, preferred_element_type=F32)
    return out[:n] + out[n : 2 * n] + out[2 * n :]


def iota(shape, axis):
    return lax.broadcasted_iota(jnp.int32, shape, axis)


FACES = (2, 1, 3, 0)
LAST = FACES.index(3)


def pick_lane(row, lane):
    return jnp.sum(jnp.where(iota(row.shape, 1) == lane, row, 0.0), axis=1, keepdims=True)


def face_vectors(info, dofs):
    width = dofs // 4
    pos = iota((1, dofs), 1)
    sub_pos, grp_pos = lax.axis_index("sub"), lax.axis_index("grp")
    bits = [sub_pos & 1, (sub_pos >> 1) & 1, (sub_pos >> 2) & 1, grp_pos & 1]
    sign = jnp.zeros((1, dofs), F32)
    live = jnp.zeros((1, dofs), jnp.int32)
    node = pos
    for f in range(4):
        inside = (pos >= f * width) & (pos < (f + 1) * width)
        sign = jnp.where(inside, (1 - 2 * bits[f]).astype(F32), sign)
        live = jnp.where(inside, pick_lane(info, f).astype(jnp.int32), live)
    for step in range(1, 12):
        node = jnp.where(pos >= step * (width // 3), pos - step * (width // 3), node)
    mask = jnp.where(node < live, 1.0, 0.0)
    return sign, mask


def corner_ids(info, corners):
    row = iota((16, 1), 0)
    ids = jnp.sum(jnp.where(iota((16, info.shape[1]), 1) == 4 + row % 4 * 4 + row // 4, info, 0.0), axis=1, keepdims=True)
    return jnp.where(row % 4 * 4 < corners, ids, -1.0)


def corner_rows(ids, dofs):
    return jnp.where(ids == iota((16, dofs), 1), 1.0, 0.0)


def size(n_row):
    return n_row + n_row // 2


def put_faces(refs, field):
    n, dofs = field.shape
    width = dofs // 4
    for f, ref in zip(FACES, refs):
        low = f * width
        start = low if low % LANES == 0 else low + LANES // 2
        half = field[:, low + LANES : low + 2 * LANES] if low % LANES == 0 else field[:, start - LANES : start]
        top, bottom = half[: n // 2], half[n // 2 :]
        if low % LANES == 0:
            bottom = pltpu.roll(bottom, LANES // 2, 1)
        else:
            top = pltpu.roll(top, LANES // 2, 1)
        ref[:n, :] = field[:, start : start + LANES]
        ref[n : size(n), :] = jnp.where(iota(top.shape, 1) < LANES // 2, top, bottom)


def from_faces(faces, n):
    by_face = [face for _, face in sorted(zip(FACES, faces), key=lambda item: item[0])]
    tiles = []
    for even, odd in (by_face[:2], by_face[2:]):
        first, second = even[n:], odd[n:]
        left = iota(first.shape, 1) < LANES // 2
        top = jnp.where(left, first, pltpu.roll(second, LANES // 2, 1))
        bottom = jnp.where(left, pltpu.roll(first, LANES // 2, 1), second)
        tiles += [even[:n], jnp.concatenate([top, bottom], axis=0), odd[:n]]
    return jnp.concatenate(tiles, axis=1)


def jump(own, came, n, sign_mask):
    return from_faces([a[: size(n), :] - b[: size(n), :] for a, b in zip(own, came)], n) * sign_mask


def same_block(n_row, n_col, row_block, col_block):
    return iota((n_row, n_col), 0) // row_block == iota((n_row, n_col), 1) // col_block


def to_column(row):
    n = row.shape[1]
    return jnp.sum(jnp.where(same_block(n, n, 1, 1), row, 0.0), axis=1, keepdims=True)


def to_row(column):
    n = column.shape[0]
    return jnp.sum(jnp.where(same_block(n, n, 1, 1), column, 0.0), axis=0, keepdims=True)


def total_of(received):
    total = received[0:8]
    for low in range(8, received.shape[0], 8):
        total = total + received[low : low + 8]
    return total + pltpu.roll(total, 4, 0)


def sums_of(total, n_load):
    column = to_column(total[3:4])
    return [column[i * n_load : (i + 1) * n_load] for i in range(4)]


def halves(x):
    high = x.astype(BF16)
    return jnp.concatenate([high, (x - high.astype(F32)).astype(BF16)], axis=0)


def fine(x, matrix):
    n = x.shape[0]
    both = rounded(halves(x), matrix)
    return both[:n] + both[n:]


def finer(x, matrix):
    n = x.shape[0]
    high = matrix.astype(BF16)
    low = (matrix - high.astype(F32)).astype(BF16)
    parts = halves(x)
    both = lax.dot_general(parts, high, NT, preferred_element_type=F32)
    return both[:n] + both[n:] + lax.dot_general(parts[:n], low, NT, preferred_element_type=F32)


def packed_corners(scaled, corner):
    n_load = scaled.shape[0]
    values = by_map(scaled, corner, NT)
    flipped = jnp.concatenate([values] * 4, axis=0).T
    flipped = jnp.where(same_block(16, 4 * n_load, 4, n_load), flipped, 0.0)
    block = flipped[:8] + flipped[8:]
    return block + pltpu.roll(block, 4, 0)


def with_sums(block, sums):
    zero = jnp.zeros_like(sums[0])
    row = to_row(jnp.concatenate(sums + [zero] * (4 - len(sums)), axis=0))
    return jnp.where(iota(block.shape, 0) % 4 == 3, row, block)


def put_all(out, block):
    for low in range(0, out.shape[0], 8):
        out[low : low + 8, :] = block


def group_corners(received, which, rows, n_load):
    block = received[pl.ds(pl.multiple_of(which * rows, 8), rows), :]
    block = jnp.where(iota(block.shape, 0) % 4 == 3, 0.0, block)
    tall = jnp.concatenate([block] * 4, axis=0)
    flipped = jnp.where(same_block(4 * rows, 4 * n_load, rows, n_load), tall, 0.0).T
    return sum(flipped[r * n_load : (r + 1) * n_load] for r in range(1, 4)) + flipped[:n_load]


def coarse_of(inner, outer, spread):
    n = inner.shape[0]
    both = finer(jnp.concatenate([inner, outer], axis=0), spread)
    return jnp.where(iota((n, both.shape[1]), 1) < 64, both[:n], both[n:])


def two_groups(received, rows, n_load):
    grp_pos = lax.axis_index("grp")
    if received.shape[0] == 2 * rows:
        grp_pos = grp_pos & 1
    return [group_corners(received, which, rows, n_load) for which in (grp_pos, grp_pos ^ 1)]


def to_tiles(matrix):
    return jnp.concatenate([matrix[:, low : low + LANES] for low in range(0, matrix.shape[1], LANES)], axis=0)


def from_tiles(rows, n):
    n_row = rows.shape[0] * LANES // n
    return jnp.concatenate([rows[low : low + n_row] for low in range(0, rows.shape[0], n_row)], axis=1)


def rows_sum(x):
    return jnp.sum(x, axis=1, keepdims=True)


def start(
    corners, rhs_hbm, stiff_hbm, small,
    sent, vectors, corner_out, resid_out, spread_out, coarse_out, low_out, w0, w1, w2, w3,
    rhs, stiff, block, sems,
):
    pairs = [(rhs_hbm, rhs), (stiff_hbm, stiff), (block, sent)]
    copies = [pltpu.make_async_copy(a, b, sems.at[i]) for i, (a, b) in enumerate(pairs)]
    for copy in copies[:2]:
        copy.start()
    n_load, dofs = rhs.shape
    wins = [w0, w1, w2, w3]
    n = small.shape[0] - 8
    info = small[n : n + 1, :LANES]
    sign, mask = face_vectors(info, dofs)
    vectors[0:1, :] = sign
    vectors[1:2, :] = mask
    vectors[2:3, :] = sign * mask
    vectors[3:8, :] = jnp.zeros((5, dofs), F32)
    ids = corner_ids(info, corners)
    corner = corner_rows(ids.astype(jnp.int32), dofs).astype(BF16)
    corner_out[...] = corner
    ids = jnp.sum(jnp.where(same_block(16, LANES, 1, 1), ids, 0.0), axis=0, keepdims=True)
    for ref in wins:
        ref[size(n_load) : size(n_load) + 8, :] = jnp.broadcast_to(ids, (8, LANES))
    copies[0].wait()
    resid = rhs[...] * mask
    resid_out[...] = resid
    scaled = 0.5 * sign * resid
    put_all(block, packed_corners(scaled, corner))
    copies[2].start()
    wide = small.shape[1]
    subs = n // corners
    sub_pos = lax.axis_index("sub")
    row = iota((64, 1), 0)
    owner = jnp.where(row < 16, sub_pos, jnp.where(row < 32, sub_pos ^ 1, jnp.where(row < 48, sub_pos ^ 2, sub_pos ^ 4)))
    source = owner * corners + row % 4 * 4 + row // 4 % 4
    pick = jnp.where((source == iota((64, n), 1)) & (row % 4 * 4 < corners), 1.0, 0.0)
    place = iota((16 * subs, 1), 0)
    source = place // 4 % subs * corners + place % 4 * 4 + place // (4 * subs)
    order = jnp.where((source == iota((16 * subs, wide), 1)) & (place % 4 * 4 < corners), 1.0, 0.0).astype(BF16)
    pick = jnp.concatenate([pick, order[:, :n].astype(F32)], axis=0).astype(BF16)
    parts = thirds(small[:n, :])
    picked = rounded(pick, parts[:n]) + rounded(pick, parts[n : 2 * n]) + rounded(pick, parts[2 * n :])
    both = by_map(picked, order, NT)
    spread_out[...] = both[:64]
    coarse_out[...] = to_tiles(both[64:])
    wins[LAST][size(n_load) + 8 :, :] = to_tiles(both[:16])
    wins[0][size(n_load) + 8 :, :] = jnp.zeros((EXTRA, LANES), F32)
    copies[1].wait()
    local = rounded(halves(scaled), stiff[...])
    put_faces(wins, local[:n_load])
    low_out[...] = local[n_load:]
    copies[2].wait()


def first_image(
    received, o0, o1, o2, o3, a0, a1, a2, a3, vectors, corner, resid, spread, low, inverse, flex,
    z_out, sums_out, map_out, spread_out, *wins,
):
    n_load, dofs = resid.shape
    came = [a0, a1, a2, a3]
    sign, sign_mask = vectors[0:1, :], vectors[2:3, :]
    width = dofs // 4
    pos = iota((1, dofs), 1)
    pieces = [corner[...].astype(F32) * sign_mask]
    for f in range(4):
        ids = to_column(came[FACES.index(f)][size(n_load) : size(n_load) + 1, :])[:16].astype(jnp.int32)
        inside = (pos >= f * width) & (pos < (f + 1) * width)
        pieces.append(corner_rows(ids, dofs) * jnp.where(inside, -sign_mask, 0.0))
    corner_map = jnp.concatenate(pieces, axis=0).astype(BF16)
    map_out[...] = corner_map
    n = spread.shape[1]
    cross = from_tiles(came[LAST][size(n_load) + 8 :, :], n)
    spread_rows = jnp.concatenate([spread[...], cross], axis=0)
    spread_out[...] = spread_rows
    coarse = coarse_of(*two_groups(received, n // 4, n_load), spread_rows)
    zvec = jump([o0, o1, o2, o3], came, n_load, sign_mask) + by_map(coarse, corner_map, NN)
    z_out[...] = zvec
    signed = sign * zvec
    image = rounded(signed.astype(BF16), flex[...])
    put_faces(wins, jnp.concatenate([image, low[...]], axis=0))
    wins[LAST][size(2 * n_load) :, :] = inverse[...]
    sums_out[...] = with_sums(
        jnp.zeros((8, 4 * n_load), F32), [rows_sum(resid[...] * zvec), 2.0 * rows_sum(signed * image)]
    )


def second_local(
    o0, o1, o2, o3, a0, a1, a2, a3, sums, vectors, corner_map, stiff,
    flexed_out, low_out, inverse_out, sent, w0, w1, w2, w3, block, sem,
):
    n_load, dofs = flexed_out.shape
    sign, sign_mask = vectors[0:1, :], vectors[2:3, :]
    jumped = jump([o0, o1, o2, o3], [a0, a1, a2, a3], 2 * n_load, sign_mask)
    flexed = jumped[:n_load]
    flexed_out[...] = flexed
    for i, ref in enumerate([[o0, o1, o2, o3][LAST], [a0, a1, a2, a3][LAST]]):
        n_row = inverse_out.shape[0] // 2
        inverse_out[i * n_row : (i + 1) * n_row, :] = ref[size(2 * n_load) :, :]
    low_out[...] = jumped[n_load:].astype(BF16)
    scaled = 0.5 * sign * flexed
    is_sum = iota((8, 1), 0) % 4 == 3
    corners = packed_corners(scaled, abs(corner_map[:16, :]))
    put_all(block, jnp.where(is_sum, sums[...], corners))
    copy = pltpu.make_async_copy(block, sent, sem)
    copy.start()
    put_faces([w0, w1, w2, w3], fine(scaled, stiff[...]))
    copy.wait()


def second_image(
    received, o0, o1, o2, o3, a0, a1, a2, a3, flexed, zold, low, resid, vectors, corner_map, spread, flex,
    z_out, step_out, sums_out, total_out, *wins,
):
    n_load, dofs = resid.shape
    sign, sign_mask = vectors[0:1, :], vectors[2:3, :]
    total = total_of(received)
    total_out[...] = total
    rz, curve, _, _ = sums_of(total, n_load)
    alpha = rz / curve
    coarse = coarse_of(*two_groups(received, spread.shape[1] // 4, n_load), spread[...])
    step = jump([o0, o1, o2, o3], [a0, a1, a2, a3], n_load, sign_mask) + by_map(coarse, corner_map[...], NN)
    step = alpha * step
    step_out[...] = step
    zvec = zold[...] + low[...].astype(F32) - step
    z_out[...] = zvec
    signed = sign * zvec
    image = alpha * fine(signed, flex[...])
    put_faces(wins, image)
    scaled_flexed = alpha * flexed[...]
    sums = [
        rows_sum((resid[...] - scaled_flexed) * zvec),
        2.0 * rows_sum(signed * image),
        rows_sum(zvec * scaled_flexed),
    ]
    sums_out[...] = with_sums(jnp.zeros((8, 4 * n_load), F32), sums)


def third_local(o0, o1, o2, o3, a0, a1, a2, a3, sums, vectors, corner_map, stiff, sent, w0, w1, w2, w3, block, sem):
    n_load, dofs = o0.shape[0] * 2 // 3, vectors.shape[1]
    sign, sign_mask = vectors[0:1, :], vectors[2:3, :]
    flexed = jump([o0, o1, o2, o3], [a0, a1, a2, a3], n_load, sign_mask)
    scaled = 0.5 * sign * flexed
    local = fine(scaled, stiff[...])
    fourth = jnp.where(iota((1, 4 * n_load), 1) // n_load == 3, 1.0, 0.0)
    square = with_sums(jnp.zeros((8, 4 * n_load), F32), [4.0 * rows_sum(scaled * local)] * 4) * fourth
    is_sum = iota((8, 1), 0) % 4 == 3
    put_all(block, jnp.where(is_sum, sums[...] + square, packed_corners(scaled, abs(corner_map[:16, :]))))
    copy = pltpu.make_async_copy(block, sent, sem)
    copy.start()
    put_faces([w0, w1, w2, w3], local)
    copy.wait()


def finish(
    received, o0, o1, o2, o3, a0, a1, a2, a3, before, zold, znew, step, vectors, corner_map, spread, *rest
):
    inverses, (mult_hbm, direction_hbm, mult, direction_out, sems) = rest[:-5], rest[-5:]
    n_load, dofs = zold.shape
    sign_mask = vectors[2:3, :]
    rz0, curve0, _, _ = sums_of(before[...], n_load)
    rz1, curve, mixed, square = sums_of(total_of(received), n_load)
    alpha = rz0 / curve0
    beta = rz1 / rz0
    gamma = rz1 / (curve + 2.0 * beta * mixed + beta * beta * rz0)
    direction = znew[...] + beta * zold[...]
    mult[...] = alpha * (zold[...] + gamma * direction)
    copies = [pltpu.make_async_copy(a, b, sems.at[i]) for i, (a, b) in enumerate([(mult, mult_hbm), (direction_out, direction_hbm)])]
    copies[0].start()
    n = spread.shape[1]
    height = n * n // LANES
    corners = two_groups(received, n // 4, n_load)
    index = 0
    for ref in inverses:
        for low in range(0, ref.shape[0], height):
            if index == len(corners):
                corners.append(group_corners(received, lax.axis_index("grp") ^ index, n // 4, n_load))
            values = corners[index]
            square = square + 4.0 * rows_sum(values * finer(values, from_tiles(ref[low : low + height, :], n)))
            index += 1
    rz2 = square + 2.0 * beta * (mixed - curve) + beta * beta * (rz0 - mixed)
    rz2 = rz1 - 2.0 * gamma * (curve + beta * mixed) + gamma * gamma * rz2
    coarse = coarse_of(*corners[:2], spread[...])
    image = jump([o0, o1, o2, o3], [a0, a1, a2, a3], n_load, sign_mask) + by_map(coarse, corner_map[...], NN)
    direction_out[...] = znew[...] - gamma * (image + beta * step[...]) + (rz2 / rz1) * direction
    copies[1].start()
    copies[0].wait()
    copies[1].wait()


def call(name, kernel, args, outs, scratch=(), in_place=(), out_place=(), limit=None):
    shapes = [jax.ShapeDtypeStruct(s, d) for s, d in outs]
    n_bytes = sum(a.size * a.dtype.itemsize for a in args) + sum(s.size * s.dtype.itemsize for s in shapes)
    return pl.pallas_call(
        kernel,
        out_shape=shapes,
        in_specs=[pl.BlockSpec(memory_space=pl.ANY if i in in_place else pltpu.VMEM) for i in range(len(args))],
        out_specs=[pl.BlockSpec(memory_space=pl.ANY if i in out_place else pltpu.VMEM) for i in range(len(outs))],
        scratch_shapes=scratch,
        cost_estimate=pl.CostEstimate(flops=40_000_000, bytes_accessed=n_bytes, transcendentals=0),
        compiler_params=pltpu.CompilerParams(vmem_limit_bytes=limit or (12 << 20) + 2 * n_bytes),
        name=name,
    )(*args)


def behind(block, other):
    return pl.pallas_call(
        lambda block_ref, other_ref, out_ref: None,
        out_shape=jax.ShapeDtypeStruct(block.shape, block.dtype),
        in_specs=[pl.BlockSpec(memory_space=pl.ANY)] * 2,
        out_specs=pl.BlockSpec(memory_space=pl.ANY),
        input_output_aliases={0: 0},
        compiler_params=pltpu.CompilerParams(vmem_limit_bytes=1 << 20),
        name="behind",
    )(block, other)


def swap(block, axis, distance):
    count = lax.axis_size(axis)
    return lax.ppermute(block, axis, [(i, i ^ distance) for i in range(count) if i ^ distance < count])


def exchange(wins):
    return [swap(win, "grp", 1) if f == 3 else swap(win, "sub", 1 << f) for f, win in zip(FACES, wins)]


def send_pair(rows):
    subs = lax.axis_size("sub")
    devices = 2 * subs
    blocks = rows.reshape(devices, 4, rows.shape[1])
    teams = [list(range(low, low + devices)) for low in range(0, lax.axis_size("grp") * subs, devices)]
    return lax.all_to_all(blocks, ("grp", "sub"), 0, 0, tiled=True, axis_index_groups=teams).reshape(rows.shape)


def send_all(rows):
    devices = lax.axis_size("grp") * lax.axis_size("sub")
    blocks = rows.reshape(devices, 4, rows.shape[1])
    return lax.all_to_all(blocks, ("grp", "sub"), 0, 0, tiled=True).reshape(rows.shape)


def body(loads, stiffness, flexibility, coarse_inverse, face_nodes, corner_index):
    rhs, stiff, flex, inverse = loads[0, 0], stiffness[0, 0], flexibility[0, 0], coarse_inverse[0]
    nodes, ids = face_nodes[0, 0], corner_index[0, 0]
    n_load, dofs = rhs.shape
    groups, subs = lax.axis_size("grp"), lax.axis_size("sub")
    n = 16 * subs
    field = ((n_load, dofs), F32)
    sent = ((groups * subs * 4, 4 * n_load), F32)
    total = ((8, 4 * n_load), F32)
    n_tile = n * n // LANES

    def faces(rows, more=0, last=0, first=0):
        return [((size(rows) + more + last * (i == LAST) + first * (i == 0), LANES), F32) for i in range(4)]

    order = inverse.shape[0]
    wide = -(-order // LANES) * LANES
    few = ids.shape[0]
    small = jnp.pad(inverse, ((0, 8), (0, wide - order)))
    small = small + jnp.pad(nodes[None], ((order, 7), (0, wide - 4))).astype(F32)
    small = small + jnp.pad(ids[None], ((order, 7), (4, wide - 4 - few))).astype(F32)
    block = [pltpu.VMEM(sent[0], F32), pltpu.SemaphoreType.DMA]
    corners, vectors, corner, resid, spread, inverse, low, *own = call(
        "start", functools.partial(start, ids.shape[0]), [rhs, stiff, small],
        [((2 * subs * 4, 4 * n_load), F32), ((8, dofs), F32), ((16, dofs), BF16), field, ((64, n), F32), ((n_tile, LANES), F32), field]
        + faces(n_load, 8, 16 * n // LANES, EXTRA),
        [pltpu.VMEM(rhs.shape, F32), pltpu.VMEM(stiff.shape, BF16), pltpu.VMEM((2 * subs * 4, 4 * n_load), F32),
         pltpu.SemaphoreType.DMA((3,))],
        [0, 1], [0], START_LIMIT << 10,
    )
    received = send_pair(corners)
    came = exchange(own)
    zold, sums, corner_map, spread, *own = call(
        "image1", first_image, [received] + own + came + [vectors, corner, resid, spread, low, inverse, flex],
        [field, total, ((80, dofs), BF16), ((80, n), F32)] + faces(2 * n_load, 0, n_tile),
    )
    came = exchange(own)
    flexed, low, inverse, sent_rows, *own = call(
        "local2", second_local, own + came + [sums, vectors, corner_map, stiff],
        [field, ((n_load, dofs), BF16), ((2 * n_tile, LANES), F32), sent] + faces(n_load),
        block, out_place=[3],
    )
    received = send_all(sent_rows)
    came = exchange(own)
    znew, step, sums, before, *own = call(
        "image2", second_image, [received] + own + came + [flexed, zold, low, resid, vectors, corner_map, spread, flex],
        [field, field, total, total] + faces(n_load),
    )
    came = exchange(own)
    inverses = [inverse]
    distance = 2
    while distance < groups:
        held = inverses[0] if distance == 2 else jnp.concatenate(inverses, axis=0)
        inverses.append(swap(behind(held, came[-1]), "grp", distance))
        distance *= 2
    sent_rows, *own = call(
        "local3", third_local, own + came + [sums, vectors, corner_map, stiff], [sent] + faces(n_load),
        block, out_place=[0],
    )
    received = send_all(sent_rows)
    came = exchange(own)
    mult, direction = call(
        "finish", finish,
        [received] + own + came + [before, zold, znew, step, vectors, corner_map, spread] + inverses, [field, field],
        [pltpu.VMEM(rhs.shape, F32)] * 2 + [pltpu.SemaphoreType.DMA((2,))], out_place=[0, 1],
    )
    return (mult[None, None], direction[None, None])


def solution(mesh):
    in_specs = (
        P("grp", "sub", None, None),
        P("grp", "sub", None, None),
        P("grp", "sub", None, None),
        P("grp", None, None),
        P("grp", "sub", None),
        P("grp", "sub", None),
    )
    out_specs = (P("grp", "sub", None, None), P("grp", "sub", None, None))
    return jax.shard_map(body, mesh=mesh, in_specs=in_specs, out_specs=out_specs, check_vma=False)
```

```python
import functools

import jax
import jax.numpy as jnp
from jax import lax
from jax.experimental import pallas as pl
from jax.experimental.pallas import tpu as pltpu
from jax.sharding import PartitionSpec as P

F32, BF16 = jnp.float32, jnp.bfloat16
NT = (((1,), (1,)), ((), ()))
NN = (((1,), (0,)), ((), ()))
LANES = 128
EXTRA = 72
START_LIMIT = 54600


def exact(a, b, dims=NN):
    return lax.dot_general(a, b, dims, precision=lax.Precision.HIGHEST, preferred_element_type=F32)


def rounded(a, b):
    return lax.dot_general(a, b, NN, preferred_element_type=F32)


def thirds(x):
    high = x.astype(BF16)
    rest = x - high.astype(F32)
    mid = rest.astype(BF16)
    return jnp.concatenate([high, mid, (rest - mid.astype(F32)).astype(BF16)], axis=0)


def by_map(x, corner_map, dims):
    n = x.shape[0]
    out = lax.dot_general(thirds(x), corner_map, dims, preferred_element_type=F32)
    return out[:n] + out[n : 2 * n] + out[2 * n :]


def iota(shape, axis):
    return lax.broadcasted_iota(jnp.int32, shape, axis)


FACES = (2, 1, 3, 0)
LAST = FACES.index(3)


def pick_lane(row, lane):
    return jnp.sum(jnp.where(iota(row.shape, 1) == lane, row, 0.0), axis=1, keepdims=True)


def face_vectors(info, dofs):
    width = dofs // 4
    pos = iota((1, dofs), 1)
    sub_pos, grp_pos = lax.axis_index("sub"), lax.axis_index("grp")
    bits = [sub_pos & 1, (sub_pos >> 1) & 1, (sub_pos >> 2) & 1, grp_pos & 1]
    sign = jnp.zeros((1, dofs), F32)
    live = jnp.zeros((1, dofs), jnp.int32)
    node = pos
    for f in range(4):
        inside = (pos >= f * width) & (pos < (f + 1) * width)
        sign = jnp.where(inside, (1 - 2 * bits[f]).astype(F32), sign)
        live = jnp.where(inside, pick_lane(info, f).astype(jnp.int32), live)
    for step in range(1, 12):
        node = jnp.where(pos >= step * (width // 3), pos - step * (width // 3), node)
    mask = jnp.where(node < live, 1.0, 0.0)
    return sign, mask


def corner_ids(info, corners):
    row = iota((16, 1), 0)
    ids = jnp.sum(jnp.where(iota((16, info.shape[1]), 1) == 4 + row % 4 * 4 + row // 4, info, 0.0), axis=1, keepdims=True)
    return jnp.where(row % 4 * 4 < corners, ids, -1.0)


def corner_rows(ids, dofs):
    return jnp.where(ids == iota((16, dofs), 1), 1.0, 0.0)


def size(n_row):
    return n_row + n_row // 2


def put_faces(refs, field):
    n, dofs = field.shape
    width = dofs // 4
    for f, ref in zip(FACES, refs):
        low = f * width
        start = low if low % LANES == 0 else low + LANES // 2
        half = field[:, low + LANES : low + 2 * LANES] if low % LANES == 0 else field[:, start - LANES : start]
        top, bottom = half[: n // 2], half[n // 2 :]
        if low % LANES == 0:
            bottom = pltpu.roll(bottom, LANES // 2, 1)
        else:
            top = pltpu.roll(top, LANES // 2, 1)
        ref[:n, :] = field[:, start : start + LANES]
        ref[n : size(n), :] = jnp.where(iota(top.shape, 1) < LANES // 2, top, bottom)


def from_faces(faces, n):
    by_face = [face for _, face in sorted(zip(FACES, faces), key=lambda item: item[0])]
    tiles = []
    for even, odd in (by_face[:2], by_face[2:]):
        first, second = even[n:], odd[n:]
        left = iota(first.shape, 1) < LANES // 2
        top = jnp.where(left, first, pltpu.roll(second, LANES // 2, 1))
        bottom = jnp.where(left, pltpu.roll(first, LANES // 2, 1), second)
        tiles += [even[:n], jnp.concatenate([top, bottom], axis=0), odd[:n]]
    return jnp.concatenate(tiles, axis=1)


def jump(own, came, n, sign_mask):
    return from_faces([a[: size(n), :] - b[: size(n), :] for a, b in zip(own, came)], n) * sign_mask


def same_block(n_row, n_col, row_block, col_block):
    return iota((n_row, n_col), 0) // row_block == iota((n_row, n_col), 1) // col_block


def to_column(row):
    n = row.shape[1]
    return jnp.sum(jnp.where(same_block(n, n, 1, 1), row, 0.0), axis=1, keepdims=True)


def to_row(column):
    n = column.shape[0]
    return jnp.sum(jnp.where(same_block(n, n, 1, 1), column, 0.0), axis=0, keepdims=True)


def total_of(received):
    total = received[0:8]
    for low in range(8, received.shape[0], 8):
        total = total + received[low : low + 8]
    return total + pltpu.roll(total, 4, 0)


def sums_of(total, n_load):
    column = to_column(total[3:4])
    return [column[i * n_load : (i + 1) * n_load] for i in range(4)]


def halves(x):
    high = x.astype(BF16)
    return jnp.concatenate([high, (x - high.astype(F32)).astype(BF16)], axis=0)


def fine(x, matrix):
    n = x.shape[0]
    both = rounded(halves(x), matrix)
    return both[:n] + both[n:]


def finer(x, matrix):
    n = x.shape[0]
    high = matrix.astype(BF16)
    low = (matrix - high.astype(F32)).astype(BF16)
    parts = halves(x)
    both = lax.dot_general(parts, high, NT, preferred_element_type=F32)
    return both[:n] + both[n:] + lax.dot_general(parts[:n], low, NT, preferred_element_type=F32)


def packed_corners(scaled, corner):
    n_load = scaled.shape[0]
    values = by_map(scaled, corner, NT)
    flipped = jnp.concatenate([values] * 4, axis=0).T
    flipped = jnp.where(same_block(16, 4 * n_load, 4, n_load), flipped, 0.0)
    block = flipped[:8] + flipped[8:]
    return block + pltpu.roll(block, 4, 0)


def with_sums(block, sums):
    zero = jnp.zeros_like(sums[0])
    row = to_row(jnp.concatenate(sums + [zero] * (4 - len(sums)), axis=0))
    return jnp.where(iota(block.shape, 0) % 4 == 3, row, block)


def put_all(out, block):
    for low in range(0, out.shape[0], 8):
        out[low : low + 8, :] = block


def group_corners(received, which, rows, n_load):
    block = received[pl.ds(pl.multiple_of(which * rows, 8), rows), :]
    block = jnp.where(iota(block.shape, 0) % 4 == 3, 0.0, block)
    tall = jnp.concatenate([block] * 4, axis=0)
    flipped = jnp.where(same_block(4 * rows, 4 * n_load, rows, n_load), tall, 0.0).T
    return sum(flipped[r * n_load : (r + 1) * n_load] for r in range(1, 4)) + flipped[:n_load]


def coarse_of(inner, outer, spread):
    n = inner.shape[0]
    both = finer(jnp.concatenate([inner, outer], axis=0), spread)
    return jnp.where(iota((n, both.shape[1]), 1) < 64, both[:n], both[n:])


def two_groups(received, rows, n_load):
    grp_pos = lax.axis_index("grp")
    if received.shape[0] == 2 * rows:
        grp_pos = grp_pos & 1
    return [group_corners(received, which, rows, n_load) for which in (grp_pos, grp_pos ^ 1)]


def to_tiles(matrix):
    return jnp.concatenate([matrix[:, low : low + LANES] for low in range(0, matrix.shape[1], LANES)], axis=0)


def from_tiles(rows, n):
    n_row = rows.shape[0] * LANES // n
    return jnp.concatenate([rows[low : low + n_row] for low in range(0, rows.shape[0], n_row)], axis=1)


def rows_sum(x):
    return jnp.sum(x, axis=1, keepdims=True)


def start(
    corners, rhs_hbm, stiff_hbm, small,
    sent, vectors, corner_out, resid_out, spread_out, coarse_out, low_out, w0, w1, w2, w3,
    rhs, stiff, block, sems,
):
    pairs = [(rhs_hbm, rhs), (stiff_hbm, stiff), (block, sent)]
    copies = [pltpu.make_async_copy(a, b, sems.at[i]) for i, (a, b) in enumerate(pairs)]
    for copy in copies[:2]:
        copy.start()
    n_load, dofs = rhs.shape
    wins = [w0, w1, w2, w3]
    n = small.shape[0] - 8
    info = small[n : n + 1, :LANES]
    sign, mask = face_vectors(info, dofs)
    vectors[0:1, :] = sign
    vectors[1:2, :] = mask
    vectors[2:3, :] = sign * mask
    vectors[3:8, :] = jnp.zeros((5, dofs), F32)
    ids = corner_ids(info, corners)
    corner = corner_rows(ids.astype(jnp.int32), dofs).astype(BF16)
    corner_out[...] = corner
    ids = jnp.sum(jnp.where(same_block(16, LANES, 1, 1), ids, 0.0), axis=0, keepdims=True)
    for ref in wins:
        ref[size(n_load) : size(n_load) + 8, :] = jnp.broadcast_to(ids, (8, LANES))
    copies[0].wait()
    resid = rhs[...] * mask
    resid_out[...] = resid
    scaled = 0.5 * sign * resid
    put_all(block, packed_corners(scaled, corner))
    copies[2].start()
    wide = small.shape[1]
    subs = n // corners
    sub_pos = lax.axis_index("sub")
    row = iota((64, 1), 0)
    owner = jnp.where(row < 16, sub_pos, jnp.where(row < 32, sub_pos ^ 1, jnp.where(row < 48, sub_pos ^ 2, sub_pos ^ 4)))
    source = owner * corners + row % 4 * 4 + row // 4 % 4
    pick = jnp.where((source == iota((64, n), 1)) & (row % 4 * 4 < corners), 1.0, 0.0)
    place = iota((16 * subs, 1), 0)
    source = place // 4 % subs * corners + place % 4 * 4 + place // (4 * subs)
    order = jnp.where((source == iota((16 * subs, wide), 1)) & (place % 4 * 4 < corners), 1.0, 0.0).astype(BF16)
    pick = jnp.concatenate([pick, order[:, :n].astype(F32)], axis=0).astype(BF16)
    parts = thirds(small[:n, :])
    picked = rounded(pick, parts[:n]) + rounded(pick, parts[n : 2 * n]) + rounded(pick, parts[2 * n :])
    both = by_map(picked, order, NT)
    spread_out[...] = both[:64]
    coarse_out[...] = to_tiles(both[64:])
    wins[LAST][size(n_load) + 8 :, :] = to_tiles(both[:16])
    wins[0][size(n_load) + 8 :, :] = jnp.zeros((EXTRA, LANES), F32)
    copies[1].wait()
    local = rounded(halves(scaled), stiff[...])
    put_faces(wins, local[:n_load])
    low_out[...] = local[n_load:]
    copies[2].wait()


def first_image(
    received, o0, o1, o2, o3, a0, a1, a2, a3, vectors, corner, resid, spread, low, flex,
    z_out, sums_out, map_out, spread_out, *wins,
):
    n_load, dofs = resid.shape
    came = [a0, a1, a2, a3]
    sign, sign_mask = vectors[0:1, :], vectors[2:3, :]
    width = dofs // 4
    pos = iota((1, dofs), 1)
    pieces = [corner[...].astype(F32) * sign_mask]
    for f in range(4):
        ids = to_column(came[FACES.index(f)][size(n_load) : size(n_load) + 1, :])[:16].astype(jnp.int32)
        inside = (pos >= f * width) & (pos < (f + 1) * width)
        pieces.append(corner_rows(ids, dofs) * jnp.where(inside, -sign_mask, 0.0))
    corner_map = jnp.concatenate(pieces, axis=0).astype(BF16)
    map_out[...] = corner_map
    n = spread.shape[1]
    cross = from_tiles(came[LAST][size(n_load) + 8 :, :], n)
    spread_rows = jnp.concatenate([spread[...], cross], axis=0)
    spread_out[...] = spread_rows
    coarse = coarse_of(*two_groups(received, n // 4, n_load), spread_rows)
    zvec = jump([o0, o1, o2, o3], came, n_load, sign_mask) + by_map(coarse, corner_map, NN)
    z_out[...] = zvec
    signed = sign * zvec
    image = rounded(signed.astype(BF16), flex[...])
    put_faces(wins, jnp.concatenate([image, low[...]], axis=0))
    sums_out[...] = with_sums(
        jnp.zeros((8, 4 * n_load), F32), [rows_sum(resid[...] * zvec), 2.0 * rows_sum(signed * image)]
    )


def second_local(
    o0, o1, o2, o3, a0, a1, a2, a3, sums, vectors, corner_map, inverse, other, stiff,
    flexed_out, low_out, inverse_out, sent, w0, w1, w2, w3, block, sem,
):
    n_load, dofs = flexed_out.shape
    sign, sign_mask = vectors[0:1, :], vectors[2:3, :]
    jumped = jump([o0, o1, o2, o3], [a0, a1, a2, a3], 2 * n_load, sign_mask)
    flexed = jumped[:n_load]
    flexed_out[...] = flexed
    inverse_out[: inverse.shape[0], :] = inverse[...]
    inverse_out[inverse.shape[0] :, :] = other[...]
    low_out[...] = jumped[n_load:].astype(BF16)
    scaled = 0.5 * sign * flexed
    is_sum = iota((8, 1), 0) % 4 == 3
    corners = packed_corners(scaled, abs(corner_map[:16, :]))
    put_all(block, jnp.where(is_sum, sums[...], corners))
    copy = pltpu.make_async_copy(block, sent, sem)
    copy.start()
    put_faces([w0, w1, w2, w3], fine(scaled, stiff[...]))
    copy.wait()


def second_image(
    received, o0, o1, o2, o3, a0, a1, a2, a3, flexed, zold, low, resid, vectors, corner_map, spread, flex,
    z_out, step_out, sums_out, total_out, *wins,
):
    n_load, dofs = resid.shape
    sign, sign_mask = vectors[0:1, :], vectors[2:3, :]
    total = total_of(received)
    total_out[...] = total
    rz, curve, _, _ = sums_of(total, n_load)
    alpha = rz / curve
    coarse = coarse_of(*two_groups(received, spread.shape[1] // 4, n_load), spread[...])
    step = jump([o0, o1, o2, o3], [a0, a1, a2, a3], n_load, sign_mask) + by_map(coarse, corner_map[...], NN)
    step = alpha * step
    step_out[...] = step
    zvec = zold[...] + low[...].astype(F32) - step
    z_out[...] = zvec
    signed = sign * zvec
    image = alpha * fine(signed, flex[...])
    put_faces(wins, image)
    scaled_flexed = alpha * flexed[...]
    sums = [
        rows_sum((resid[...] - scaled_flexed) * zvec),
        2.0 * rows_sum(signed * image),
        rows_sum(zvec * scaled_flexed),
    ]
    sums_out[...] = with_sums(jnp.zeros((8, 4 * n_load), F32), sums)


def third_local(o0, o1, o2, o3, a0, a1, a2, a3, sums, vectors, corner_map, stiff, sent, w0, w1, w2, w3, block, sem):
    n_load, dofs = o0.shape[0] * 2 // 3, vectors.shape[1]
    sign, sign_mask = vectors[0:1, :], vectors[2:3, :]
    flexed = jump([o0, o1, o2, o3], [a0, a1, a2, a3], n_load, sign_mask)
    scaled = 0.5 * sign * flexed
    local = fine(scaled, stiff[...])
    fourth = jnp.where(iota((1, 4 * n_load), 1) // n_load == 3, 1.0, 0.0)
    square = with_sums(jnp.zeros((8, 4 * n_load), F32), [4.0 * rows_sum(scaled * local)] * 4) * fourth
    is_sum = iota((8, 1), 0) % 4 == 3
    put_all(block, jnp.where(is_sum, sums[...] + square, packed_corners(scaled, abs(corner_map[:16, :]))))
    copy = pltpu.make_async_copy(block, sent, sem)
    copy.start()
    put_faces([w0, w1, w2, w3], local)
    copy.wait()


def finish(
    received, o0, o1, o2, o3, a0, a1, a2, a3, before, zold, znew, step, vectors, corner_map, spread, *rest
):
    inverses, (mult_hbm, direction_hbm, mult, direction_out, sems) = rest[:-5], rest[-5:]
    n_load, dofs = zold.shape
    sign_mask = vectors[2:3, :]
    rz0, curve0, _, _ = sums_of(before[...], n_load)
    rz1, curve, mixed, square = sums_of(total_of(received), n_load)
    alpha = rz0 / curve0
    beta = rz1 / rz0
    gamma = rz1 / (curve + 2.0 * beta * mixed + beta * beta * rz0)
    direction = znew[...] + beta * zold[...]
    mult[...] = alpha * (zold[...] + gamma * direction)
    copies = [pltpu.make_async_copy(a, b, sems.at[i]) for i, (a, b) in enumerate([(mult, mult_hbm), (direction_out, direction_hbm)])]
    copies[0].start()
    n = spread.shape[1]
    height = n * n // LANES
    corners = two_groups(received, n // 4, n_load)
    index = 0
    for ref in inverses:
        for low in range(0, ref.shape[0], height):
            if index == len(corners):
                corners.append(group_corners(received, lax.axis_index("grp") ^ index, n // 4, n_load))
            values = corners[index]
            square = square + 4.0 * rows_sum(values * finer(values, from_tiles(ref[low : low + height, :], n)))
            index += 1
    rz2 = square + 2.0 * beta * (mixed - curve) + beta * beta * (rz0 - mixed)
    rz2 = rz1 - 2.0 * gamma * (curve + beta * mixed) + gamma * gamma * rz2
    coarse = coarse_of(*corners[:2], spread[...])
    image = jump([o0, o1, o2, o3], [a0, a1, a2, a3], n_load, sign_mask) + by_map(coarse, corner_map[...], NN)
    direction_out[...] = znew[...] - gamma * (image + beta * step[...]) + (rz2 / rz1) * direction
    copies[1].start()
    copies[0].wait()
    copies[1].wait()


def call(name, kernel, args, outs, scratch=(), in_place=(), out_place=(), limit=None):
    shapes = [jax.ShapeDtypeStruct(s, d) for s, d in outs]
    n_bytes = sum(a.size * a.dtype.itemsize for a in args) + sum(s.size * s.dtype.itemsize for s in shapes)
    return pl.pallas_call(
        kernel,
        out_shape=shapes,
        in_specs=[pl.BlockSpec(memory_space=pl.ANY if i in in_place else pltpu.VMEM) for i in range(len(args))],
        out_specs=[pl.BlockSpec(memory_space=pl.ANY if i in out_place else pltpu.VMEM) for i in range(len(outs))],
        scratch_shapes=scratch,
        cost_estimate=pl.CostEstimate(flops=40_000_000, bytes_accessed=n_bytes, transcendentals=0),
        compiler_params=pltpu.CompilerParams(vmem_limit_bytes=limit or (12 << 20) + 2 * n_bytes),
        name=name,
    )(*args)


def behind(block, other):
    return pl.pallas_call(
        lambda block_ref, other_ref, out_ref: None,
        out_shape=jax.ShapeDtypeStruct(block.shape, block.dtype),
        in_specs=[pl.BlockSpec(memory_space=pl.ANY)] * 2,
        out_specs=pl.BlockSpec(memory_space=pl.ANY),
        input_output_aliases={0: 0},
        compiler_params=pltpu.CompilerParams(vmem_limit_bytes=1 << 20),
        name="behind",
    )(block, other)


def swap(block, axis, distance):
    count = lax.axis_size(axis)
    return lax.ppermute(block, axis, [(i, i ^ distance) for i in range(count) if i ^ distance < count])


def exchange(wins):
    return [swap(win, "grp", 1) if f == 3 else swap(win, "sub", 1 << f) for f, win in zip(FACES, wins)]


def send_pair(rows):
    subs = lax.axis_size("sub")
    devices = 2 * subs
    blocks = rows.reshape(devices, 4, rows.shape[1])
    teams = [list(range(low, low + devices)) for low in range(0, lax.axis_size("grp") * subs, devices)]
    return lax.all_to_all(blocks, ("grp", "sub"), 0, 0, tiled=True, axis_index_groups=teams).reshape(rows.shape)


def send_all(rows):
    devices = lax.axis_size("grp") * lax.axis_size("sub")
    blocks = rows.reshape(devices, 4, rows.shape[1])
    return lax.all_to_all(blocks, ("grp", "sub"), 0, 0, tiled=True).reshape(rows.shape)


def body(loads, stiffness, flexibility, coarse_inverse, face_nodes, corner_index):
    rhs, stiff, flex, inverse = loads[0, 0], stiffness[0, 0], flexibility[0, 0], coarse_inverse[0]
    nodes, ids = face_nodes[0, 0], corner_index[0, 0]
    n_load, dofs = rhs.shape
    groups, subs = lax.axis_size("grp"), lax.axis_size("sub")
    n = 16 * subs
    field = ((n_load, dofs), F32)
    sent = ((groups * subs * 4, 4 * n_load), F32)
    total = ((8, 4 * n_load), F32)
    n_tile = n * n // LANES

    def faces(rows, more=0, last=0, first=0):
        return [((size(rows) + more + last * (i == LAST) + first * (i == 0), LANES), F32) for i in range(4)]

    order = inverse.shape[0]
    wide = -(-order // LANES) * LANES
    few = ids.shape[0]
    small = jnp.pad(inverse, ((0, 8), (0, wide - order)))
    small = small + jnp.pad(nodes[None], ((order, 7), (0, wide - 4))).astype(F32)
    small = small + jnp.pad(ids[None], ((order, 7), (4, wide - 4 - few))).astype(F32)
    block = [pltpu.VMEM(sent[0], F32), pltpu.SemaphoreType.DMA]
    corners, vectors, corner, resid, spread, inverse, low, *own = call(
        "start", functools.partial(start, ids.shape[0]), [rhs, stiff, small],
        [((2 * subs * 4, 4 * n_load), F32), ((8, dofs), F32), ((16, dofs), BF16), field, ((64, n), F32), ((n_tile, LANES), F32), field]
        + faces(n_load, 8, 16 * n // LANES, EXTRA),
        [pltpu.VMEM(rhs.shape, F32), pltpu.VMEM(stiff.shape, BF16), pltpu.VMEM((2 * subs * 4, 4 * n_load), F32),
         pltpu.SemaphoreType.DMA((3,))],
        [0, 1], [0], START_LIMIT << 10,
    )
    received = send_pair(corners)
    came = exchange(own)
    inverse = behind(inverse, came[-1])
    other = swap(inverse, "grp", 1)
    zold, sums, corner_map, spread, *own = call(
        "image1", first_image, [received] + own + came + [vectors, corner, resid, spread, low, flex],
        [field, total, ((80, dofs), BF16), ((80, n), F32)] + faces(2 * n_load),
    )
    came = exchange(own)
    flexed, low, inverse, sent_rows, *own = call(
        "local2", second_local, own + came + [sums, vectors, corner_map, inverse, other, stiff],
        [field, ((n_load, dofs), BF16), ((2 * n_tile, LANES), F32), sent] + faces(n_load),
        block, out_place=[3],
    )
    received = send_all(sent_rows)
    came = exchange(own)
    znew, step, sums, before, *own = call(
        "image2", second_image, [received] + own + came + [flexed, zold, low, resid, vectors, corner_map, spread, flex],
        [field, field, total, total] + faces(n_load),
    )
    came = exchange(own)
    inverses = [inverse]
    distance = 2
    while distance < groups:
        held = inverses[0] if distance == 2 else jnp.concatenate(inverses, axis=0)
        inverses.append(swap(behind(held, came[-1]), "grp", distance))
        distance *= 2
    sent_rows, *own = call(
        "local3", third_local, own + came + [sums, vectors, corner_map, stiff], [sent] + faces(n_load),
        block, out_place=[0],
    )
    received = send_all(sent_rows)
    came = exchange(own)
    mult, direction = call(
        "finish", finish,
        [received] + own + came + [before, zold, znew, step, vectors, corner_map, spread] + inverses, [field, field],
        [pltpu.VMEM(rhs.shape, F32)] * 2 + [pltpu.SemaphoreType.DMA((2,))], out_place=[0, 1],
    )
    return (mult[None, None], direction[None, None])


def solution(mesh):
    in_specs = (
        P("grp", "sub", None, None),
        P("grp", "sub", None, None),
        P("grp", "sub", None, None),
        P("grp", None, None),
        P("grp", "sub", None),
        P("grp", "sub", None),
    )
    out_specs = (P("grp", "sub", None, None), P("grp", "sub", None, None))
    return jax.shard_map(body, mesh=mesh, in_specs=in_specs, out_specs=out_specs, check_vma=False)
```

```python
import functools

import jax
import jax.numpy as jnp
from jax import lax
from jax.experimental import pallas as pl
from jax.experimental.pallas import tpu as pltpu
from jax.sharding import PartitionSpec as P

F32, BF16 = jnp.float32, jnp.bfloat16
NT = (((1,), (1,)), ((), ()))
NN = (((1,), (0,)), ((), ()))
LANES = 128
EXTRA = 72
START_LIMIT = 54600


def exact(a, b, dims=NN):
    return lax.dot_general(a, b, dims, precision=lax.Precision.HIGHEST, preferred_element_type=F32)


def rounded(a, b):
    return lax.dot_general(a, b, NN, preferred_element_type=F32)


def thirds(x):
    high = x.astype(BF16)
    rest = x - high.astype(F32)
    mid = rest.astype(BF16)
    return jnp.concatenate([high, mid, (rest - mid.astype(F32)).astype(BF16)], axis=0)


def by_map(x, corner_map, dims):
    n = x.shape[0]
    out = lax.dot_general(thirds(x), corner_map, dims, preferred_element_type=F32)
    return out[:n] + out[n : 2 * n] + out[2 * n :]


def iota(shape, axis):
    return lax.broadcasted_iota(jnp.int32, shape, axis)


FACES = (2, 1, 3, 0)
LAST = FACES.index(3)


def pick_lane(row, lane):
    return jnp.sum(jnp.where(iota(row.shape, 1) == lane, row, 0.0), axis=1, keepdims=True)


def face_vectors(info, dofs):
    width = dofs // 4
    pos = iota((1, dofs), 1)
    sub_pos, grp_pos = lax.axis_index("sub"), lax.axis_index("grp")
    bits = [sub_pos & 1, (sub_pos >> 1) & 1, (sub_pos >> 2) & 1, grp_pos & 1]
    sign = jnp.zeros((1, dofs), F32)
    live = jnp.zeros((1, dofs), jnp.int32)
    node = pos
    for f in range(4):
        inside = (pos >= f * width) & (pos < (f + 1) * width)
        sign = jnp.where(inside, (1 - 2 * bits[f]).astype(F32), sign)
        live = jnp.where(inside, pick_lane(info, f).astype(jnp.int32), live)
    for step in range(1, 12):
        node = jnp.where(pos >= step * (width // 3), pos - step * (width // 3), node)
    mask = jnp.where(node < live, 1.0, 0.0)
    return sign, mask


def corner_ids(info, corners):
    row = iota((16, 1), 0)
    ids = jnp.sum(jnp.where(iota((16, info.shape[1]), 1) == 4 + row % 4 * 4 + row // 4, info, 0.0), axis=1, keepdims=True)
    return jnp.where(row % 4 * 4 < corners, ids, -1.0)


def corner_rows(ids, dofs):
    return jnp.where(ids == iota((16, dofs), 1), 1.0, 0.0)


def size(n_row):
    return n_row + n_row // 2


def put_faces(refs, field):
    n, dofs = field.shape
    width = dofs // 4
    for f, ref in zip(FACES, refs):
        low = f * width
        start = low if low % LANES == 0 else low + LANES // 2
        half = field[:, low + LANES : low + 2 * LANES] if low % LANES == 0 else field[:, start - LANES : start]
        top, bottom = half[: n // 2], half[n // 2 :]
        if low % LANES == 0:
            bottom = pltpu.roll(bottom, LANES // 2, 1)
        else:
            top = pltpu.roll(top, LANES // 2, 1)
        ref[:n, :] = field[:, start : start + LANES]
        ref[n : size(n), :] = jnp.where(iota(top.shape, 1) < LANES // 2, top, bottom)


def from_faces(faces, n):
    by_face = [face for _, face in sorted(zip(FACES, faces), key=lambda item: item[0])]
    tiles = []
    for even, odd in (by_face[:2], by_face[2:]):
        first, second = even[n:], odd[n:]
        left = iota(first.shape, 1) < LANES // 2
        top = jnp.where(left, first, pltpu.roll(second, LANES // 2, 1))
        bottom = jnp.where(left, pltpu.roll(first, LANES // 2, 1), second)
        tiles += [even[:n], jnp.concatenate([top, bottom], axis=0), odd[:n]]
    return jnp.concatenate(tiles, axis=1)


def jump(own, came, n, sign_mask):
    return from_faces([a[: size(n), :] - b[: size(n), :] for a, b in zip(own, came)], n) * sign_mask


def same_block(n_row, n_col, row_block, col_block):
    return iota((n_row, n_col), 0) // row_block == iota((n_row, n_col), 1) // col_block


def to_column(row):
    n = row.shape[1]
    return jnp.sum(jnp.where(same_block(n, n, 1, 1), row, 0.0), axis=1, keepdims=True)


def to_row(column):
    n = column.shape[0]
    return jnp.sum(jnp.where(same_block(n, n, 1, 1), column, 0.0), axis=0, keepdims=True)


def total_of(received):
    total = received[0:8]
    for low in range(8, received.shape[0], 8):
        total = total + received[low : low + 8]
    return total + pltpu.roll(total, 4, 0)


def sums_of(total, n_load):
    column = to_column(total[3:4])
    return [column[i * n_load : (i + 1) * n_load] for i in range(4)]


def halves(x):
    high = x.astype(BF16)
    return jnp.concatenate([high, (x - high.astype(F32)).astype(BF16)], axis=0)


def fine(x, matrix):
    n = x.shape[0]
    both = rounded(halves(x), matrix)
    return both[:n] + both[n:]


def finer(x, matrix):
    n = x.shape[0]
    high = matrix.astype(BF16)
    low = (matrix - high.astype(F32)).astype(BF16)
    parts = halves(x)
    both = lax.dot_general(parts, high, NT, preferred_element_type=F32)
    return both[:n] + both[n:] + lax.dot_general(parts[:n], low, NT, preferred_element_type=F32)


def packed_corners(scaled, corner):
    n_load = scaled.shape[0]
    values = by_map(scaled, corner, NT)
    flipped = jnp.concatenate([values] * 4, axis=0).T
    flipped = jnp.where(same_block(16, 4 * n_load, 4, n_load), flipped, 0.0)
    block = flipped[:8] + flipped[8:]
    return block + pltpu.roll(block, 4, 0)


def with_sums(block, sums):
    zero = jnp.zeros_like(sums[0])
    row = to_row(jnp.concatenate(sums + [zero] * (4 - len(sums)), axis=0))
    return jnp.where(iota(block.shape, 0) % 4 == 3, row, block)


def put_all(out, block):
    for low in range(0, out.shape[0], 8):
        out[low : low + 8, :] = block


def group_corners(received, which, rows, n_load):
    block = received[pl.ds(pl.multiple_of(which * rows, 8), rows), :]
    block = jnp.where(iota(block.shape, 0) % 4 == 3, 0.0, block)
    tall = jnp.concatenate([block] * 4, axis=0)
    flipped = jnp.where(same_block(4 * rows, 4 * n_load, rows, n_load), tall, 0.0).T
    return sum(flipped[r * n_load : (r + 1) * n_load] for r in range(1, 4)) + flipped[:n_load]


def coarse_of(inner, outer, spread):
    n = inner.shape[0]
    both = finer(jnp.concatenate([inner, outer], axis=0), spread)
    return jnp.where(iota((n, both.shape[1]), 1) < 64, both[:n], both[n:])


def two_groups(received, rows, n_load):
    grp_pos = lax.axis_index("grp")
    if received.shape[0] == 2 * rows:
        grp_pos = grp_pos & 1
    return [group_corners(received, which, rows, n_load) for which in (grp_pos, grp_pos ^ 1)]


def to_tiles(matrix):
    return jnp.concatenate([matrix[:, low : low + LANES] for low in range(0, matrix.shape[1], LANES)], axis=0)


def from_tiles(rows, n):
    n_row = rows.shape[0] * LANES // n
    return jnp.concatenate([rows[low : low + n_row] for low in range(0, rows.shape[0], n_row)], axis=1)


def rows_sum(x):
    return jnp.sum(x, axis=1, keepdims=True)


def start(
    corners, rhs_hbm, stiff_hbm, small,
    sent, vectors, corner_out, resid_out, spread_out, coarse_out, low_out, w0, w1, w2, w3,
    rhs, stiff, block, sems,
):
    pairs = [(rhs_hbm, rhs), (stiff_hbm, stiff), (block, sent)]
    copies = [pltpu.make_async_copy(a, b, sems.at[i]) for i, (a, b) in enumerate(pairs)]
    for copy in copies[:2]:
        copy.start()
    n_load, dofs = rhs.shape
    wins = [w0, w1, w2, w3]
    n = small.shape[0] - 8
    info = small[n : n + 1, :LANES]
    sign, mask = face_vectors(info, dofs)
    vectors[0:1, :] = sign
    vectors[1:2, :] = mask
    vectors[2:3, :] = sign * mask
    vectors[3:8, :] = jnp.zeros((5, dofs), F32)
    ids = corner_ids(info, corners)
    corner = corner_rows(ids.astype(jnp.int32), dofs).astype(BF16)
    corner_out[...] = corner
    ids = jnp.sum(jnp.where(same_block(16, LANES, 1, 1), ids, 0.0), axis=0, keepdims=True)
    for ref in wins:
        ref[size(n_load) : size(n_load) + 8, :] = jnp.broadcast_to(ids, (8, LANES))
    copies[0].wait()
    resid = rhs[...] * mask
    resid_out[...] = resid
    scaled = 0.5 * sign * resid
    put_all(block, packed_corners(scaled, corner))
    copies[2].start()
    wide = small.shape[1]
    subs = n // corners
    sub_pos = lax.axis_index("sub")
    row = iota((64, 1), 0)
    owner = jnp.where(row < 16, sub_pos, jnp.where(row < 32, sub_pos ^ 1, jnp.where(row < 48, sub_pos ^ 2, sub_pos ^ 4)))
    source = owner * corners + row % 4 * 4 + row // 4 % 4
    pick = jnp.where((source == iota((64, n), 1)) & (row % 4 * 4 < corners), 1.0, 0.0)
    place = iota((16 * subs, 1), 0)
    source = place // 4 % subs * corners + place % 4 * 4 + place // (4 * subs)
    order = jnp.where((source == iota((16 * subs, wide), 1)) & (place % 4 * 4 < corners), 1.0, 0.0).astype(BF16)
    pick = jnp.concatenate([pick, order[:, :n].astype(F32)], axis=0).astype(BF16)
    parts = thirds(small[:n, :])
    picked = rounded(pick, parts[:n]) + rounded(pick, parts[n : 2 * n]) + rounded(pick, parts[2 * n :])
    both = by_map(picked, order, NT)
    spread_out[...] = both[:64]
    coarse_out[...] = to_tiles(both[64:])
    wins[LAST][size(n_load) + 8 :, :] = to_tiles(both[:16])
    wins[0][size(n_load) + 8 :, :] = jnp.zeros((EXTRA, LANES), F32)
    copies[1].wait()
    local = rounded(halves(scaled), stiff[...])
    put_faces(wins, local[:n_load])
    low_out[...] = local[n_load:]
    copies[2].wait()


def first_image(
    received, o0, o1, o2, o3, a0, a1, a2, a3, vectors, corner, resid, spread, low, flex,
    z_out, sums_out, map_out, spread_out, *wins,
):
    n_load, dofs = resid.shape
    came = [a0, a1, a2, a3]
    sign, sign_mask = vectors[0:1, :], vectors[2:3, :]
    width = dofs // 4
    pos = iota((1, dofs), 1)
    pieces = [corner[...].astype(F32) * sign_mask]
    for f in range(4):
        ids = to_column(came[FACES.index(f)][size(n_load) : size(n_load) + 1, :])[:16].astype(jnp.int32)
        inside = (pos >= f * width) & (pos < (f + 1) * width)
        pieces.append(corner_rows(ids, dofs) * jnp.where(inside, -sign_mask, 0.0))
    corner_map = jnp.concatenate(pieces, axis=0).astype(BF16)
    map_out[...] = corner_map
    n = spread.shape[1]
    cross = from_tiles(came[LAST][size(n_load) + 8 :, :], n)
    spread_rows = jnp.concatenate([spread[...], cross], axis=0)
    spread_out[...] = spread_rows
    coarse = coarse_of(*two_groups(received, n // 4, n_load), spread_rows)
    zvec = jump([o0, o1, o2, o3], came, n_load, sign_mask) + by_map(coarse, corner_map, NN)
    z_out[...] = zvec
    signed = sign * zvec
    image = rounded(signed.astype(BF16), flex[...])
    put_faces(wins, jnp.concatenate([image, low[...]], axis=0))
    sums_out[...] = with_sums(
        jnp.zeros((8, 4 * n_load), F32), [rows_sum(resid[...] * zvec), 2.0 * rows_sum(signed * image)]
    )


def second_local(
    o0, o1, o2, o3, a0, a1, a2, a3, sums, vectors, corner_map, inverse, other, stiff,
    flexed_out, low_out, inverse_out, sent, w0, w1, w2, w3, block, sem,
):
    n_load, dofs = flexed_out.shape
    sign, sign_mask = vectors[0:1, :], vectors[2:3, :]
    jumped = jump([o0, o1, o2, o3], [a0, a1, a2, a3], 2 * n_load, sign_mask)
    flexed = jumped[:n_load]
    flexed_out[...] = flexed
    inverse_out[: inverse.shape[0], :] = inverse[...]
    inverse_out[inverse.shape[0] :, :] = other[...]
    low_out[...] = jumped[n_load:].astype(BF16)
    scaled = 0.5 * sign * flexed
    is_sum = iota((8, 1), 0) % 4 == 3
    corners = packed_corners(scaled, abs(corner_map[:16, :]))
    put_all(block, jnp.where(is_sum, sums[...], corners))
    copy = pltpu.make_async_copy(block, sent, sem)
    copy.start()
    put_faces([w0, w1, w2, w3], fine(scaled, stiff[...]))
    copy.wait()


def second_coarse(received, corner_map, spread, total_out, field_out):
    n_load = field_out.shape[0]
    total_out[...] = total_of(received)
    coarse = coarse_of(*two_groups(received, spread.shape[1] // 4, n_load), spread[...])
    field_out[...] = by_map(coarse, corner_map[...], NN)


def second_image(
    total, field, o0, o1, o2, o3, a0, a1, a2, a3, flexed, zold, low, resid, vectors, flex,
    z_out, step_out, sums_out, *wins,
):
    n_load, dofs = resid.shape
    sign, sign_mask = vectors[0:1, :], vectors[2:3, :]
    rz, curve, _, _ = sums_of(total[...], n_load)
    alpha = rz / curve
    step = jump([o0, o1, o2, o3], [a0, a1, a2, a3], n_load, sign_mask) + field[...]
    step = alpha * step
    step_out[...] = step
    zvec = zold[...] + low[...].astype(F32) - step
    z_out[...] = zvec
    signed = sign * zvec
    image = alpha * fine(signed, flex[...])
    put_faces(wins, image)
    scaled_flexed = alpha * flexed[...]
    sums = [
        rows_sum((resid[...] - scaled_flexed) * zvec),
        2.0 * rows_sum(signed * image),
        rows_sum(zvec * scaled_flexed),
    ]
    sums_out[...] = with_sums(jnp.zeros((8, 4 * n_load), F32), sums)


def third_local(o0, o1, o2, o3, a0, a1, a2, a3, sums, vectors, corner_map, stiff, sent, w0, w1, w2, w3, block, sem):
    n_load, dofs = o0.shape[0] * 2 // 3, vectors.shape[1]
    sign, sign_mask = vectors[0:1, :], vectors[2:3, :]
    flexed = jump([o0, o1, o2, o3], [a0, a1, a2, a3], n_load, sign_mask)
    scaled = 0.5 * sign * flexed
    local = fine(scaled, stiff[...])
    fourth = jnp.where(iota((1, 4 * n_load), 1) // n_load == 3, 1.0, 0.0)
    square = with_sums(jnp.zeros((8, 4 * n_load), F32), [4.0 * rows_sum(scaled * local)] * 4) * fourth
    is_sum = iota((8, 1), 0) % 4 == 3
    put_all(block, jnp.where(is_sum, sums[...] + square, packed_corners(scaled, abs(corner_map[:16, :]))))
    copy = pltpu.make_async_copy(block, sent, sem)
    copy.start()
    put_faces([w0, w1, w2, w3], local)
    copy.wait()


def third_coarse(received, before, zold, znew, step, corner_map, spread, *rest):
    inverses, (mult_out, base_out, gamma_out) = rest[:-3], rest[-3:]
    n_load = zold.shape[0]
    rz0, curve0, _, _ = sums_of(before[...], n_load)
    rz1, curve, mixed, square = sums_of(total_of(received), n_load)
    alpha = rz0 / curve0
    beta = rz1 / rz0
    gamma = rz1 / (curve + 2.0 * beta * mixed + beta * beta * rz0)
    direction = znew[...] + beta * zold[...]
    mult_out[...] = alpha * (zold[...] + gamma * direction)
    n = spread.shape[1]
    height = n * n // LANES
    corners = two_groups(received, n // 4, n_load)
    index = 0
    for ref in inverses:
        for low in range(0, ref.shape[0], height):
            if index == len(corners):
                corners.append(group_corners(received, lax.axis_index("grp") ^ index, n // 4, n_load))
            values = corners[index]
            square = square + 4.0 * rows_sum(values * finer(values, from_tiles(ref[low : low + height, :], n)))
            index += 1
    rz2 = square + 2.0 * beta * (mixed - curve) + beta * beta * (rz0 - mixed)
    rz2 = rz1 - 2.0 * gamma * (curve + beta * mixed) + gamma * gamma * rz2
    field = by_map(coarse_of(*corners[:2], spread[...]), corner_map[...], NN)
    base_out[...] = znew[...] - gamma * (field + beta * step[...]) + (rz2 / rz1) * direction
    gamma_out[...] = jnp.broadcast_to(gamma, gamma_out.shape)


def finish(o0, o1, o2, o3, a0, a1, a2, a3, base, gamma, mult, vectors, mult_hbm, direction_hbm, out, sems):
    n_load = base.shape[0]
    first = pltpu.make_async_copy(mult, mult_hbm, sems.at[0])
    first.start()
    jumped = jump([o0, o1, o2, o3], [a0, a1, a2, a3], n_load, vectors[2:3, :])
    out[...] = base[...] - gamma[:, :1] * jumped
    second = pltpu.make_async_copy(out, direction_hbm, sems.at[1])
    second.start()
    first.wait()
    second.wait()


def call(name, kernel, args, outs, scratch=(), in_place=(), out_place=(), limit=None):
    shapes = [jax.ShapeDtypeStruct(s, d) for s, d in outs]
    n_bytes = sum(a.size * a.dtype.itemsize for a in args) + sum(s.size * s.dtype.itemsize for s in shapes)
    return pl.pallas_call(
        kernel,
        out_shape=shapes,
        in_specs=[pl.BlockSpec(memory_space=pl.ANY if i in in_place else pltpu.VMEM) for i in range(len(args))],
        out_specs=[pl.BlockSpec(memory_space=pl.ANY if i in out_place else pltpu.VMEM) for i in range(len(outs))],
        scratch_shapes=scratch,
        cost_estimate=pl.CostEstimate(flops=40_000_000, bytes_accessed=n_bytes, transcendentals=0),
        compiler_params=pltpu.CompilerParams(vmem_limit_bytes=limit or (12 << 20) + 2 * n_bytes),
        name=name,
    )(*args)


def behind(block, other):
    return pl.pallas_call(
        lambda block_ref, other_ref, out_ref: None,
        out_shape=jax.ShapeDtypeStruct(block.shape, block.dtype),
        in_specs=[pl.BlockSpec(memory_space=pl.ANY)] * 2,
        out_specs=pl.BlockSpec(memory_space=pl.ANY),
        input_output_aliases={0: 0},
        compiler_params=pltpu.CompilerParams(vmem_limit_bytes=1 << 20),
        name="behind",
    )(block, other)


def swap(block, axis, distance):
    count = lax.axis_size(axis)
    return lax.ppermute(block, axis, [(i, i ^ distance) for i in range(count) if i ^ distance < count])


def exchange(wins):
    return [swap(win, "grp", 1) if f == 3 else swap(win, "sub", 1 << f) for f, win in zip(FACES, wins)]


def send_pair(rows):
    subs = lax.axis_size("sub")
    devices = 2 * subs
    blocks = rows.reshape(devices, 4, rows.shape[1])
    teams = [list(range(low, low + devices)) for low in range(0, lax.axis_size("grp") * subs, devices)]
    return lax.all_to_all(blocks, ("grp", "sub"), 0, 0, tiled=True, axis_index_groups=teams).reshape(rows.shape)


def send_all(rows):
    devices = lax.axis_size("grp") * lax.axis_size("sub")
    blocks = rows.reshape(devices, 4, rows.shape[1])
    return lax.all_to_all(blocks, ("grp", "sub"), 0, 0, tiled=True).reshape(rows.shape)


def body(loads, stiffness, flexibility, coarse_inverse, face_nodes, corner_index):
    rhs, stiff, flex, inverse = loads[0, 0], stiffness[0, 0], flexibility[0, 0], coarse_inverse[0]
    nodes, ids = face_nodes[0, 0], corner_index[0, 0]
    n_load, dofs = rhs.shape
    groups, subs = lax.axis_size("grp"), lax.axis_size("sub")
    n = 16 * subs
    field = ((n_load, dofs), F32)
    sent = ((groups * subs * 4, 4 * n_load), F32)
    total = ((8, 4 * n_load), F32)
    n_tile = n * n // LANES

    def faces(rows, more=0, last=0, first=0):
        return [((size(rows) + more + last * (i == LAST) + first * (i == 0), LANES), F32) for i in range(4)]

    order = inverse.shape[0]
    wide = -(-order // LANES) * LANES
    few = ids.shape[0]
    small = jnp.pad(inverse, ((0, 8), (0, wide - order)))
    small = small + jnp.pad(nodes[None], ((order, 7), (0, wide - 4))).astype(F32)
    small = small + jnp.pad(ids[None], ((order, 7), (4, wide - 4 - few))).astype(F32)
    block = [pltpu.VMEM(sent[0], F32), pltpu.SemaphoreType.DMA]
    corners, vectors, corner, resid, spread, inverse, low, *own = call(
        "start", functools.partial(start, ids.shape[0]), [rhs, stiff, small],
        [((2 * subs * 4, 4 * n_load), F32), ((8, dofs), F32), ((16, dofs), BF16), field, ((64, n), F32), ((n_tile, LANES), F32), field]
        + faces(n_load, 8, 16 * n // LANES, EXTRA),
        [pltpu.VMEM(rhs.shape, F32), pltpu.VMEM(stiff.shape, BF16), pltpu.VMEM((2 * subs * 4, 4 * n_load), F32),
         pltpu.SemaphoreType.DMA((3,))],
        [0, 1], [0], START_LIMIT << 10,
    )
    received = send_pair(corners)
    came = exchange(own)
    inverse = behind(inverse, came[-1])
    other = swap(inverse, "grp", 1)
    zold, sums, corner_map, spread, *own = call(
        "image1", first_image, [received] + own + came + [vectors, corner, resid, spread, low, flex],
        [field, total, ((80, dofs), BF16), ((80, n), F32)] + faces(2 * n_load),
    )
    came = exchange(own)
    flexed, low, inverse, sent_rows, *own = call(
        "local2", second_local, own + came + [sums, vectors, corner_map, inverse, other, stiff],
        [field, ((n_load, dofs), BF16), ((2 * n_tile, LANES), F32), sent] + faces(n_load),
        block, out_place=[3],
    )
    received = send_all(sent_rows)
    came = exchange(own)
    before, coarse = call("coarse2", second_coarse, [received, corner_map, spread], [total, field])
    znew, step, sums, *own = call(
        "image2", second_image, [before, coarse] + own + came + [flexed, zold, low, resid, vectors, flex],
        [field, field, total] + faces(n_load),
    )
    came = exchange(own)
    inverses = [inverse]
    distance = 2
    while distance < groups:
        held = inverses[0] if distance == 2 else jnp.concatenate(inverses, axis=0)
        inverses.append(swap(behind(held, came[-1]), "grp", distance))
        distance *= 2
    sent_rows, *own = call(
        "local3", third_local, own + came + [sums, vectors, corner_map, stiff], [sent] + faces(n_load),
        block, out_place=[0],
    )
    received = send_all(sent_rows)
    came = exchange(own)
    mult, base, gamma = call(
        "coarse3", third_coarse, [received, before, zold, znew, step, corner_map, spread] + inverses,
        [field, field, ((n_load, LANES), F32)],
    )
    mult, direction = call(
        "finish", finish, own + came + [base, gamma, mult, vectors], [field, field],
        [pltpu.VMEM(rhs.shape, F32), pltpu.SemaphoreType.DMA((2,))], out_place=[0, 1],
    )
    return (mult[None, None], direction[None, None])


def solution(mesh):
    in_specs = (
        P("grp", "sub", None, None),
        P("grp", "sub", None, None),
        P("grp", "sub", None, None),
        P("grp", None, None),
        P("grp", "sub", None),
        P("grp", "sub", None),
    )
    out_specs = (P("grp", "sub", None, None), P("grp", "sub", None, None))
    return jax.shard_map(body, mesh=mesh, in_specs=in_specs, out_specs=out_specs, check_vma=False)
```

```python
import functools

import jax
import jax.numpy as jnp
from jax import lax
from jax.experimental import pallas as pl
from jax.experimental.pallas import tpu as pltpu
from jax.sharding import PartitionSpec as P

F32, BF16 = jnp.float32, jnp.bfloat16
NT = (((1,), (1,)), ((), ()))
NN = (((1,), (0,)), ((), ()))
LANES = 128
EXTRA = 72
START_LIMIT = 54600


def exact(a, b, dims=NN):
    return lax.dot_general(a, b, dims, precision=lax.Precision.HIGHEST, preferred_element_type=F32)


def rounded(a, b):
    return lax.dot_general(a, b, NN, preferred_element_type=F32)


def thirds(x):
    high = x.astype(BF16)
    rest = x - high.astype(F32)
    mid = rest.astype(BF16)
    return jnp.concatenate([high, mid, (rest - mid.astype(F32)).astype(BF16)], axis=0)


def by_map(x, corner_map, dims):
    n = x.shape[0]
    out = lax.dot_general(thirds(x), corner_map, dims, preferred_element_type=F32)
    return out[:n] + out[n : 2 * n] + out[2 * n :]


def iota(shape, axis):
    return lax.broadcasted_iota(jnp.int32, shape, axis)


FACES = (2, 1, 3, 0)
LAST = FACES.index(3)


def pick_lane(row, lane):
    return jnp.sum(jnp.where(iota(row.shape, 1) == lane, row, 0.0), axis=1, keepdims=True)


def face_vectors(info, dofs):
    width = dofs // 4
    pos = iota((1, dofs), 1)
    sub_pos, grp_pos = lax.axis_index("sub"), lax.axis_index("grp")
    bits = [sub_pos & 1, (sub_pos >> 1) & 1, (sub_pos >> 2) & 1, grp_pos & 1]
    sign = jnp.zeros((1, dofs), F32)
    live = jnp.zeros((1, dofs), jnp.int32)
    node = pos
    for f in range(4):
        inside = (pos >= f * width) & (pos < (f + 1) * width)
        sign = jnp.where(inside, (1 - 2 * bits[f]).astype(F32), sign)
        live = jnp.where(inside, pick_lane(info, f).astype(jnp.int32), live)
    for step in range(1, 12):
        node = jnp.where(pos >= step * (width // 3), pos - step * (width // 3), node)
    mask = jnp.where(node < live, 1.0, 0.0)
    return sign, mask


def corner_ids(info, corners):
    row = iota((16, 1), 0)
    ids = jnp.sum(jnp.where(iota((16, info.shape[1]), 1) == 4 + row % 4 * 4 + row // 4, info, 0.0), axis=1, keepdims=True)
    return jnp.where(row % 4 * 4 < corners, ids, -1.0)


def corner_rows(ids, dofs):
    return jnp.where(ids == iota((16, dofs), 1), 1.0, 0.0)


def size(n_row):
    return n_row + n_row // 2


def put_faces(refs, field):
    n, dofs = field.shape
    width = dofs // 4
    for f, ref in zip(FACES, refs):
        low = f * width
        start = low if low % LANES == 0 else low + LANES // 2
        half = field[:, low + LANES : low + 2 * LANES] if low % LANES == 0 else field[:, start - LANES : start]
        top, bottom = half[: n // 2], half[n // 2 :]
        if low % LANES == 0:
            bottom = pltpu.roll(bottom, LANES // 2, 1)
        else:
            top = pltpu.roll(top, LANES // 2, 1)
        ref[:n, :] = field[:, start : start + LANES]
        ref[n : size(n), :] = jnp.where(iota(top.shape, 1) < LANES // 2, top, bottom)


def from_faces(faces, n):
    by_face = [face for _, face in sorted(zip(FACES, faces), key=lambda item: item[0])]
    tiles = []
    for even, odd in (by_face[:2], by_face[2:]):
        first, second = even[n:], odd[n:]
        left = iota(first.shape, 1) < LANES // 2
        top = jnp.where(left, first, pltpu.roll(second, LANES // 2, 1))
        bottom = jnp.where(left, pltpu.roll(first, LANES // 2, 1), second)
        tiles += [even[:n], jnp.concatenate([top, bottom], axis=0), odd[:n]]
    return jnp.concatenate(tiles, axis=1)


def jump(own, came, n, sign_mask):
    return from_faces([a[: size(n), :] - b[: size(n), :] for a, b in zip(own, came)], n) * sign_mask


def same_block(n_row, n_col, row_block, col_block):
    return iota((n_row, n_col), 0) // row_block == iota((n_row, n_col), 1) // col_block


def to_column(row):
    n = row.shape[1]
    return jnp.sum(jnp.where(same_block(n, n, 1, 1), row, 0.0), axis=1, keepdims=True)


def to_row(column):
    n = column.shape[0]
    return jnp.sum(jnp.where(same_block(n, n, 1, 1), column, 0.0), axis=0, keepdims=True)


def total_of(received):
    total = received[0:8]
    for low in range(8, received.shape[0], 8):
        total = total + received[low : low + 8]
    return total + pltpu.roll(total, 4, 0)


def sums_of(total, n_load):
    column = to_column(total[3:4])
    return [column[i * n_load : (i + 1) * n_load] for i in range(4)]


def halves(x):
    high = x.astype(BF16)
    return jnp.concatenate([high, (x - high.astype(F32)).astype(BF16)], axis=0)


def fine(x, matrix):
    n = x.shape[0]
    both = rounded(halves(x), matrix)
    return both[:n] + both[n:]


def finer(x, matrix):
    n = x.shape[0]
    high = matrix.astype(BF16)
    low = (matrix - high.astype(F32)).astype(BF16)
    parts = halves(x)
    both = lax.dot_general(parts, high, NT, preferred_element_type=F32)
    return both[:n] + both[n:] + lax.dot_general(parts[:n], low, NT, preferred_element_type=F32)


def packed_corners(scaled, corner):
    n_load = scaled.shape[0]
    values = by_map(scaled, corner, NT)
    flipped = jnp.concatenate([values] * 4, axis=0).T
    flipped = jnp.where(same_block(16, 4 * n_load, 4, n_load), flipped, 0.0)
    block = flipped[:8] + flipped[8:]
    return block + pltpu.roll(block, 4, 0)


def with_sums(block, sums):
    zero = jnp.zeros_like(sums[0])
    row = to_row(jnp.concatenate(sums + [zero] * (4 - len(sums)), axis=0))
    return jnp.where(iota(block.shape, 0) % 4 == 3, row, block)


def put_all(out, block):
    for low in range(0, out.shape[0], 8):
        out[low : low + 8, :] = block


def group_corners(received, which, rows, n_load):
    block = received[pl.ds(pl.multiple_of(which * rows, 8), rows), :]
    block = jnp.where(iota(block.shape, 0) % 4 == 3, 0.0, block)
    tall = jnp.concatenate([block] * 4, axis=0)
    flipped = jnp.where(same_block(4 * rows, 4 * n_load, rows, n_load), tall, 0.0).T
    return sum(flipped[r * n_load : (r + 1) * n_load] for r in range(1, 4)) + flipped[:n_load]


def coarse_of(inner, outer, spread):
    n = inner.shape[0]
    both = finer(jnp.concatenate([inner, outer], axis=0), spread)
    return jnp.where(iota((n, both.shape[1]), 1) < 64, both[:n], both[n:])


def two_groups(received, rows, n_load):
    grp_pos = lax.axis_index("grp")
    if received.shape[0] == 2 * rows:
        grp_pos = grp_pos & 1
    return [group_corners(received, which, rows, n_load) for which in (grp_pos, grp_pos ^ 1)]


def to_tiles(matrix):
    return jnp.concatenate([matrix[:, low : low + LANES] for low in range(0, matrix.shape[1], LANES)], axis=0)


def from_tiles(rows, n):
    n_row = rows.shape[0] * LANES // n
    return jnp.concatenate([rows[low : low + n_row] for low in range(0, rows.shape[0], n_row)], axis=1)


def rows_sum(x):
    return jnp.sum(x, axis=1, keepdims=True)


def start(
    corners, rhs_hbm, stiff_hbm, small,
    sent, vectors, corner_out, resid_out, spread_out, coarse_out, low_out, w0, w1, w2, w3,
    rhs, stiff, block, sems,
):
    pairs = [(rhs_hbm, rhs), (stiff_hbm, stiff), (block, sent)]
    copies = [pltpu.make_async_copy(a, b, sems.at[i]) for i, (a, b) in enumerate(pairs)]
    for copy in copies[:2]:
        copy.start()
    n_load, dofs = rhs.shape
    wins = [w0, w1, w2, w3]
    n = small.shape[0] - 8
    info = small[n : n + 1, :LANES]
    sign, mask = face_vectors(info, dofs)
    vectors[0:1, :] = sign
    vectors[1:2, :] = mask
    vectors[2:3, :] = sign * mask
    vectors[3:8, :] = jnp.zeros((5, dofs), F32)
    ids = corner_ids(info, corners)
    corner = corner_rows(ids.astype(jnp.int32), dofs).astype(BF16)
    corner_out[...] = corner
    ids = jnp.sum(jnp.where(same_block(16, LANES, 1, 1), ids, 0.0), axis=0, keepdims=True)
    for ref in wins:
        ref[size(n_load) : size(n_load) + 8, :] = jnp.broadcast_to(ids, (8, LANES))
    copies[0].wait()
    resid = rhs[...] * mask
    resid_out[...] = resid
    scaled = 0.5 * sign * resid
    put_all(block, packed_corners(scaled, corner))
    copies[2].start()
    wide = small.shape[1]
    subs = n // corners
    sub_pos = lax.axis_index("sub")
    row = iota((64, 1), 0)
    owner = jnp.where(row < 16, sub_pos, jnp.where(row < 32, sub_pos ^ 1, jnp.where(row < 48, sub_pos ^ 2, sub_pos ^ 4)))
    source = owner * corners + row % 4 * 4 + row // 4 % 4
    pick = jnp.where((source == iota((64, n), 1)) & (row % 4 * 4 < corners), 1.0, 0.0)
    place = iota((16 * subs, 1), 0)
    source = place // 4 % subs * corners + place % 4 * 4 + place // (4 * subs)
    order = jnp.where((source == iota((16 * subs, wide), 1)) & (place % 4 * 4 < corners), 1.0, 0.0).astype(BF16)
    pick = jnp.concatenate([pick, order[:, :n].astype(F32)], axis=0).astype(BF16)
    parts = thirds(small[:n, :])
    picked = rounded(pick, parts[:n]) + rounded(pick, parts[n : 2 * n]) + rounded(pick, parts[2 * n :])
    both = by_map(picked, order, NT)
    spread_out[...] = both[:64]
    coarse_out[...] = to_tiles(both[64:])
    wins[LAST][size(n_load) + 8 :, :] = to_tiles(both[:16])
    wins[0][size(n_load) + 8 :, :] = jnp.zeros((EXTRA, LANES), F32)
    copies[1].wait()
    local = rounded(halves(scaled), stiff[...])
    put_faces(wins, local[:n_load])
    low_out[...] = local[n_load:]
    copies[2].wait()


def first_image(
    received, o0, o1, o2, o3, a0, a1, a2, a3, vectors, corner, spread, low, flex,
    z_out, map_out, spread_out, *wins,
):
    n_load, dofs = low.shape
    came = [a0, a1, a2, a3]
    sign, sign_mask = vectors[0:1, :], vectors[2:3, :]
    width = dofs // 4
    pos = iota((1, dofs), 1)
    pieces = [corner[...].astype(F32) * sign_mask]
    for f in range(4):
        ids = to_column(came[FACES.index(f)][size(n_load) : size(n_load) + 1, :])[:16].astype(jnp.int32)
        inside = (pos >= f * width) & (pos < (f + 1) * width)
        pieces.append(corner_rows(ids, dofs) * jnp.where(inside, -sign_mask, 0.0))
    corner_map = jnp.concatenate(pieces, axis=0).astype(BF16)
    map_out[...] = corner_map
    n = spread.shape[1]
    cross = from_tiles(came[LAST][size(n_load) + 8 :, :], n)
    spread_rows = jnp.concatenate([spread[...], cross], axis=0)
    spread_out[...] = spread_rows
    coarse = coarse_of(*two_groups(received, n // 4, n_load), spread_rows)
    zvec = jump([o0, o1, o2, o3], came, n_load, sign_mask) + by_map(coarse, corner_map, NN)
    z_out[...] = zvec
    signed = sign * zvec
    image = rounded(signed.astype(BF16), flex[...])
    put_faces(wins, jnp.concatenate([image, low[...]], axis=0))


def first_sums(o0, o1, o2, o3, zvec, resid, vectors, out):
    n_load = zvec.shape[0]
    image = from_faces([o0[...], o1[...], o2[...], o3[...]], 2 * n_load)[:n_load]
    sums = [rows_sum(resid[...] * zvec[...]), 2.0 * rows_sum(vectors[0:1, :] * zvec[...] * image)]
    out[...] = with_sums(jnp.zeros((8, 4 * n_load), F32), sums)


def second_local(
    o0, o1, o2, o3, a0, a1, a2, a3, sums, vectors, corner_map, inverse, other, stiff,
    flexed_out, low_out, inverse_out, sent, w0, w1, w2, w3, block, sem,
):
    n_load, dofs = flexed_out.shape
    sign, sign_mask = vectors[0:1, :], vectors[2:3, :]
    jumped = jump([o0, o1, o2, o3], [a0, a1, a2, a3], 2 * n_load, sign_mask)
    flexed = jumped[:n_load]
    flexed_out[...] = flexed
    inverse_out[: inverse.shape[0], :] = inverse[...]
    inverse_out[inverse.shape[0] :, :] = other[...]
    low_out[...] = jumped[n_load:].astype(BF16)
    scaled = 0.5 * sign * flexed
    is_sum = iota((8, 1), 0) % 4 == 3
    corners = packed_corners(scaled, abs(corner_map[:16, :]))
    put_all(block, jnp.where(is_sum, sums[...], corners))
    copy = pltpu.make_async_copy(block, sent, sem)
    copy.start()
    put_faces([w0, w1, w2, w3], fine(scaled, stiff[...]))
    copy.wait()


def second_coarse(received, corner_map, spread, total_out, field_out):
    n_load = field_out.shape[0]
    total_out[...] = total_of(received)
    coarse = coarse_of(*two_groups(received, spread.shape[1] // 4, n_load), spread[...])
    field_out[...] = by_map(coarse, corner_map[...], NN)


def second_image(
    total, field, o0, o1, o2, o3, a0, a1, a2, a3, zold, low, vectors, flex, z_out, step_out, *wins,
):
    n_load, dofs = zold.shape
    sign, sign_mask = vectors[0:1, :], vectors[2:3, :]
    rz, curve, _, _ = sums_of(total[...], n_load)
    alpha = rz / curve
    step = jump([o0, o1, o2, o3], [a0, a1, a2, a3], n_load, sign_mask) + field[...]
    step = alpha * step
    step_out[...] = step
    zvec = zold[...] + low[...].astype(F32) - step
    z_out[...] = zvec
    signed = sign * zvec
    image = alpha * fine(signed, flex[...])
    put_faces(wins, image)


def second_sums(total, o0, o1, o2, o3, zvec, flexed, resid, vectors, out):
    n_load = zvec.shape[0]
    rz, curve, _, _ = sums_of(total[...], n_load)
    scaled_flexed = rz / curve * flexed[...]
    image = from_faces([o0[...], o1[...], o2[...], o3[...]], n_load)
    sums = [
        rows_sum((resid[...] - scaled_flexed) * zvec[...]),
        2.0 * rows_sum(vectors[0:1, :] * zvec[...] * image),
        rows_sum(zvec[...] * scaled_flexed),
    ]
    out[...] = with_sums(jnp.zeros((8, 4 * n_load), F32), sums)


def third_local(o0, o1, o2, o3, a0, a1, a2, a3, sums, vectors, corner_map, stiff, sent, w0, w1, w2, w3, block, sem):
    n_load, dofs = o0.shape[0] * 2 // 3, vectors.shape[1]
    sign, sign_mask = vectors[0:1, :], vectors[2:3, :]
    flexed = jump([o0, o1, o2, o3], [a0, a1, a2, a3], n_load, sign_mask)
    scaled = 0.5 * sign * flexed
    local = fine(scaled, stiff[...])
    fourth = jnp.where(iota((1, 4 * n_load), 1) // n_load == 3, 1.0, 0.0)
    square = with_sums(jnp.zeros((8, 4 * n_load), F32), [4.0 * rows_sum(scaled * local)] * 4) * fourth
    is_sum = iota((8, 1), 0) % 4 == 3
    put_all(block, jnp.where(is_sum, sums[...] + square, packed_corners(scaled, abs(corner_map[:16, :]))))
    copy = pltpu.make_async_copy(block, sent, sem)
    copy.start()
    put_faces([w0, w1, w2, w3], local)
    copy.wait()


def third_coarse(received, before, zold, znew, step, corner_map, spread, *rest):
    inverses, (mult_out, base_out, gamma_out) = rest[:-3], rest[-3:]
    n_load = zold.shape[0]
    rz0, curve0, _, _ = sums_of(before[...], n_load)
    rz1, curve, mixed, square = sums_of(total_of(received), n_load)
    alpha = rz0 / curve0
    beta = rz1 / rz0
    gamma = rz1 / (curve + 2.0 * beta * mixed + beta * beta * rz0)
    direction = znew[...] + beta * zold[...]
    mult_out[...] = alpha * (zold[...] + gamma * direction)
    n = spread.shape[1]
    height = n * n // LANES
    corners = two_groups(received, n // 4, n_load)
    index = 0
    for ref in inverses:
        for low in range(0, ref.shape[0], height):
            if index == len(corners):
                corners.append(group_corners(received, lax.axis_index("grp") ^ index, n // 4, n_load))
            values = corners[index]
            square = square + 4.0 * rows_sum(values * finer(values, from_tiles(ref[low : low + height, :], n)))
            index += 1
    rz2 = square + 2.0 * beta * (mixed - curve) + beta * beta * (rz0 - mixed)
    rz2 = rz1 - 2.0 * gamma * (curve + beta * mixed) + gamma * gamma * rz2
    field = by_map(coarse_of(*corners[:2], spread[...]), corner_map[...], NN)
    base_out[...] = znew[...] - gamma * (field + beta * step[...]) + (rz2 / rz1) * direction
    gamma_out[...] = jnp.broadcast_to(gamma, gamma_out.shape)


def finish(o0, o1, o2, o3, a0, a1, a2, a3, base, gamma, mult, vectors, mult_hbm, direction_hbm, out, sems):
    n_load = base.shape[0]
    first = pltpu.make_async_copy(mult, mult_hbm, sems.at[0])
    first.start()
    jumped = jump([o0, o1, o2, o3], [a0, a1, a2, a3], n_load, vectors[2:3, :])
    out[...] = base[...] - gamma[:, :1] * jumped
    second = pltpu.make_async_copy(out, direction_hbm, sems.at[1])
    second.start()
    first.wait()
    second.wait()


def call(name, kernel, args, outs, scratch=(), in_place=(), out_place=(), limit=None):
    shapes = [jax.ShapeDtypeStruct(s, d) for s, d in outs]
    n_bytes = sum(a.size * a.dtype.itemsize for a in args) + sum(s.size * s.dtype.itemsize for s in shapes)
    return pl.pallas_call(
        kernel,
        out_shape=shapes,
        in_specs=[pl.BlockSpec(memory_space=pl.ANY if i in in_place else pltpu.VMEM) for i in range(len(args))],
        out_specs=[pl.BlockSpec(memory_space=pl.ANY if i in out_place else pltpu.VMEM) for i in range(len(outs))],
        scratch_shapes=scratch,
        cost_estimate=pl.CostEstimate(flops=40_000_000, bytes_accessed=n_bytes, transcendentals=0),
        compiler_params=pltpu.CompilerParams(vmem_limit_bytes=limit or (12 << 20) + 2 * n_bytes),
        name=name,
    )(*args)


def behind(block, other):
    return pl.pallas_call(
        lambda block_ref, other_ref, out_ref: None,
        out_shape=jax.ShapeDtypeStruct(block.shape, block.dtype),
        in_specs=[pl.BlockSpec(memory_space=pl.ANY)] * 2,
        out_specs=pl.BlockSpec(memory_space=pl.ANY),
        input_output_aliases={0: 0},
        compiler_params=pltpu.CompilerParams(vmem_limit_bytes=1 << 20),
        name="behind",
    )(block, other)


def swap(block, axis, distance):
    count = lax.axis_size(axis)
    return lax.ppermute(block, axis, [(i, i ^ distance) for i in range(count) if i ^ distance < count])


def exchange(wins):
    return [swap(win, "grp", 1) if f == 3 else swap(win, "sub", 1 << f) for f, win in zip(FACES, wins)]


def send_pair(rows):
    subs = lax.axis_size("sub")
    devices = 2 * subs
    blocks = rows.reshape(devices, 4, rows.shape[1])
    teams = [list(range(low, low + devices)) for low in range(0, lax.axis_size("grp") * subs, devices)]
    return lax.all_to_all(blocks, ("grp", "sub"), 0, 0, tiled=True, axis_index_groups=teams).reshape(rows.shape)


def send_all(rows):
    devices = lax.axis_size("grp") * lax.axis_size("sub")
    blocks = rows.reshape(devices, 4, rows.shape[1])
    return lax.all_to_all(blocks, ("grp", "sub"), 0, 0, tiled=True).reshape(rows.shape)


def body(loads, stiffness, flexibility, coarse_inverse, face_nodes, corner_index):
    rhs, stiff, flex, inverse = loads[0, 0], stiffness[0, 0], flexibility[0, 0], coarse_inverse[0]
    nodes, ids = face_nodes[0, 0], corner_index[0, 0]
    n_load, dofs = rhs.shape
    groups, subs = lax.axis_size("grp"), lax.axis_size("sub")
    n = 16 * subs
    field = ((n_load, dofs), F32)
    sent = ((groups * subs * 4, 4 * n_load), F32)
    total = ((8, 4 * n_load), F32)
    n_tile = n * n // LANES

    def faces(rows, more=0, last=0, first=0):
        return [((size(rows) + more + last * (i == LAST) + first * (i == 0), LANES), F32) for i in range(4)]

    order = inverse.shape[0]
    wide = -(-order // LANES) * LANES
    few = ids.shape[0]
    small = jnp.pad(inverse, ((0, 8), (0, wide - order)))
    small = small + jnp.pad(nodes[None], ((order, 7), (0, wide - 4))).astype(F32)
    small = small + jnp.pad(ids[None], ((order, 7), (4, wide - 4 - few))).astype(F32)
    block = [pltpu.VMEM(sent[0], F32), pltpu.SemaphoreType.DMA]
    corners, vectors, corner, resid, spread, inverse, low, *own = call(
        "start", functools.partial(start, ids.shape[0]), [rhs, stiff, small],
        [((2 * subs * 4, 4 * n_load), F32), ((8, dofs), F32), ((16, dofs), BF16), field, ((64, n), F32), ((n_tile, LANES), F32), field]
        + faces(n_load, 8, 16 * n // LANES, EXTRA),
        [pltpu.VMEM(rhs.shape, F32), pltpu.VMEM(stiff.shape, BF16), pltpu.VMEM((2 * subs * 4, 4 * n_load), F32),
         pltpu.SemaphoreType.DMA((3,))],
        [0, 1], [0], START_LIMIT << 10,
    )
    received = send_pair(corners)
    came = exchange(own)
    inverse = behind(inverse, came[-1])
    other = swap(inverse, "grp", 1)
    zold, corner_map, spread, *own = call(
        "image1", first_image, [received] + own + came + [vectors, corner, spread, low, flex],
        [field, ((80, dofs), BF16), ((80, n), F32)] + faces(2 * n_load),
    )
    (sums,) = call("sums1", first_sums, own + [zold, resid, vectors], [total])
    came = exchange(own)
    flexed, low, inverse, sent_rows, *own = call(
        "local2", second_local, own + came + [sums, vectors, corner_map, inverse, other, stiff],
        [field, ((n_load, dofs), BF16), ((2 * n_tile, LANES), F32), sent] + faces(n_load),
        block, out_place=[3],
    )
    received = send_all(sent_rows)
    came = exchange(own)
    before, coarse = call("coarse2", second_coarse, [received, corner_map, spread], [total, field])
    znew, step, *own = call(
        "image2", second_image, [before, coarse] + own + came + [zold, low, vectors, flex],
        [field, field] + faces(n_load),
    )
    (sums,) = call("sums2", second_sums, [before] + own + [znew, flexed, resid, vectors], [total])
    came = exchange(own)
    inverses = [inverse]
    distance = 2
    while distance < groups:
        held = inverses[0] if distance == 2 else jnp.concatenate(inverses, axis=0)
        inverses.append(swap(behind(held, came[-1]), "grp", distance))
        distance *= 2
    sent_rows, *own = call(
        "local3", third_local, own + came + [sums, vectors, corner_map, stiff], [sent] + faces(n_load),
        block, out_place=[0],
    )
    received = send_all(sent_rows)
    came = exchange(own)
    mult, base, gamma = call(
        "coarse3", third_coarse, [received, before, zold, znew, step, corner_map, spread] + inverses,
        [field, field, ((n_load, LANES), F32)],
    )
    mult, direction = call(
        "finish", finish, own + came + [base, gamma, mult, vectors], [field, field],
        [pltpu.VMEM(rhs.shape, F32), pltpu.SemaphoreType.DMA((2,))], out_place=[0, 1],
    )
    return (mult[None, None], direction[None, None])


def solution(mesh):
    in_specs = (
        P("grp", "sub", None, None),
        P("grp", "sub", None, None),
        P("grp", "sub", None, None),
        P("grp", None, None),
        P("grp", "sub", None),
        P("grp", "sub", None),
    )
    out_specs = (P("grp", "sub", None, None), P("grp", "sub", None, None))
    return jax.shard_map(body, mesh=mesh, in_specs=in_specs, out_specs=out_specs, check_vma=False)
```

```python
import functools

import jax
import jax.numpy as jnp
from jax import lax
from jax.experimental import pallas as pl
from jax.experimental.pallas import tpu as pltpu
from jax.sharding import PartitionSpec as P

F32, BF16 = jnp.float32, jnp.bfloat16
NT = (((1,), (1,)), ((), ()))
NN = (((1,), (0,)), ((), ()))
LANES = 128
EXTRA = 72
START_LIMIT = 54600


def exact(a, b, dims=NN):
    return lax.dot_general(a, b, dims, precision=lax.Precision.HIGHEST, preferred_element_type=F32)


def rounded(a, b):
    return lax.dot_general(a, b, NN, preferred_element_type=F32)


def thirds(x):
    high = x.astype(BF16)
    rest = x - high.astype(F32)
    mid = rest.astype(BF16)
    return jnp.concatenate([high, mid, (rest - mid.astype(F32)).astype(BF16)], axis=0)


def by_map(x, corner_map, dims):
    n = x.shape[0]
    out = lax.dot_general(thirds(x), corner_map, dims, preferred_element_type=F32)
    return out[:n] + out[n : 2 * n] + out[2 * n :]


def iota(shape, axis):
    return lax.broadcasted_iota(jnp.int32, shape, axis)


FACES = (2, 1, 3, 0)
LAST = FACES.index(3)


def pick_lane(row, lane):
    return jnp.sum(jnp.where(iota(row.shape, 1) == lane, row, 0.0), axis=1, keepdims=True)


def face_vectors(info, dofs):
    width = dofs // 4
    pos = iota((1, dofs), 1)
    sub_pos, grp_pos = lax.axis_index("sub"), lax.axis_index("grp")
    bits = [sub_pos & 1, (sub_pos >> 1) & 1, (sub_pos >> 2) & 1, grp_pos & 1]
    sign = jnp.zeros((1, dofs), F32)
    live = jnp.zeros((1, dofs), jnp.int32)
    node = pos
    for f in range(4):
        inside = (pos >= f * width) & (pos < (f + 1) * width)
        sign = jnp.where(inside, (1 - 2 * bits[f]).astype(F32), sign)
        live = jnp.where(inside, pick_lane(info, f).astype(jnp.int32), live)
    for step in range(1, 12):
        node = jnp.where(pos >= step * (width // 3), pos - step * (width // 3), node)
    mask = jnp.where(node < live, 1.0, 0.0)
    return sign, mask


def corner_ids(info, corners):
    row = iota((16, 1), 0)
    ids = jnp.sum(jnp.where(iota((16, info.shape[1]), 1) == 4 + row % 4 * 4 + row // 4, info, 0.0), axis=1, keepdims=True)
    return jnp.where(row % 4 * 4 < corners, ids, -1.0)


def corner_rows(ids, dofs):
    return jnp.where(ids == iota((16, dofs), 1), 1.0, 0.0)


def size(n_row):
    return n_row + n_row // 2


def put_faces(refs, field):
    n, dofs = field.shape
    width = dofs // 4
    for f, ref in zip(FACES, refs):
        low = f * width
        start = low if low % LANES == 0 else low + LANES // 2
        half = field[:, low + LANES : low + 2 * LANES] if low % LANES == 0 else field[:, start - LANES : start]
        top, bottom = half[: n // 2], half[n // 2 :]
        if low % LANES == 0:
            bottom = pltpu.roll(bottom, LANES // 2, 1)
        else:
            top = pltpu.roll(top, LANES // 2, 1)
        ref[:n, :] = field[:, start : start + LANES]
        ref[n : size(n), :] = jnp.where(iota(top.shape, 1) < LANES // 2, top, bottom)


def from_faces(faces, n):
    by_face = [face for _, face in sorted(zip(FACES, faces), key=lambda item: item[0])]
    tiles = []
    for even, odd in (by_face[:2], by_face[2:]):
        first, second = even[n:], odd[n:]
        left = iota(first.shape, 1) < LANES // 2
        top = jnp.where(left, first, pltpu.roll(second, LANES // 2, 1))
        bottom = jnp.where(left, pltpu.roll(first, LANES // 2, 1), second)
        tiles += [even[:n], jnp.concatenate([top, bottom], axis=0), odd[:n]]
    return jnp.concatenate(tiles, axis=1)


def jump(own, came, n, sign_mask):
    return from_faces([a[: size(n), :] - b[: size(n), :] for a, b in zip(own, came)], n) * sign_mask


def same_block(n_row, n_col, row_block, col_block):
    return iota((n_row, n_col), 0) // row_block == iota((n_row, n_col), 1) // col_block


def to_column(row):
    n = row.shape[1]
    return jnp.sum(jnp.where(same_block(n, n, 1, 1), row, 0.0), axis=1, keepdims=True)


def to_row(column):
    n = column.shape[0]
    return jnp.sum(jnp.where(same_block(n, n, 1, 1), column, 0.0), axis=0, keepdims=True)


def total_of(received):
    total = received[0:8]
    for low in range(8, received.shape[0], 8):
        total = total + received[low : low + 8]
    return total + pltpu.roll(total, 4, 0)


def sums_of(total, n_load):
    column = to_column(total[3:4])
    return [column[i * n_load : (i + 1) * n_load] for i in range(4)]


def halves(x):
    high = x.astype(BF16)
    return jnp.concatenate([high, (x - high.astype(F32)).astype(BF16)], axis=0)


def fine(x, matrix):
    n = x.shape[0]
    both = rounded(halves(x), matrix)
    return both[:n] + both[n:]


def finer(x, matrix):
    n = x.shape[0]
    high = matrix.astype(BF16)
    low = (matrix - high.astype(F32)).astype(BF16)
    parts = halves(x)
    both = lax.dot_general(parts, high, NT, preferred_element_type=F32)
    return both[:n] + both[n:] + lax.dot_general(parts[:n], low, NT, preferred_element_type=F32)


def packed_corners(scaled, corner):
    n_load = scaled.shape[0]
    values = by_map(scaled, corner, NT)
    flipped = jnp.concatenate([values] * 4, axis=0).T
    flipped = jnp.where(same_block(16, 4 * n_load, 4, n_load), flipped, 0.0)
    block = flipped[:8] + flipped[8:]
    return block + pltpu.roll(block, 4, 0)


def with_sums(block, sums):
    zero = jnp.zeros_like(sums[0])
    row = to_row(jnp.concatenate(sums + [zero] * (4 - len(sums)), axis=0))
    return jnp.where(iota(block.shape, 0) % 4 == 3, row, block)


def put_all(out, block):
    for low in range(0, out.shape[0], 8):
        out[low : low + 8, :] = block


def group_corners(received, which, rows, n_load):
    block = received[pl.ds(pl.multiple_of(which * rows, 8), rows), :]
    block = jnp.where(iota(block.shape, 0) % 4 == 3, 0.0, block)
    tall = jnp.concatenate([block] * 4, axis=0)
    flipped = jnp.where(same_block(4 * rows, 4 * n_load, rows, n_load), tall, 0.0).T
    return sum(flipped[r * n_load : (r + 1) * n_load] for r in range(1, 4)) + flipped[:n_load]


def coarse_of(inner, outer, spread):
    n = inner.shape[0]
    both = finer(jnp.concatenate([inner, outer], axis=0), spread)
    return jnp.where(iota((n, both.shape[1]), 1) < 64, both[:n], both[n:])


def two_groups(received, rows, n_load):
    grp_pos = lax.axis_index("grp")
    if received.shape[0] == 2 * rows:
        grp_pos = grp_pos & 1
    return [group_corners(received, which, rows, n_load) for which in (grp_pos, grp_pos ^ 1)]


def to_tiles(matrix):
    return jnp.concatenate([matrix[:, low : low + LANES] for low in range(0, matrix.shape[1], LANES)], axis=0)


def from_tiles(rows, n):
    n_row = rows.shape[0] * LANES // n
    return jnp.concatenate([rows[low : low + n_row] for low in range(0, rows.shape[0], n_row)], axis=1)


def rows_sum(x):
    return jnp.sum(x, axis=1, keepdims=True)


def start(
    corners, rhs_hbm, stiff_hbm, small,
    sent, vectors, corner_out, resid_out, spread_out, coarse_out, low_out, w0, w1, w2, w3,
    rhs, stiff, block, sems,
):
    pairs = [(rhs_hbm, rhs), (stiff_hbm, stiff), (block, sent)]
    copies = [pltpu.make_async_copy(a, b, sems.at[i]) for i, (a, b) in enumerate(pairs)]
    for copy in copies[:2]:
        copy.start()
    n_load, dofs = rhs.shape
    wins = [w0, w1, w2, w3]
    n = small.shape[0] - 8
    info = small[n : n + 1, :LANES]
    sign, mask = face_vectors(info, dofs)
    vectors[0:1, :] = sign
    vectors[1:2, :] = mask
    vectors[2:3, :] = sign * mask
    vectors[3:8, :] = jnp.zeros((5, dofs), F32)
    ids = corner_ids(info, corners)
    corner = corner_rows(ids.astype(jnp.int32), dofs).astype(BF16)
    corner_out[...] = corner
    ids = jnp.sum(jnp.where(same_block(16, LANES, 1, 1), ids, 0.0), axis=0, keepdims=True)
    for ref in wins:
        ref[size(n_load) : size(n_load) + 8, :] = jnp.broadcast_to(ids, (8, LANES))
    copies[0].wait()
    resid = rhs[...] * mask
    resid_out[...] = resid
    scaled = 0.5 * sign * resid
    put_all(block, packed_corners(scaled, corner))
    copies[2].start()
    wide = small.shape[1]
    subs = n // corners
    sub_pos = lax.axis_index("sub")
    row = iota((64, 1), 0)
    owner = jnp.where(row < 16, sub_pos, jnp.where(row < 32, sub_pos ^ 1, jnp.where(row < 48, sub_pos ^ 2, sub_pos ^ 4)))
    source = owner * corners + row % 4 * 4 + row // 4 % 4
    pick = jnp.where((source == iota((64, n), 1)) & (row % 4 * 4 < corners), 1.0, 0.0)
    place = iota((16 * subs, 1), 0)
    source = place // 4 % subs * corners + place % 4 * 4 + place // (4 * subs)
    order = jnp.where((source == iota((16 * subs, wide), 1)) & (place % 4 * 4 < corners), 1.0, 0.0).astype(BF16)
    pick = jnp.concatenate([pick, order[:, :n].astype(F32)], axis=0).astype(BF16)
    parts = thirds(small[:n, :])
    picked = rounded(pick, parts[:n]) + rounded(pick, parts[n : 2 * n]) + rounded(pick, parts[2 * n :])
    both = by_map(picked, order, NT)
    spread_out[...] = both[:64]
    coarse_out[...] = to_tiles(both[64:])
    wins[LAST][size(n_load) + 8 :, :] = to_tiles(both[:16])
    wins[0][size(n_load) + 8 :, :] = jnp.zeros((EXTRA, LANES), F32)
    copies[1].wait()
    local = rounded(halves(scaled), stiff[...])
    put_faces(wins, local[:n_load])
    low_out[...] = local[n_load:]
    copies[2].wait()


def first_image(
    received, o0, o1, o2, o3, a0, a1, a2, a3, vectors, corner, spread, low, flex,
    z_out, map_out, spread_out, *wins,
):
    n_load, dofs = low.shape
    came = [a0, a1, a2, a3]
    sign, sign_mask = vectors[0:1, :], vectors[2:3, :]
    width = dofs // 4
    pos = iota((1, dofs), 1)
    pieces = [corner[...].astype(F32) * sign_mask]
    for f in range(4):
        ids = to_column(came[FACES.index(f)][size(n_load) : size(n_load) + 1, :])[:16].astype(jnp.int32)
        inside = (pos >= f * width) & (pos < (f + 1) * width)
        pieces.append(corner_rows(ids, dofs) * jnp.where(inside, -sign_mask, 0.0))
    corner_map = jnp.concatenate(pieces, axis=0).astype(BF16)
    map_out[...] = corner_map
    n = spread.shape[1]
    cross = from_tiles(came[LAST][size(n_load) + 8 :, :], n)
    spread_rows = jnp.concatenate([spread[...], cross], axis=0)
    spread_out[...] = spread_rows
    coarse = coarse_of(*two_groups(received, n // 4, n_load), spread_rows)
    zvec = jump([o0, o1, o2, o3], came, n_load, sign_mask) + by_map(coarse, corner_map, NN)
    z_out[...] = zvec
    signed = sign * zvec
    image = rounded(signed.astype(BF16), flex[...])
    put_faces(wins, jnp.concatenate([image, low[...]], axis=0))


def first_sums(o0, o1, o2, o3, zvec, resid, vectors, out):
    n_load = zvec.shape[0]
    image = from_faces([o0[...], o1[...], o2[...], o3[...]], 2 * n_load)[:n_load]
    sums = [rows_sum(resid[...] * zvec[...]), 2.0 * rows_sum(vectors[0:1, :] * zvec[...] * image)]
    out[...] = with_sums(jnp.zeros((8, 4 * n_load), F32), sums)


def second_local(
    o0, o1, o2, o3, a0, a1, a2, a3, sums, vectors, corner_map, inverse, other, stiff,
    flexed_out, low_out, inverse_out, sent, w0, w1, w2, w3, block, sem,
):
    n_load, dofs = flexed_out.shape
    sign, sign_mask = vectors[0:1, :], vectors[2:3, :]
    jumped = jump([o0, o1, o2, o3], [a0, a1, a2, a3], 2 * n_load, sign_mask)
    flexed = jumped[:n_load]
    flexed_out[...] = flexed
    inverse_out[: inverse.shape[0], :] = inverse[...]
    inverse_out[inverse.shape[0] :, :] = other[...]
    low_out[...] = jumped[n_load:].astype(BF16)
    scaled = 0.5 * sign * flexed
    is_sum = iota((8, 1), 0) % 4 == 3
    corners = packed_corners(scaled, abs(corner_map[:16, :]))
    put_all(block, jnp.where(is_sum, sums[...], corners))
    copy = pltpu.make_async_copy(block, sent, sem)
    copy.start()
    put_faces([w0, w1, w2, w3], fine(scaled, stiff[...]))
    copy.wait()


def second_coarse(received, corner_map, spread, total_out, field_out):
    n_load = field_out.shape[0]
    total_out[...] = total_of(received)
    coarse = coarse_of(*two_groups(received, spread.shape[1] // 4, n_load), spread[...])
    field_out[...] = by_map(coarse, corner_map[...], NN)


def second_image(
    total, field, o0, o1, o2, o3, a0, a1, a2, a3, zold, low, vectors, flex, z_out, step_out, *wins,
):
    n_load, dofs = zold.shape
    sign, sign_mask = vectors[0:1, :], vectors[2:3, :]
    rz, curve, _, _ = sums_of(total[...], n_load)
    alpha = rz / curve
    step = jump([o0, o1, o2, o3], [a0, a1, a2, a3], n_load, sign_mask) + field[...]
    step = alpha * step
    step_out[...] = step
    zvec = zold[...] + low[...].astype(F32) - step
    z_out[...] = zvec
    signed = sign * zvec
    image = alpha * fine(signed, flex[...])
    put_faces(wins, image)


def second_sums(total, o0, o1, o2, o3, zvec, flexed, resid, vectors, out):
    n_load = zvec.shape[0]
    rz, curve, _, _ = sums_of(total[...], n_load)
    scaled_flexed = rz / curve * flexed[...]
    image = from_faces([o0[...], o1[...], o2[...], o3[...]], n_load)
    sums = [
        rows_sum((resid[...] - scaled_flexed) * zvec[...]),
        2.0 * rows_sum(vectors[0:1, :] * zvec[...] * image),
        rows_sum(zvec[...] * scaled_flexed),
    ]
    out[...] = with_sums(jnp.zeros((8, 4 * n_load), F32), sums)


def third_local(o0, o1, o2, o3, a0, a1, a2, a3, sums, vectors, corner_map, stiff, sent, w0, w1, w2, w3, block, sem):
    n_load, dofs = o0.shape[0] * 2 // 3, vectors.shape[1]
    sign, sign_mask = vectors[0:1, :], vectors[2:3, :]
    flexed = jump([o0, o1, o2, o3], [a0, a1, a2, a3], n_load, sign_mask)
    scaled = 0.5 * sign * flexed
    local = fine(scaled, stiff[...])
    fourth = jnp.where(iota((1, 4 * n_load), 1) // n_load == 3, 1.0, 0.0)
    square = with_sums(jnp.zeros((8, 4 * n_load), F32), [4.0 * rows_sum(scaled * local)] * 4) * fourth
    is_sum = iota((8, 1), 0) % 4 == 3
    put_all(block, jnp.where(is_sum, sums[...] + square, packed_corners(scaled, abs(corner_map[:16, :]))))
    copy = pltpu.make_async_copy(block, sent, sem)
    copy.start()
    put_faces([w0, w1, w2, w3], local)
    copy.wait()


def third_coarse(received, before, zold, znew, step, corner_map, spread, *rest):
    inverses, (mult_out, base_out, gamma_out) = rest[:-3], rest[-3:]
    n_load = zold.shape[0]
    rz0, curve0, _, _ = sums_of(before[...], n_load)
    rz1, curve, mixed, square = sums_of(total_of(received), n_load)
    alpha = rz0 / curve0
    beta = rz1 / rz0
    gamma = rz1 / (curve + 2.0 * beta * mixed + beta * beta * rz0)
    direction = znew[...] + beta * zold[...]
    mult_out[...] = alpha * (zold[...] + gamma * direction)
    n = spread.shape[1]
    height = n * n // LANES
    corners = two_groups(received, n // 4, n_load)
    index = 0
    for ref in inverses:
        for low in range(0, ref.shape[0], height):
            if index == len(corners):
                corners.append(group_corners(received, lax.axis_index("grp") ^ index, n // 4, n_load))
            values = corners[index]
            square = square + 4.0 * rows_sum(values * finer(values, from_tiles(ref[low : low + height, :], n)))
            index += 1
    rz2 = square + 2.0 * beta * (mixed - curve) + beta * beta * (rz0 - mixed)
    rz2 = rz1 - 2.0 * gamma * (curve + beta * mixed) + gamma * gamma * rz2
    field = by_map(coarse_of(*corners[:2], spread[...]), corner_map[...], NN)
    base_out[...] = znew[...] - gamma * (field + beta * step[...]) + (rz2 / rz1) * direction
    gamma_out[...] = jnp.broadcast_to(gamma, gamma_out.shape)


def finish(o0, o1, o2, o3, a0, a1, a2, a3, base, gamma, mult, vectors, mult_hbm, direction_hbm, out, sems):
    n_load = base.shape[0]
    first = pltpu.make_async_copy(mult, mult_hbm, sems.at[0])
    first.start()
    jumped = jump([o0, o1, o2, o3], [a0, a1, a2, a3], n_load, vectors[2:3, :])
    out[...] = base[...] - gamma[:, :1] * jumped
    second = pltpu.make_async_copy(out, direction_hbm, sems.at[1])
    second.start()
    first.wait()
    second.wait()


def call(name, kernel, args, outs, scratch=(), in_place=(), out_place=(), limit=None):
    shapes = [jax.ShapeDtypeStruct(s, d) for s, d in outs]
    n_bytes = sum(a.size * a.dtype.itemsize for a in args) + sum(s.size * s.dtype.itemsize for s in shapes)
    return pl.pallas_call(
        kernel,
        out_shape=shapes,
        in_specs=[pl.BlockSpec(memory_space=pl.ANY if i in in_place else pltpu.VMEM) for i in range(len(args))],
        out_specs=[pl.BlockSpec(memory_space=pl.ANY if i in out_place else pltpu.VMEM) for i in range(len(outs))],
        scratch_shapes=scratch,
        cost_estimate=pl.CostEstimate(flops=40_000_000, bytes_accessed=n_bytes, transcendentals=0),
        compiler_params=pltpu.CompilerParams(vmem_limit_bytes=limit or (12 << 20) + 2 * n_bytes),
        name=name,
    )(*args)


def behind(block, other):
    return pl.pallas_call(
        lambda block_ref, other_ref, out_ref: None,
        out_shape=jax.ShapeDtypeStruct(block.shape, block.dtype),
        in_specs=[pl.BlockSpec(memory_space=pl.ANY)] * 2,
        out_specs=pl.BlockSpec(memory_space=pl.ANY),
        input_output_aliases={0: 0},
        compiler_params=pltpu.CompilerParams(vmem_limit_bytes=1 << 20),
        name="behind",
    )(block, other)


def swap(block, axis, distance):
    count = lax.axis_size(axis)
    return lax.ppermute(block, axis, [(i, i ^ distance) for i in range(count) if i ^ distance < count])


def exchange(wins):
    return [swap(win, "grp", 1) if f == 3 else swap(win, "sub", 1 << f) for f, win in zip(FACES, wins)]


def send_pair(rows):
    subs = lax.axis_size("sub")
    devices = 2 * subs
    blocks = rows.reshape(devices, 4, rows.shape[1])
    teams = [list(range(low, low + devices)) for low in range(0, lax.axis_size("grp") * subs, devices)]
    return lax.all_to_all(blocks, ("grp", "sub"), 0, 0, tiled=True, axis_index_groups=teams).reshape(rows.shape)


def send_all(rows):
    devices = lax.axis_size("grp") * lax.axis_size("sub")
    blocks = rows.reshape(devices, 4, rows.shape[1])
    return lax.all_to_all(blocks, ("grp", "sub"), 0, 0, tiled=True).reshape(rows.shape)


def body(loads, stiffness, flexibility, coarse_inverse, face_nodes, corner_index):
    rhs, stiff, flex, inverse = loads[0, 0], stiffness[0, 0], flexibility[0, 0], coarse_inverse[0]
    nodes, ids = face_nodes[0, 0], corner_index[0, 0]
    n_load, dofs = rhs.shape
    groups, subs = lax.axis_size("grp"), lax.axis_size("sub")
    n = 16 * subs
    field = ((n_load, dofs), F32)
    sent = ((groups * subs * 4, 4 * n_load), F32)
    total = ((8, 4 * n_load), F32)
    n_tile = n * n // LANES

    def faces(rows, more=0, last=0, first=0):
        return [((size(rows) + more + last * (i == LAST) + first * (i == 0), LANES), F32) for i in range(4)]

    order = inverse.shape[0]
    wide = -(-order // LANES) * LANES
    few = ids.shape[0]
    small = jnp.pad(inverse, ((0, 8), (0, wide - order)))
    small = small + jnp.pad(nodes[None], ((order, 7), (0, wide - 4))).astype(F32)
    small = small + jnp.pad(ids[None], ((order, 7), (4, wide - 4 - few))).astype(F32)
    block = [pltpu.VMEM(sent[0], F32), pltpu.SemaphoreType.DMA]
    corners, vectors, corner, resid, spread, inverse, low, *own = call(
        "start", functools.partial(start, ids.shape[0]), [rhs, stiff, small],
        [((2 * subs * 4, 4 * n_load), F32), ((8, dofs), F32), ((16, dofs), BF16), field, ((64, n), F32), ((n_tile, LANES), F32), field]
        + faces(n_load, 8, 16 * n // LANES, EXTRA),
        [pltpu.VMEM(rhs.shape, F32), pltpu.VMEM(stiff.shape, BF16), pltpu.VMEM((2 * subs * 4, 4 * n_load), F32),
         pltpu.SemaphoreType.DMA((3,))],
        [0, 1], [0], START_LIMIT << 10,
    )
    received = send_pair(corners)
    came = exchange(own)
    inverse = inverse
    other = swap(inverse, "grp", 1)
    zold, corner_map, spread, *own = call(
        "image1", first_image, [received] + own + came + [vectors, corner, spread, low, flex],
        [field, ((80, dofs), BF16), ((80, n), F32)] + faces(2 * n_load),
    )
    (sums,) = call("sums1", first_sums, own + [zold, resid, vectors], [total])
    came = exchange(own)
    flexed, low, inverse, sent_rows, *own = call(
        "local2", second_local, own + came + [sums, vectors, corner_map, inverse, other, stiff],
        [field, ((n_load, dofs), BF16), ((2 * n_tile, LANES), F32), sent] + faces(n_load),
        block, out_place=[3],
    )
    received = send_all(sent_rows)
    came = exchange(own)
    before, coarse = call("coarse2", second_coarse, [received, corner_map, spread], [total, field])
    znew, step, *own = call(
        "image2", second_image, [before, coarse] + own + came + [zold, low, vectors, flex],
        [field, field] + faces(n_load),
    )
    (sums,) = call("sums2", second_sums, [before] + own + [znew, flexed, resid, vectors], [total])
    came = exchange(own)
    inverses = [inverse]
    distance = 2
    while distance < groups:
        held = inverses[0] if distance == 2 else jnp.concatenate(inverses, axis=0)
        inverses.append(swap(held, "grp", distance))
        distance *= 2
    sent_rows, *own = call(
        "local3", third_local, own + came + [sums, vectors, corner_map, stiff], [sent] + faces(n_load),
        block, out_place=[0],
    )
    received = send_all(sent_rows)
    came = exchange(own)
    mult, base, gamma = call(
        "coarse3", third_coarse, [received, before, zold, znew, step, corner_map, spread] + inverses,
        [field, field, ((n_load, LANES), F32)],
    )
    mult, direction = call(
        "finish", finish, own + came + [base, gamma, mult, vectors], [field, field],
        [pltpu.VMEM(rhs.shape, F32), pltpu.SemaphoreType.DMA((2,))], out_place=[0, 1],
    )
    return (mult[None, None], direction[None, None])


def solution(mesh):
    in_specs = (
        P("grp", "sub", None, None),
        P("grp", "sub", None, None),
        P("grp", "sub", None, None),
        P("grp", None, None),
        P("grp", "sub", None),
        P("grp", "sub", None),
    )
    out_specs = (P("grp", "sub", None, None), P("grp", "sub", None, None))
    return jax.shard_map(body, mesh=mesh, in_specs=in_specs, out_specs=out_specs, check_vma=False)
```

```python
import functools

import jax
import jax.numpy as jnp
from jax import lax
from jax.experimental import pallas as pl
from jax.experimental.pallas import tpu as pltpu
from jax.sharding import PartitionSpec as P

F32, BF16 = jnp.float32, jnp.bfloat16
NT = (((1,), (1,)), ((), ()))
NN = (((1,), (0,)), ((), ()))
LANES = 128
EXTRA = 72
START_LIMIT = 54600


def exact(a, b, dims=NN):
    return lax.dot_general(a, b, dims, precision=lax.Precision.HIGHEST, preferred_element_type=F32)


def rounded(a, b):
    return lax.dot_general(a, b, NN, preferred_element_type=F32)


def thirds(x):
    high = x.astype(BF16)
    rest = x - high.astype(F32)
    mid = rest.astype(BF16)
    return jnp.concatenate([high, mid, (rest - mid.astype(F32)).astype(BF16)], axis=0)


def by_map(x, corner_map, dims):
    n = x.shape[0]
    out = lax.dot_general(thirds(x), corner_map, dims, preferred_element_type=F32)
    return out[:n] + out[n : 2 * n] + out[2 * n :]


def iota(shape, axis):
    return lax.broadcasted_iota(jnp.int32, shape, axis)


FACES = (2, 1, 3, 0)
LAST = FACES.index(3)


def pick_lane(row, lane):
    return jnp.sum(jnp.where(iota(row.shape, 1) == lane, row, 0.0), axis=1, keepdims=True)


def face_vectors(info, dofs):
    width = dofs // 4
    pos = iota((1, dofs), 1)
    sub_pos, grp_pos = lax.axis_index("sub"), lax.axis_index("grp")
    bits = [sub_pos & 1, (sub_pos >> 1) & 1, (sub_pos >> 2) & 1, grp_pos & 1]
    sign = jnp.zeros((1, dofs), F32)
    live = jnp.zeros((1, dofs), jnp.int32)
    node = pos
    for f in range(4):
        inside = (pos >= f * width) & (pos < (f + 1) * width)
        sign = jnp.where(inside, (1 - 2 * bits[f]).astype(F32), sign)
        live = jnp.where(inside, pick_lane(info, f).astype(jnp.int32), live)
    for step in range(1, 12):
        node = jnp.where(pos >= step * (width // 3), pos - step * (width // 3), node)
    mask = jnp.where(node < live, 1.0, 0.0)
    return sign, mask


def corner_ids(info, corners):
    row = iota((16, 1), 0)
    ids = jnp.sum(jnp.where(iota((16, info.shape[1]), 1) == 4 + row % 4 * 4 + row // 4, info, 0.0), axis=1, keepdims=True)
    return jnp.where(row % 4 * 4 < corners, ids, -1.0)


def corner_rows(ids, dofs):
    return jnp.where(ids == iota((16, dofs), 1), 1.0, 0.0)


def size(n_row):
    return n_row + n_row // 2


def put_faces(refs, field):
    n, dofs = field.shape
    width = dofs // 4
    for f, ref in zip(FACES, refs):
        low = f * width
        start = low if low % LANES == 0 else low + LANES // 2
        half = field[:, low + LANES : low + 2 * LANES] if low % LANES == 0 else field[:, start - LANES : start]
        top, bottom = half[: n // 2], half[n // 2 :]
        if low % LANES == 0:
            bottom = pltpu.roll(bottom, LANES // 2, 1)
        else:
            top = pltpu.roll(top, LANES // 2, 1)
        ref[:n, :] = field[:, start : start + LANES]
        ref[n : size(n), :] = jnp.where(iota(top.shape, 1) < LANES // 2, top, bottom)


def from_faces(faces, n):
    by_face = [face for _, face in sorted(zip(FACES, faces), key=lambda item: item[0])]
    tiles = []
    for even, odd in (by_face[:2], by_face[2:]):
        first, second = even[n:], odd[n:]
        left = iota(first.shape, 1) < LANES // 2
        top = jnp.where(left, first, pltpu.roll(second, LANES // 2, 1))
        bottom = jnp.where(left, pltpu.roll(first, LANES // 2, 1), second)
        tiles += [even[:n], jnp.concatenate([top, bottom], axis=0), odd[:n]]
    return jnp.concatenate(tiles, axis=1)


def jump(own, came, n, sign_mask):
    return from_faces([a[: size(n), :] - b[: size(n), :] for a, b in zip(own, came)], n) * sign_mask


def same_block(n_row, n_col, row_block, col_block):
    return iota((n_row, n_col), 0) // row_block == iota((n_row, n_col), 1) // col_block


def to_column(row):
    n = row.shape[1]
    return jnp.sum(jnp.where(same_block(n, n, 1, 1), row, 0.0), axis=1, keepdims=True)


def to_row(column):
    n = column.shape[0]
    return jnp.sum(jnp.where(same_block(n, n, 1, 1), column, 0.0), axis=0, keepdims=True)


def total_of(received):
    total = received[0:8]
    for low in range(8, received.shape[0], 8):
        total = total + received[low : low + 8]
    return total + pltpu.roll(total, 4, 0)


def sums_of(total, n_load):
    shape = (n_load, 4 * n_load)
    away = iota(shape, 1) - iota(shape, 0)
    return [rows_sum(jnp.where(away == i * n_load, total[3:4], 0.0)) for i in range(4)]


def halves(x):
    high = x.astype(BF16)
    return jnp.concatenate([high, (x - high.astype(F32)).astype(BF16)], axis=0)


def fine(x, matrix):
    n = x.shape[0]
    both = rounded(halves(x), matrix)
    return both[:n] + both[n:]


def finer(x, matrix):
    n = x.shape[0]
    high = matrix.astype(BF16)
    low = (matrix - high.astype(F32)).astype(BF16)
    parts = halves(x)
    both = lax.dot_general(parts, high, NT, preferred_element_type=F32)
    return both[:n] + both[n:] + lax.dot_general(parts[:n], low, NT, preferred_element_type=F32)


def packed_corners(scaled, corner):
    n_load = scaled.shape[0]
    values = by_map(scaled, corner, NT)
    flipped = jnp.concatenate([values] * 4, axis=0).T
    flipped = jnp.where(same_block(16, 4 * n_load, 4, n_load), flipped, 0.0)
    block = flipped[:8] + flipped[8:]
    return block + pltpu.roll(block, 4, 0)


def with_sums(block, sums, first=0):
    n_load = sums[0].shape[0]
    shape = (n_load, 4 * n_load)
    away = iota(shape, 1) - iota(shape, 0)
    spread = jnp.zeros(shape, F32)
    for i, one in enumerate(sums):
        spread = jnp.where(away == (first + i) * n_load, one, spread)
    return jnp.where(iota(block.shape, 0) % 4 == 3, jnp.sum(spread, axis=0, keepdims=True), block)


def put_all(out, block):
    for low in range(0, out.shape[0], 8):
        out[low : low + 8, :] = block


def group_corners(received, which, rows, n_load):
    block = received[pl.ds(pl.multiple_of(which * rows, 8), rows), :]
    block = jnp.where(iota(block.shape, 0) % 4 == 3, 0.0, block)
    tall = jnp.concatenate([block] * 4, axis=0)
    flipped = jnp.where(same_block(4 * rows, 4 * n_load, rows, n_load), tall, 0.0).T
    return sum(flipped[r * n_load : (r + 1) * n_load] for r in range(1, 4)) + flipped[:n_load]


def coarse_of(inner, outer, spread):
    n = inner.shape[0]
    both = finer(jnp.concatenate([inner, outer], axis=0), spread)
    return jnp.where(iota((n, both.shape[1]), 1) < 64, both[:n], both[n:])


def two_groups(received, rows, n_load):
    grp_pos = lax.axis_index("grp")
    if received.shape[0] == 2 * rows:
        grp_pos = grp_pos & 1
    return [group_corners(received, which, rows, n_load) for which in (grp_pos, grp_pos ^ 1)]


def to_tiles(matrix):
    return jnp.concatenate([matrix[:, low : low + LANES] for low in range(0, matrix.shape[1], LANES)], axis=0)


def from_tiles(rows, n):
    n_row = rows.shape[0] * LANES // n
    return jnp.concatenate([rows[low : low + n_row] for low in range(0, rows.shape[0], n_row)], axis=1)


def rows_sum(x):
    return jnp.sum(x, axis=1, keepdims=True)


def start(
    corners, rhs_hbm, stiff_hbm, small,
    sent, vectors, corner_out, resid_out, spread_out, coarse_out, low_out, w0, w1, w2, w3,
    rhs, stiff, block, sems,
):
    pairs = [(rhs_hbm, rhs), (stiff_hbm, stiff), (block, sent)]
    copies = [pltpu.make_async_copy(a, b, sems.at[i]) for i, (a, b) in enumerate(pairs)]
    for copy in copies[:2]:
        copy.start()
    n_load, dofs = rhs.shape
    wins = [w0, w1, w2, w3]
    n = small.shape[0] - 8
    info = small[n : n + 1, :LANES]
    sign, mask = face_vectors(info, dofs)
    vectors[0:1, :] = sign
    vectors[1:2, :] = mask
    vectors[2:3, :] = sign * mask
    vectors[3:8, :] = jnp.zeros((5, dofs), F32)
    ids = corner_ids(info, corners)
    corner = corner_rows(ids.astype(jnp.int32), dofs).astype(BF16)
    corner_out[...] = corner
    ids = jnp.sum(jnp.where(same_block(16, LANES, 1, 1), ids, 0.0), axis=0, keepdims=True)
    for ref in wins:
        ref[size(n_load) : size(n_load) + 8, :] = jnp.broadcast_to(ids, (8, LANES))
    copies[0].wait()
    resid = rhs[...] * mask
    resid_out[...] = resid
    scaled = 0.5 * sign * resid
    put_all(block, packed_corners(scaled, corner))
    copies[2].start()
    wide = small.shape[1]
    subs = n // corners
    sub_pos = lax.axis_index("sub")
    row = iota((64, 1), 0)
    owner = jnp.where(row < 16, sub_pos, jnp.where(row < 32, sub_pos ^ 1, jnp.where(row < 48, sub_pos ^ 2, sub_pos ^ 4)))
    source = owner * corners + row % 4 * 4 + row // 4 % 4
    pick = jnp.where((source == iota((64, n), 1)) & (row % 4 * 4 < corners), 1.0, 0.0)
    place = iota((16 * subs, 1), 0)
    source = place // 4 % subs * corners + place % 4 * 4 + place // (4 * subs)
    order = jnp.where((source == iota((16 * subs, wide), 1)) & (place % 4 * 4 < corners), 1.0, 0.0).astype(BF16)
    pick = jnp.concatenate([pick, order[:, :n].astype(F32)], axis=0).astype(BF16)
    parts = thirds(small[:n, :])
    picked = rounded(pick, parts[:n]) + rounded(pick, parts[n : 2 * n]) + rounded(pick, parts[2 * n :])
    both = by_map(picked, order, NT)
    spread_out[...] = both[:64]
    coarse_out[...] = to_tiles(both[64:])
    wins[LAST][size(n_load) + 8 :, :] = to_tiles(both[:16])
    wins[0][size(n_load) + 8 :, :] = jnp.zeros((EXTRA, LANES), F32)
    copies[1].wait()
    local = rounded(halves(scaled), stiff[...])
    put_faces(wins, local[:n_load])
    low_out[...] = local[n_load:]
    copies[2].wait()


def first_image(
    received, o0, o1, o2, o3, a0, a1, a2, a3, vectors, corner, spread, low, flex,
    z_out, map_out, spread_out, *wins,
):
    n_load, dofs = low.shape
    came = [a0, a1, a2, a3]
    sign, sign_mask = vectors[0:1, :], vectors[2:3, :]
    width = dofs // 4
    pos = iota((1, dofs), 1)
    pieces = [corner[...].astype(F32) * sign_mask]
    for f in range(4):
        ids = to_column(came[FACES.index(f)][size(n_load) : size(n_load) + 1, :])[:16].astype(jnp.int32)
        inside = (pos >= f * width) & (pos < (f + 1) * width)
        pieces.append(corner_rows(ids, dofs) * jnp.where(inside, -sign_mask, 0.0))
    corner_map = jnp.concatenate(pieces, axis=0).astype(BF16)
    map_out[...] = corner_map
    n = spread.shape[1]
    cross = from_tiles(came[LAST][size(n_load) + 8 :, :], n)
    spread_rows = jnp.concatenate([spread[...], cross], axis=0)
    spread_out[...] = spread_rows
    coarse = coarse_of(*two_groups(received, n // 4, n_load), spread_rows)
    zvec = jump([o0, o1, o2, o3], came, n_load, sign_mask) + by_map(coarse, corner_map, NN)
    z_out[...] = zvec
    signed = sign * zvec
    image = rounded(signed.astype(BF16), flex[...])
    put_faces(wins, jnp.concatenate([image, low[...]], axis=0))


def first_sums(o0, o1, o2, o3, zvec, resid, vectors, out):
    n_load = zvec.shape[0]
    image = from_faces([o0[...], o1[...], o2[...], o3[...]], 2 * n_load)[:n_load]
    sums = [rows_sum(resid[...] * zvec[...]), 2.0 * rows_sum(vectors[0:1, :] * zvec[...] * image)]
    out[...] = with_sums(jnp.zeros((8, 4 * n_load), F32), sums)


def second_local(
    o0, o1, o2, o3, a0, a1, a2, a3, sums, vectors, corner_map, inverse, other, stiff,
    flexed_out, low_out, inverse_out, sent, w0, w1, w2, w3, block, sem,
):
    n_load, dofs = flexed_out.shape
    sign, sign_mask = vectors[0:1, :], vectors[2:3, :]
    jumped = jump([o0, o1, o2, o3], [a0, a1, a2, a3], 2 * n_load, sign_mask)
    flexed = jumped[:n_load]
    flexed_out[...] = flexed
    inverse_out[: inverse.shape[0], :] = inverse[...]
    inverse_out[inverse.shape[0] :, :] = other[...]
    low_out[...] = jumped[n_load:].astype(BF16)
    scaled = 0.5 * sign * flexed
    is_sum = iota((8, 1), 0) % 4 == 3
    corners = packed_corners(scaled, abs(corner_map[:16, :]))
    put_all(block, jnp.where(is_sum, sums[...], corners))
    copy = pltpu.make_async_copy(block, sent, sem)
    copy.start()
    put_faces([w0, w1, w2, w3], fine(scaled, stiff[...]))
    copy.wait()


def second_coarse(received, corner_map, spread, total_out, field_out):
    n_load = field_out.shape[0]
    total_out[...] = total_of(received)
    coarse = coarse_of(*two_groups(received, spread.shape[1] // 4, n_load), spread[...])
    field_out[...] = by_map(coarse, corner_map[...], NN)


def second_image(
    total, field, o0, o1, o2, o3, a0, a1, a2, a3, zold, low, vectors, flex, z_out, step_out, *wins,
):
    n_load, dofs = zold.shape
    sign, sign_mask = vectors[0:1, :], vectors[2:3, :]
    rz, curve, _, _ = sums_of(total[...], n_load)
    alpha = rz / curve
    step = jump([o0, o1, o2, o3], [a0, a1, a2, a3], n_load, sign_mask) + field[...]
    step = alpha * step
    step_out[...] = step
    zvec = zold[...] + low[...].astype(F32) - step
    z_out[...] = zvec
    signed = sign * zvec
    image = alpha * fine(signed, flex[...])
    put_faces(wins, image)


def second_sums(total, o0, o1, o2, o3, zvec, flexed, resid, vectors, out):
    n_load = zvec.shape[0]
    rz, curve, _, _ = sums_of(total[...], n_load)
    scaled_flexed = rz / curve * flexed[...]
    image = from_faces([o0[...], o1[...], o2[...], o3[...]], n_load)
    sums = [
        rows_sum((resid[...] - scaled_flexed) * zvec[...]),
        2.0 * rows_sum(vectors[0:1, :] * zvec[...] * image),
        rows_sum(zvec[...] * scaled_flexed),
    ]
    out[...] = with_sums(jnp.zeros((8, 4 * n_load), F32), sums)


def third_local(o0, o1, o2, o3, a0, a1, a2, a3, sums, vectors, corner_map, stiff, sent, w0, w1, w2, w3, block, sem):
    n_load, dofs = o0.shape[0] * 2 // 3, vectors.shape[1]
    sign, sign_mask = vectors[0:1, :], vectors[2:3, :]
    flexed = jump([o0, o1, o2, o3], [a0, a1, a2, a3], n_load, sign_mask)
    scaled = 0.5 * sign * flexed
    local = fine(scaled, stiff[...])
    square = with_sums(jnp.zeros((8, 4 * n_load), F32), [4.0 * rows_sum(scaled * local)], 3)
    is_sum = iota((8, 1), 0) % 4 == 3
    put_all(block, jnp.where(is_sum, sums[...] + square, packed_corners(scaled, abs(corner_map[:16, :]))))
    copy = pltpu.make_async_copy(block, sent, sem)
    copy.start()
    put_faces([w0, w1, w2, w3], local)
    copy.wait()


def third_coarse(received, before, zold, znew, step, corner_map, spread, *rest):
    inverses, (mult_out, base_out, gamma_out) = rest[:-3], rest[-3:]
    n_load = zold.shape[0]
    rz0, curve0, _, _ = sums_of(before[...], n_load)
    rz1, curve, mixed, square = sums_of(total_of(received), n_load)
    alpha = rz0 / curve0
    beta = rz1 / rz0
    gamma = rz1 / (curve + 2.0 * beta * mixed + beta * beta * rz0)
    direction = znew[...] + beta * zold[...]
    mult_out[...] = alpha * (zold[...] + gamma * direction)
    n = spread.shape[1]
    height = n * n // LANES
    corners = two_groups(received, n // 4, n_load)
    index = 0
    for ref in inverses:
        for low in range(0, ref.shape[0], height):
            if index == len(corners):
                corners.append(group_corners(received, lax.axis_index("grp") ^ index, n // 4, n_load))
            values = corners[index]
            square = square + 4.0 * rows_sum(values * finer(values, from_tiles(ref[low : low + height, :], n)))
            index += 1
    rz2 = square + 2.0 * beta * (mixed - curve) + beta * beta * (rz0 - mixed)
    rz2 = rz1 - 2.0 * gamma * (curve + beta * mixed) + gamma * gamma * rz2
    field = by_map(coarse_of(*corners[:2], spread[...]), corner_map[...], NN)
    base_out[...] = znew[...] - gamma * (field + beta * step[...]) + (rz2 / rz1) * direction
    gamma_out[...] = jnp.broadcast_to(gamma, gamma_out.shape)


def finish(o0, o1, o2, o3, a0, a1, a2, a3, base, gamma, mult, vectors, mult_hbm, direction_hbm, out, sems):
    n_load = base.shape[0]
    first = pltpu.make_async_copy(mult, mult_hbm, sems.at[0])
    first.start()
    jumped = jump([o0, o1, o2, o3], [a0, a1, a2, a3], n_load, vectors[2:3, :])
    out[...] = base[...] - gamma[:, :1] * jumped
    second = pltpu.make_async_copy(out, direction_hbm, sems.at[1])
    second.start()
    first.wait()
    second.wait()


def call(name, kernel, args, outs, scratch=(), in_place=(), out_place=(), limit=None):
    shapes = [jax.ShapeDtypeStruct(s, d) for s, d in outs]
    n_bytes = sum(a.size * a.dtype.itemsize for a in args) + sum(s.size * s.dtype.itemsize for s in shapes)
    return pl.pallas_call(
        kernel,
        out_shape=shapes,
        in_specs=[pl.BlockSpec(memory_space=pl.ANY if i in in_place else pltpu.VMEM) for i in range(len(args))],
        out_specs=[pl.BlockSpec(memory_space=pl.ANY if i in out_place else pltpu.VMEM) for i in range(len(outs))],
        scratch_shapes=scratch,
        cost_estimate=pl.CostEstimate(flops=40_000_000, bytes_accessed=n_bytes, transcendentals=0),
        compiler_params=pltpu.CompilerParams(vmem_limit_bytes=limit or (12 << 20) + 2 * n_bytes),
        name=name,
    )(*args)


def behind(block, other):
    return pl.pallas_call(
        lambda block_ref, other_ref, out_ref: None,
        out_shape=jax.ShapeDtypeStruct(block.shape, block.dtype),
        in_specs=[pl.BlockSpec(memory_space=pl.ANY)] * 2,
        out_specs=pl.BlockSpec(memory_space=pl.ANY),
        input_output_aliases={0: 0},
        compiler_params=pltpu.CompilerParams(vmem_limit_bytes=1 << 20),
        name="behind",
    )(block, other)


def swap(block, axis, distance):
    count = lax.axis_size(axis)
    return lax.ppermute(block, axis, [(i, i ^ distance) for i in range(count) if i ^ distance < count])


def exchange(wins):
    return [swap(win, "grp", 1) if f == 3 else swap(win, "sub", 1 << f) for f, win in zip(FACES, wins)]


def send_pair(rows):
    subs = lax.axis_size("sub")
    devices = 2 * subs
    blocks = rows.reshape(devices, 4, rows.shape[1])
    teams = [list(range(low, low + devices)) for low in range(0, lax.axis_size("grp") * subs, devices)]
    return lax.all_to_all(blocks, ("grp", "sub"), 0, 0, tiled=True, axis_index_groups=teams).reshape(rows.shape)


def send_all(rows):
    devices = lax.axis_size("grp") * lax.axis_size("sub")
    blocks = rows.reshape(devices, 4, rows.shape[1])
    return lax.all_to_all(blocks, ("grp", "sub"), 0, 0, tiled=True).reshape(rows.shape)


def body(loads, stiffness, flexibility, coarse_inverse, face_nodes, corner_index):
    rhs, stiff, flex, inverse = loads[0, 0], stiffness[0, 0], flexibility[0, 0], coarse_inverse[0]
    nodes, ids = face_nodes[0, 0], corner_index[0, 0]
    n_load, dofs = rhs.shape
    groups, subs = lax.axis_size("grp"), lax.axis_size("sub")
    n = 16 * subs
    field = ((n_load, dofs), F32)
    sent = ((groups * subs * 4, 4 * n_load), F32)
    total = ((8, 4 * n_load), F32)
    n_tile = n * n // LANES

    def faces(rows, more=0, last=0, first=0):
        return [((size(rows) + more + last * (i == LAST) + first * (i == 0), LANES), F32) for i in range(4)]

    order = inverse.shape[0]
    wide = -(-order // LANES) * LANES
    few = ids.shape[0]
    small = jnp.pad(inverse, ((0, 8), (0, wide - order)))
    small = small + jnp.pad(nodes[None], ((order, 7), (0, wide - 4))).astype(F32)
    small = small + jnp.pad(ids[None], ((order, 7), (4, wide - 4 - few))).astype(F32)
    block = [pltpu.VMEM(sent[0], F32), pltpu.SemaphoreType.DMA]
    corners, vectors, corner, resid, spread, inverse, low, *own = call(
        "start", functools.partial(start, ids.shape[0]), [rhs, stiff, small],
        [((2 * subs * 4, 4 * n_load), F32), ((8, dofs), F32), ((16, dofs), BF16), field, ((64, n), F32), ((n_tile, LANES), F32), field]
        + faces(n_load, 8, 16 * n // LANES, EXTRA),
        [pltpu.VMEM(rhs.shape, F32), pltpu.VMEM(stiff.shape, BF16), pltpu.VMEM((2 * subs * 4, 4 * n_load), F32),
         pltpu.SemaphoreType.DMA((3,))],
        [0, 1], [0], START_LIMIT << 10,
    )
    received = send_pair(corners)
    came = exchange(own)
    inverse = inverse
    other = swap(inverse, "grp", 1)
    zold, corner_map, spread, *own = call(
        "image1", first_image, [received] + own + came + [vectors, corner, spread, low, flex],
        [field, ((80, dofs), BF16), ((80, n), F32)] + faces(2 * n_load),
    )
    (sums,) = call("sums1", first_sums, own + [zold, resid, vectors], [total])
    came = exchange(own)
    flexed, low, inverse, sent_rows, *own = call(
        "local2", second_local, own + came + [sums, vectors, corner_map, inverse, other, stiff],
        [field, ((n_load, dofs), BF16), ((2 * n_tile, LANES), F32), sent] + faces(n_load),
        block, out_place=[3],
    )
    received = send_all(sent_rows)
    came = exchange(own)
    before, coarse = call("coarse2", second_coarse, [received, corner_map, spread], [total, field])
    znew, step, *own = call(
        "image2", second_image, [before, coarse] + own + came + [zold, low, vectors, flex],
        [field, field] + faces(n_load),
    )
    (sums,) = call("sums2", second_sums, [before] + own + [znew, flexed, resid, vectors], [total])
    came = exchange(own)
    inverses = [inverse]
    distance = 2
    while distance < groups:
        held = inverses[0] if distance == 2 else jnp.concatenate(inverses, axis=0)
        inverses.append(swap(held, "grp", distance))
        distance *= 2
    sent_rows, *own = call(
        "local3", third_local, own + came + [sums, vectors, corner_map, stiff], [sent] + faces(n_load),
        block, out_place=[0],
    )
    received = send_all(sent_rows)
    came = exchange(own)
    mult, base, gamma = call(
        "coarse3", third_coarse, [received, before, zold, znew, step, corner_map, spread] + inverses,
        [field, field, ((n_load, LANES), F32)],
    )
    mult, direction = call(
        "finish", finish, own + came + [base, gamma, mult, vectors], [field, field],
        [pltpu.VMEM(rhs.shape, F32), pltpu.SemaphoreType.DMA((2,))], out_place=[0, 1],
    )
    return (mult[None, None], direction[None, None])


def solution(mesh):
    in_specs = (
        P("grp", "sub", None, None),
        P("grp", "sub", None, None),
        P("grp", "sub", None, None),
        P("grp", None, None),
        P("grp", "sub", None),
        P("grp", "sub", None),
    )
    out_specs = (P("grp", "sub", None, None), P("grp", "sub", None, None))
    return jax.shard_map(body, mesh=mesh, in_specs=in_specs, out_specs=out_specs, check_vma=False)
```
